32 devices in a mesh: dp: 2 (over x), seq: 16 (over z, y, core).
Axes of the slice: x: 2, y: 2, z: 4, core: 2. Of those that a mesh axis runs over, the one named last changes fastest.
Arguments:
- tokens: bfloat16 [16384, 768], P(('dp', 'seq')), may hold values from -6 to 6
- t_embed: bfloat16 [4, 768], P('dp'), may hold values from -6 to 6
- frame_clip: int32 [64], P('dp'), may hold values from 0 to 1, as said below
- boxes: int32 [64, 4], P(('dp', 'seq')), may hold values from 0 to 16, as said below
- mod_weight: bfloat16 [768, 6912], replicated, may hold values from -0.21875 to 0.21875
- mod_bias: bfloat16 [6912], replicated, may hold values from -3 to 3
- space_qkv: bfloat16 [768, 2304], replicated, may hold values from -0.21875 to 0.21875
- space_qv_bias: bfloat16 [1536], replicated, may hold values from -4 to 4
- space_out: bfloat16 [768, 768], replicated, may hold values from -1.75 to 1.75
- space_out_bias: bfloat16 [768], replicated, may hold values from -4 to 4
- time_qkv: bfloat16 [768, 2304], replicated, may hold values from -0.21875 to 0.21875
- time_qv_bias: bfloat16 [1536], replicated, may hold values from -4 to 4
- time_out: bfloat16 [768, 768], replicated, may hold values from -0.625 to 0.625
- time_out_bias: bfloat16 [768], replicated, may hold values from -4 to 4
- up_weight: bfloat16 [768, 3072], replicated, may hold values from -0.21875 to 0.21875
- up_bias: bfloat16 [3072], replicated, may hold values from -4 to 4
- down_weight: bfloat16 [3072, 768], replicated, may hold values from -0.109375 to 0.109375
- down_bias: bfloat16 [768], replicated, may hold values from -4 to 4
- cotangent: bfloat16 [16384, 768], P(('dp', 'seq')), may hold values from -6 to 6
Outputs:
- result: bfloat16 [16384, 768], P(('dp', 'seq'))
- grad_tokens: bfloat16 [16384, 768], P(('dp', 'seq'))
- grad_mod_weight: float32 [768, 6912], replicated
- grad_mod_bias: float32 [6912], replicated
- grad_space_qkv: float32 [768, 2304], replicated
- grad_space_qv_bias: float32 [1536], replicated
- grad_space_out: float32 [768, 768], replicated
- grad_space_out_bias: float32 [768], replicated
- grad_time_qkv: float32 [768, 2304], replicated
- grad_time_qv_bias: float32 [1536], replicated
- grad_time_out: float32 [768, 768], replicated
- grad_time_out_bias: float32 [768], replicated
- grad_up_weight: float32 [768, 3072], replicated
- grad_up_bias: float32 [3072], replicated
- grad_down_weight: float32 [3072, 768], replicated
- grad_down_bias: float32 [768], replicated
The draws below stay inside these ranges and needn't reach their ends.
Inputs may be any that keep to these rules, and one draw needn't show every extreme that they name: `frame_clip`: within each replica group of 32 frames every clip number appears exactly 16 times, and the group's first and last frames belong to the same clip. `boxes`: each box has 1 to 8 rows and 1 to 8 columns inside the grid (first < end).
All inputs are finite; a program needn't handle non-finite values.
Results may differ from the reference program's by a relative error of at most 0.015.
Values may be sent and summed in bfloat16 or wider, within the bound.
No kernel may reach another device: no remote copies, remote signals or barrier semaphores. Data moves between devices by JAX's collectives and lax.ppermute only.
A program may use at most 320 MiB of HBM per device.

```python
import jax
import jax.numpy as jnp
from jax import lax

D = 768
H = 12
HD = 64
FF = 3072
GRID_H = 16
GRID_W = 16
CLIP = 16
P_SIZE = 256
GROUP_FRAMES = 32
CLIPS_G = 2
FRAMES = 64
CLIPS = 4
TOKENS = 16384


def clip_group(key):
    shuffled = jax.random.permutation(key, GROUP_FRAMES)
    clip_ids = (shuffled // CLIP).astype(jnp.int32)
    first_clip = clip_ids[0]
    positions = jnp.arange(GROUP_FRAMES, dtype=jnp.int32)
    partner = jnp.max(jnp.where((clip_ids == first_clip) & (positions > 0), positions, 0))
    final_clip = clip_ids[GROUP_FRAMES - 1]
    clip_ids = clip_ids.at[partner].set(final_clip)
    clip_ids = clip_ids.at[GROUP_FRAMES - 1].set(first_clip)
    return clip_ids


def draw_frame_clip(key, part):
    key = jax.random.fold_in(key, 11)
    group_keys = jax.random.split(key, FRAMES // GROUP_FRAMES)
    return jax.vmap(clip_group)(group_keys).reshape(FRAMES).astype(jnp.int32)


def draw_boxes(key, part):
    key = jax.random.fold_in(key, 23)
    sub_keys = jax.random.split(key, 4)
    box_rows = jax.random.randint(sub_keys[0], (FRAMES,), 1, GRID_H // 2 + 1)
    box_cols = jax.random.randint(sub_keys[1], (FRAMES,), 1, GRID_W // 2 + 1)
    row_start = jax.random.randint(sub_keys[2], (FRAMES,), 0, GRID_H) % (GRID_H - box_rows + 1)
    col_start = jax.random.randint(sub_keys[3], (FRAMES,), 0, GRID_W) % (GRID_W - box_cols + 1)
    row_start = row_start.at[0].set(GRID_H - box_rows[0])
    col_start = col_start.at[0].set(GRID_W - box_cols[0])
    return jnp.stack([row_start, row_start + box_rows, col_start, col_start + box_cols], axis=1).astype(jnp.int32)


def level_of(rng, dims, cuts, smallest, largest):
    def one(dim, parts):
        steps = jax.random.uniform(jax.random.fold_in(jax.random.fold_in(rng, 6), dim), (parts,), jnp.float32, smallest / len(cuts), largest / len(cuts))
        return jnp.repeat(jnp.exp(steps), dims[dim] // parts).reshape((-1,) + (1,) * (len(dims) - dim - 1))

    loudness = one(*cuts[0])
    for cut in cuts[1:]:
        loudness = loudness * one(*cut)
    return loudness


def scatter_about(key, extent, deviation, bound, cuts=(), held_as=jnp.bfloat16):
    factor_of = level_of(key, extent, cuts, -0.22, 0.18) if cuts else 1.0
    result = jax.random.normal(key, extent, jnp.float32) * deviation * factor_of
    return jnp.minimum(jnp.maximum(result, -bound), bound).astype(held_as)


def setup_inputs(seed: int = 0) -> dict:
    key_of = jax.random.split(jax.random.key(seed), 20)
    tokens = scatter_about(key_of[0], (TOKENS, D), 1.0, 6.0, ((0, 32),))
    t_embed = scatter_about(key_of[1], (CLIPS, D), 1.0, 6.0, ((0, 2),))
    frame_clip = draw_frame_clip(jax.random.fold_in(key_of[19], 71), 0)
    boxes = draw_boxes(jax.random.fold_in(key_of[19], 71), 0)
    mod_weight = scatter_about(key_of[4], (D, 9 * D), D ** -0.5, 0.21875)
    mod_bias = scatter_about(key_of[5], (9 * D,), 0.2, 3.0)
    space_qkv = scatter_about(key_of[6], (D, 3 * D), D ** -0.5, 0.21875)
    space_qv_bias = scatter_about(key_of[7], (2 * D,), 0.3, 4.0)
    space_out = scatter_about(key_of[8], (D, D), (D // 64) ** -0.5, 1.75)
    space_out_bias = scatter_about(key_of[9], (D,), 0.3, 4.0)
    time_qkv = scatter_about(key_of[10], (D, 3 * D), D ** -0.5, 0.21875)
    time_qv_bias = scatter_about(key_of[11], (2 * D,), 0.3, 4.0)
    time_out = scatter_about(key_of[12], (D, D), (D // 8) ** -0.5, 0.625)
    time_out_bias = scatter_about(key_of[13], (D,), 0.3, 4.0)
    up_weight = scatter_about(key_of[14], (D, FF), D ** -0.5, 0.21875)
    up_bias = scatter_about(key_of[15], (FF,), 0.3, 4.0)
    down_weight = scatter_about(key_of[16], (FF, D), FF ** -0.5, 0.109375)
    down_bias = scatter_about(key_of[17], (D,), 0.3, 4.0)
    cotangent = scatter_about(key_of[18], (TOKENS, D), 1.0, 6.0, ((0, 32),))
    return {"tokens": tokens, "t_embed": t_embed, "frame_clip": frame_clip, "boxes": boxes, "mod_weight": mod_weight, "mod_bias": mod_bias, "space_qkv": space_qkv, "space_qv_bias": space_qv_bias, "space_out": space_out, "space_out_bias": space_out_bias, "time_qkv": time_qkv, "time_qv_bias": time_qv_bias, "time_out": time_out, "time_out_bias": time_out_bias, "up_weight": up_weight, "up_bias": up_bias, "down_weight": down_weight, "down_bias": down_bias, "cotangent": cotangent}


@jax.custom_vjp
def low(v):
    return lax.optimization_barrier(v.astype(jnp.bfloat16)).astype(jnp.float32)

@jax.custom_vjp
def low_back(v):
    return v

def low_keep(v):
    return (low(v), None)

def low_pass(kept, grad):
    return (grad,)

def back_keep(v):
    return (v, None)

def back_low(kept, grad):
    return (low(grad),)
low.defvjp(low_keep, low_pass)
low_back.defvjp(back_keep, back_low)
EPS = 1e-06
HIGH = lax.Precision.HIGHEST
NEG = -1e+30

def layer_norm(values):
    center = values - lax.optimization_barrier(jnp.mean(values, axis=-1, keepdims=True))
    spread = lax.optimization_barrier(jnp.mean(center * center, axis=-1, keepdims=True))
    return center * lax.rsqrt(spread + EPS)

def modulate(values, shift_by, scale_by):
    return layer_norm(values) * (1.0 + scale_by) + shift_by

def smooth_gelu(values):
    return jax.nn.gelu(values, approximate=True)

def attend(query_in, key_in, value_in, allowed):
    factor = query_in.shape[-1] ** (-0.5)
    scores = jnp.einsum('qhe,khe->hqk', query_in, key_in, precision=HIGH) * factor
    scores = low_back(scores)
    scores = jnp.where(allowed[None], scores, NEG)
    exp_scores = jnp.exp(scores - lax.optimization_barrier(jnp.max(scores, axis=-1, keepdims=True)))
    soft_rows = low(exp_scores / lax.optimization_barrier(jnp.sum(exp_scores, axis=-1, keepdims=True)))
    return jnp.einsum('hqk,khe->qhe', soft_rows, value_in, precision=HIGH)

def split_heads(packed, model_width, head_shape):
    query_part = packed[..., :model_width].reshape(head_shape)
    key_part = packed[..., model_width:2 * model_width].reshape(head_shape)
    value_part = packed[..., 2 * model_width:].reshape(head_shape)
    return (query_part, key_part, value_part)

def full_bias(qv_bias, model_width):
    return jnp.concatenate([qv_bias[:model_width], jnp.zeros((model_width,), qv_bias.dtype), qv_bias[model_width:]])

def forward(tokens, mod_weight, mod_bias, space_qkv, space_qv_bias, space_out, space_out_bias, time_qkv, time_qv_bias, time_out, time_out_bias, up_weight, up_bias, down_weight, down_bias, smooth_in, global_clip, visible):
    model_width = tokens.shape[1]
    smooth = low(smooth_in)
    modulation = jnp.dot(smooth, mod_weight, precision=HIGH) + mod_bias
    per_frame = modulation[global_clip].reshape(FRAMES, 9, 1, model_width)
    pieces = [per_frame[:, member] for member in range(9)]
    head_shape = (FRAMES, P_SIZE, H, HD)
    hidden = tokens.reshape(FRAMES, P_SIZE, model_width)
    normed = low(modulate(hidden, pieces[0], pieces[1]))
    packed = low_back(low(jnp.einsum('fpd,de->fpe', normed, space_qkv, precision=HIGH) + full_bias(space_qv_bias, model_width)))
    query_a, key_a, value_a = split_heads(packed, model_width, head_shape)

    def space_block(group):
        return attend(group[0], group[1], group[2], group[3][None, :])
    mixed = lax.map(jax.checkpoint(space_block), (query_a, key_a, value_a, visible))
    attended = low_back(low(mixed.reshape(FRAMES, P_SIZE, model_width)))
    branch = low_back(jnp.einsum('fpd,de->fpe', attended, space_out, precision=HIGH) + space_out_bias)
    hidden = hidden + pieces[2] * branch
    normed = low(modulate(hidden, pieces[3], pieces[4]))
    packed = low_back(low(jnp.einsum('fpd,de->fpe', normed, time_qkv, precision=HIGH) + full_bias(time_qv_bias, model_width)))
    query_b, key_b, value_b = split_heads(packed, model_width, head_shape)
    same_clip = global_clip[:, None] == global_clip[None, :]

    def time_block(group):
        return attend(group[0], group[1], group[2], same_clip)
    mixed = lax.map(jax.checkpoint(time_block), (query_b.transpose(1, 0, 2, 3), key_b.transpose(1, 0, 2, 3), value_b.transpose(1, 0, 2, 3)))
    mixed = mixed.transpose(1, 0, 2, 3)
    attended = low_back(low(mixed.reshape(FRAMES, P_SIZE, model_width)))
    branch = low_back(jnp.einsum('fpd,de->fpe', attended, time_out, precision=HIGH) + time_out_bias)
    hidden = hidden + pieces[5] * branch
    normed = low(modulate(hidden, pieces[6], pieces[7]))
    hidden_up = low_back(jnp.einsum('fpd,dh->fph', normed, up_weight, precision=HIGH) + up_bias)
    activated = low(smooth_gelu(hidden_up))
    branch = low_back(jnp.einsum('fph,hd->fpd', activated, down_weight, precision=HIGH) + down_bias)
    hidden = hidden + pieces[8] * branch
    return hidden.reshape(FRAMES * P_SIZE, model_width)

def reference(tokens, t_embed, frame_clip, boxes, mod_weight, mod_bias, space_qkv, space_qv_bias, space_out, space_out_bias, time_qkv, time_qv_bias, time_out, time_out_bias, up_weight, up_bias, down_weight, down_bias, cotangent):
    frame_ids = jnp.arange(FRAMES, dtype=jnp.int32)
    global_clip = (frame_clip + frame_ids // GROUP_FRAMES * CLIPS_G).astype(jnp.int32)
    cells = jnp.arange(P_SIZE, dtype=jnp.int32)
    cell_row = cells // GRID_W
    cell_col = cells % GRID_W
    inside = (cell_row[None] >= boxes[:, 0:1]) & (cell_row[None] < boxes[:, 1:2]) & (cell_col[None] >= boxes[:, 2:3]) & (cell_col[None] < boxes[:, 3:4])
    visible = jnp.logical_not(inside)
    smooth_in = jax.nn.silu(t_embed.astype(jnp.float32))

    def run(*params):
        return forward(*params, smooth_in, global_clip, visible)
    primals = [tokens, mod_weight, mod_bias, space_qkv, space_qv_bias, space_out, space_out_bias, time_qkv, time_qv_bias, time_out, time_out_bias, up_weight, up_bias, down_weight, down_bias]
    primals = [matrix.astype(jnp.float32) for matrix in primals]
    output, pull_back = jax.vjp(run, *primals)
    grads = pull_back(cotangent.astype(jnp.float32))
    return (output.astype(jnp.bfloat16), grads[0].astype(jnp.bfloat16), grads[1], grads[2], grads[3], grads[4], grads[5], grads[6], grads[7], grads[8], grads[9], grads[10], grads[11], grads[12], grads[13], grads[14])
```

```python
import functools

import jax
import jax.numpy as jnp
from jax import lax
from jax.experimental import pallas as pl
from jax.experimental.pallas import tpu as pltpu
from jax.sharding import PartitionSpec as P

HD = 64
GRID_W = 16
EPS = 1e-06
NEG = -1e30
BLOCK = 256
LANES = 128
BF = jnp.bfloat16
F32 = jnp.float32
VMEM_BYTES = 56 * 1024 * 1024
BOTH = ("dp", "seq")
BRIEF = pl.CostEstimate(flops=1000, bytes_accessed=1000, transcendentals=0)
LONG = pl.CostEstimate(flops=3 * 10**10, bytes_accessed=1000, transcendentals=0)

SCHEDULE = (
    ("time",),
    ("t", "cross", 0),
    ("space",),
    ("t", "cross", 1),
    ("s", "cross", 0),
    ("small",),
    ("t", "along"),
    ("small",),
    ("s", "cross", 1),
    ("t", "finish"),
    ("ff",),
    ("s", "along"),
    ("small",),
    ("t", "gather"),
    ("s", "finish"),
    ("t", "relay"),
    ("small",),
    ("s", "gather"),
    ("t", "reflect"),
    ("small",),
    ("t", "widen", 0),
    ("s", "relay"),
    ("t", "widen", 1),
    ("mod",),
    ("s", "reflect"),
    ("s", "widen", 0),
    ("s", "widen", 1),
)


def params():
    return pltpu.CompilerParams(vmem_limit_bytes=VMEM_BYTES)


def alone():
    return pltpu.CompilerParams(vmem_limit_bytes=60 * 1024 * 1024)


def dot_nn(a, b):
    return lax.dot_general(a, b, (((1,), (0,)), ((), ())), preferred_element_type=F32)


def dot_nt(a, b):
    return lax.dot_general(a, b, (((1,), (1,)), ((), ())), preferred_element_type=F32)


def dot_tn(a, b):
    return lax.dot_general(a, b, (((0,), (0,)), ((), ())), preferred_element_type=F32)


def normalize(x):
    center = x - jnp.mean(x, axis=-1, keepdims=True)
    r = lax.rsqrt(jnp.mean(center * center, axis=-1, keepdims=True) + EPS)
    return center * r, r


def normalize_back(n, r, m):
    return r * (
        m - jnp.mean(m, axis=-1, keepdims=True) - n * jnp.mean(m * n, axis=-1, keepdims=True)
    )


def head_halves(width):
    lane = lax.broadcasted_iota(jnp.int32, (1, width), 1)
    low = (lane < HD).astype(F32).astype(BF)
    return low, (lane >= HD).astype(F32).astype(BF)


def attend(packed, attended, bias, blocks, width):
    halves = head_halves(2 * HD)

    def pair(index, carry):
        off = pl.multiple_of(index * 2 * HD, 2 * HD)
        for b in range(blocks):
            rows = pl.ds(b * BLOCK, BLOCK)
            q = packed[rows, pl.ds(off, 2 * HD)]
            k = packed[rows, pl.ds(width + off, 2 * HD)]
            v = packed[rows, pl.ds(2 * width + off, 2 * HD)]
            out = None
            for half in halves:
                s = dot_nt(q, k * half) * (HD**-0.5) + bias(b)
                e = jnp.exp(s - jnp.max(s, axis=-1, keepdims=True))
                p = (e * (1.0 / jnp.sum(e, axis=-1, keepdims=True))).astype(BF)
                o = dot_nn(p, v * half)
                out = o if out is None else out + o
            attended[rows, pl.ds(off, 2 * HD)] = out.astype(BF)
        return carry

    lax.fori_loop(0, width // (2 * HD), pair, 0)


def attend_back(packed, grad_in, grad_packed, bias, blocks, width):
    halves = head_halves(2 * HD)
    factor = HD**-0.5

    def pair(index, carry):
        off = pl.multiple_of(index * 2 * HD, 2 * HD)
        for b in range(blocks):
            rows = pl.ds(b * BLOCK, BLOCK)
            q = packed[rows, pl.ds(off, 2 * HD)]
            k = packed[rows, pl.ds(width + off, 2 * HD)]
            v = packed[rows, pl.ds(2 * width + off, 2 * HD)]
            g = grad_in[rows, pl.ds(off, 2 * HD)]
            dq = dk = dv = 0.0
            for half in halves:
                kh = k * half
                s = dot_nt(q, kh) * factor + bias(b)
                e = jnp.exp(s - jnp.max(s, axis=-1, keepdims=True))
                p = e * (1.0 / jnp.sum(e, axis=-1, keepdims=True))
                gs = dot_nt(g, v * half)
                ds = (p * (gs - jnp.sum(p * gs, axis=-1, keepdims=True))).astype(BF)
                dv = dv + dot_tn(p.astype(BF), g * half)
                dq = dq + dot_nn(ds, kh)
                dk = dk + dot_tn(ds, q * half)
            grad_packed[rows, pl.ds(off, 2 * HD)] = (dq * factor).astype(BF)
            grad_packed[rows, pl.ds(width + off, 2 * HD)] = (dk * factor).astype(BF)
            grad_packed[rows, pl.ds(2 * width + off, 2 * HD)] = dv.astype(BF)
        return carry

    lax.fori_loop(0, width // (2 * HD), pair, 0)


def project_qkv(normed, weight, qv_bias, packed, width):
    for c in range(3):
        cols = pl.ds(c * width, width)
        value = dot_nn(normed[...], weight[:, cols])
        if c != 1:
            value = value + as_row(qv_bias[pl.ds((c // 2) * width, width)])
        packed[:, cols] = value.astype(BF)


def modulation_kernel(first, t_ref, w_ref, b_ref, out_ref):
    t = t_ref[...].astype(F32)
    smooth = (t / (1.0 + jnp.exp(-t))).astype(BF)
    bias = chunk_row(b_ref, first + pl.program_id(0), t.shape[1])
    out_ref[0] = dot_nn(smooth, w_ref[...]) + bias


def modulation(t_embed, weight, bias, first, count):
    clips, width = t_embed.shape
    return pl.pallas_call(
        functools.partial(modulation_kernel, first),
        grid=(count,),
        in_specs=[
            pl.BlockSpec((clips, width), lambda i: (0, 0)),
            pl.BlockSpec((width, width), lambda i: (0, first + i)),
            vmem(),
        ],
        out_specs=pl.BlockSpec((1, clips, width), lambda i: (i, 0, 0)),
        out_shape=jax.ShapeDtypeStruct((count, clips, width), F32),
        cost_estimate=BRIEF,
        name="modulation",
    )(t_embed, weight, bias)


def as_row(vector):
    return vector.astype(F32).reshape(1, -1)


def chunk_row(vector_ref, index, width):
    return as_row(vector_ref[pl.ds(pl.multiple_of(index * width, width), width)])


def own_clips(clip_ref, frames):
    first = lax.axis_index("seq") * frames
    return [clip_ref[first + f] for f in range(frames)]


def frame_row(table, member, clip):
    total = jnp.zeros(table.shape[2:], F32)[None]
    for c in range(table.shape[1]):
        total = jnp.where(clip == c, table[member, c : c + 1, :], total)
    return total


def frame_rows(table, member, clip_col):
    total = jnp.zeros((clip_col.shape[0], table.shape[2]), F32)
    for c in range(table.shape[1]):
        total = jnp.where(clip_col == c, table[member, c : c + 1, :], total)
    return total


def visible_bias(box_ref, frame, patches):
    cell = lax.broadcasted_iota(jnp.int32, (1, patches), 1)
    row, col = cell // GRID_W, cell % GRID_W
    inside = (
        (row >= box_ref[frame, 0])
        & (row < box_ref[frame, 1])
        & (col >= box_ref[frame, 2])
        & (col < box_ref[frame, 3])
    )
    return jnp.where(inside, NEG, 0.0)


def space_forward_kernel(
    clip_ref, box_ref, x_ref, table_ref, wqkv_ref, bqv_ref, wout_ref, bout_ref,
    send_ref, packed_ref, attended_ref, branch_ref, normed,
):
    frames = box_ref.shape[0]
    width = x_ref.shape[1]
    dst, _, pos, _ = send_ref.shape
    clip = own_clips(clip_ref, frames)
    for f in range(frames):
        rows = pl.ds(f * BLOCK, BLOCK)
        n, _ = normalize(x_ref[rows, :].astype(F32))
        shift = frame_row(table_ref, 0, clip[f])
        scale = frame_row(table_ref, 1, clip[f])
        normed[rows, :] = (n * (1.0 + scale) + shift).astype(BF)
    project_qkv(normed, wqkv_ref, bqv_ref, packed_ref, width)
    biases = [visible_bias(box_ref, f, BLOCK) for f in range(frames)]
    attend(packed_ref, attended_ref, lambda b: biases[b], frames, width)
    for f in range(frames):
        rows = pl.ds(f * BLOCK, BLOCK)
        branch = dot_nn(attended_ref[rows, :], wout_ref[...]) + as_row(bout_ref[...])
        branch_ref[rows, :] = branch
        gate = frame_row(table_ref, 2, clip[f])
        mid = x_ref[rows, :].astype(F32) + gate * branch
        send_ref[:, f] = mid.astype(BF).reshape(dst, pos, width)


def vmem():
    return pl.BlockSpec(memory_space=pltpu.VMEM)


def smem():
    return pl.BlockSpec(memory_space=pltpu.SMEM)


def space_forward(frame_clip, boxes, tokens, table, wqkv, bqv, wout, bout, owners):
    rows, width = tokens.shape
    frames = boxes.shape[0]
    pos = rows // frames // owners
    return pl.pallas_call(
        space_forward_kernel,
        in_specs=[smem(), smem()] + [vmem()] * 6,
        out_specs=[vmem()] * 4,
        out_shape=[
            jax.ShapeDtypeStruct((owners, frames, pos, width), BF),
            jax.ShapeDtypeStruct((rows, 3 * width), BF),
            jax.ShapeDtypeStruct((rows, width), BF),
            jax.ShapeDtypeStruct((rows, width), F32),
        ],
        scratch_shapes=[pltpu.VMEM((rows, width), BF)],
        compiler_params=params(),
        cost_estimate=BRIEF,
        name="space_forward",
    )(frame_clip, boxes, tokens, table, wqkv, bqv, wout, bout)


def to_positions(source, stage, target):
    frames, pos, width = source.shape
    for lane in range(0, width, LANES):
        cols = pl.ds(lane, LANES)
        stage[lane // LANES] = source[:, :, cols].astype(F32).reshape(frames * pos, LANES)
        for p in range(pos):
            target[pl.ds(p * frames, frames), cols] = stage[
                lane // LANES, pl.ds(p, frames, stride=pos), :
            ].astype(target.dtype)


def stage_positions(stage, value, frames, pos, first):
    for lane in range(0, value.shape[1], LANES):
        for p in range(value.shape[0] // frames):
            stage[lane // LANES, pl.ds(first + p, frames, stride=pos), :] = value[
                p * frames : (p + 1) * frames, lane : lane + LANES
            ]


def to_frames(stage, target):
    frames, pos, width = target.shape
    for lane in range(0, width, LANES):
        target[:, :, pl.ds(lane, LANES)] = (
            stage[lane // LANES].reshape(frames, pos, LANES).astype(BF)
        )


def time_mask(ids_row_ref, clip_col, positions, clips):
    frames = clip_col.shape[0]
    place = lax.broadcasted_iota(jnp.int32, (positions, frames, 1), 0) * clips
    col = (place + clip_col[None]).reshape(positions * frames, 1)
    return jnp.where(col == ids_row_ref[...], 0.0, NEG)


def spread(rows, positions):
    frames, width = rows.shape
    return jnp.broadcast_to(rows[None], (positions, frames, width)).reshape(
        positions * frames, width
    )


def gather_frames(value, frames):
    return jnp.sum(value.reshape(-1, frames, value.shape[-1]), axis=0)


def per_clip_sums(out_ref, member, rows, clip_col):
    for c in range(out_ref.shape[1]):
        out_ref[member, c : c + 1, :] = jnp.sum(
            jnp.where(clip_col == c, rows, 0.0), axis=0, keepdims=True
        )


def gelu_and_slope(v):
    c = 0.7978845608028654
    square = v * v
    t = jnp.tanh(v * (c + (c * 0.044715) * square))
    half = 0.5 + 0.5 * t
    slope = half + (0.5 * v) * (1.0 - t * t) * (c + (3.0 * c * 0.044715) * square)
    return v * half, slope


def time_forward_kernel(
    mid_ref, cot_ref, table_ref, clip_col_ref, ids_row_ref, wqkv_ref, bqv_ref, wout_ref, bout_ref,
    xa_ref, packed_ref, attended_ref, branch_ref, midb_ref, normed_ref, gbranch_ref, cot_out, gdownb_ref,
    stage, mid, cot, normed, bias,
):
    frames, pos, width = mid_ref.shape
    blocks = frames * pos // BLOCK
    per_block = BLOCK // frames
    clips = table_ref.shape[1]
    clip_col = clip_col_ref[...]

    def modvec(member):
        return spread(frame_rows(table_ref, member, clip_col), per_block)

    to_positions(mid_ref, stage, mid)
    to_positions(cot_ref, stage, cot)
    xa_ref[...] = mid[...].astype(BF)
    cot_out[...] = cot[...].astype(BF)
    bias[...] = time_mask(ids_row_ref, clip_col, per_block, clips)
    shift_b, scale_b = modvec(0), modvec(1)
    for b in range(blocks):
        part = pl.ds(b * BLOCK, BLOCK)
        n, _ = normalize(mid[part, :])
        normed[part, :] = (n * (1.0 + scale_b) + shift_b).astype(BF)
    project_qkv(normed, wqkv_ref, bqv_ref, packed_ref, width)
    attend(packed_ref, attended_ref, lambda b: bias[...], blocks, width)
    gate_b, shift_c, scale_c, gate_c = modvec(2), modvec(3), modvec(4), modvec(5)
    for b in range(blocks):
        part = pl.ds(b * BLOCK, BLOCK)
        branch = dot_nn(attended_ref[part, :], wout_ref[...]) + as_row(bout_ref[...])
        branch_ref[part, :] = branch
        mid_b = mid[part, :] + gate_b * branch
        midb_ref[part, :] = mid_b
        n, _ = normalize(mid_b)
        normed_ref[part, :] = (n * (1.0 + scale_c) + shift_c).astype(BF)
        gbranch_ref[part, :] = (gate_c * cot[part, :]).astype(BF)
    gdownb_ref[...] = jnp.sum(gbranch_ref[...].astype(F32), axis=0, keepdims=True)


def time_forward(mid, cot, table, clip_col, ids_row, wqkv, bqv, wout, bout):
    frames, pos, width = mid.shape
    rows = frames * pos
    like = lambda cols, dtype: jax.ShapeDtypeStruct((rows, cols), dtype)
    return pl.pallas_call(
        time_forward_kernel,
        in_specs=[vmem()] * 9,
        out_specs=[vmem()] * 9,
        out_shape=[
            like(width, BF),
            like(3 * width, BF),
            like(width, BF),
            like(width, F32),
            like(width, F32),
            like(width, BF),
            like(width, BF),
            like(width, BF),
            jax.ShapeDtypeStruct((1, width), F32),
        ],
        scratch_shapes=[
            pltpu.VMEM((width // LANES, rows, LANES), F32),
            pltpu.VMEM((rows, width), F32),
            pltpu.VMEM((rows, width), F32),
            pltpu.VMEM((rows, width), BF),
            pltpu.VMEM((BLOCK, BLOCK), F32),
        ],
        compiler_params=params(),
        cost_estimate=BRIEF,
        name="time_forward",
    )(mid, cot, table, clip_col, ids_row, wqkv, bqv, wout, bout)


def ff_kernel(
    last, normed_ref, gbranch_ref, branch_in, gnorm_in, up_ref, upb_ref, down_ref,
    midb_ref, cot_ref, table_ref, clip_col_ref, downb_ref, *refs,
):
    if last:
        _, grad_ref, gupb_ref, gmid_ref, result_ref, gclip_ref = refs[:6]
        normed_t, act, ghid, branch_acc, gnorm_acc, stage = refs[6:]
    else:
        grad_ref, gupb_ref, branch_acc, gnorm_acc, normed_t, act, ghid = refs
    step = pl.program_id(0)
    width = normed_ref.shape[1]
    blocks = normed_ref.shape[0] // BLOCK
    first = pl.num_programs(0) if last else 0
    up_bias = chunk_row(upb_ref, first + step, act.shape[1])

    @pl.when(step == 0)
    def _():
        normed_t[...] = normed_ref[...].T
        if last:
            branch_acc[...] = branch_in[...]
            gnorm_acc[...] = gnorm_in[...]
        else:
            branch_acc[...] = jnp.zeros_like(branch_acc)
            gnorm_acc[...] = jnp.zeros_like(gnorm_acc)

    for b in range(blocks):
        part = pl.ds(b * BLOCK, BLOCK)
        hidden = dot_nn(normed_ref[part, :], up_ref[...]) + up_bias
        value, slope = gelu_and_slope(hidden)
        value = value.astype(BF)
        act[part, :] = value
        gh = (dot_nt(gbranch_ref[part, :], down_ref[...]) * slope).astype(BF)
        ghid[part, :] = gh
        branch_acc[part, :] += dot_nn(value, down_ref[...])
        gnorm_acc[part, :] += dot_nt(gh, up_ref[...])
    grad_up = dot_nn(normed_t[...], ghid[...])
    grad_down = dot_tn(act[...], gbranch_ref[...])
    grad_ref[0] = grad_up.astype(BF)
    grad_ref[1] = grad_down.astype(BF)
    gupb_ref[0] = jnp.sum(ghid[...].astype(F32), axis=0, keepdims=True)

    if last:

        @pl.when(step == pl.num_programs(0) - 1)
        def _():
            clip_col = clip_col_ref[...]
            frames, pos, _ = result_ref.shape
            per_block = BLOCK // frames

            def modvec(member):
                return spread(frame_rows(table_ref, member, clip_col), per_block)

            scale_c, gate_c = modvec(4), modvec(5)
            sums = [0.0, 0.0, 0.0]
            for b in range(blocks):
                part = pl.ds(b * BLOCK, BLOCK)
                up = cot_ref[part, :].astype(F32)
                branch = branch_acc[part, :] + as_row(downb_ref[...])
                sums[2] = sums[2] + gather_frames(branch * up, frames)
                mid_b = midb_ref[part, :]
                n, r = normalize(mid_b)
                g = gnorm_acc[part, :]
                sums[0] = sums[0] + gather_frames(g, frames)
                sums[1] = sums[1] + gather_frames(g * n, frames)
                gmid_ref[part, :] = up + normalize_back(n, r, g * (1.0 + scale_c))
                stage_positions(stage, mid_b + gate_c * branch, frames, pos, b * per_block)
            to_frames(stage, result_ref)
            for member in range(3):
                per_clip_sums(gclip_ref, member, sums[member], clip_col)


def ff_half(half, normed, gbranch, branch_in, gnorm_in, up, upb, down, midb, cot, table, clip_col, downb, *before):
    rows, width = normed.shape
    clips = table.shape[1]
    frames = clip_col.shape[0]
    pos = rows // frames
    ff = up.shape[1]
    chunk = width
    steps = ff // chunk // 2
    last = half == 1
    first = half * steps
    whole = lambda *shape: pl.BlockSpec(shape, lambda i: (0,) * len(shape))
    grad_specs = [pl.BlockSpec((1, 1, chunk), lambda i: (i, 0, 0))]
    grad_shapes = [jax.ShapeDtypeStruct((steps, 1, chunk), F32)]
    grad_specs = [pl.BlockSpec((2, width, chunk), lambda i: (0, first + i, 0))] + grad_specs
    grad_shapes = [jax.ShapeDtypeStruct((2, 2 * steps * width, chunk), BF)] + grad_shapes
    wide = pltpu.VMEM((rows, width), F32)
    scratch = [pltpu.VMEM((width, rows), BF), pltpu.VMEM((rows, chunk), BF), pltpu.VMEM((rows, chunk), BF)]
    if last:
        out_specs = grad_specs + [whole(rows, width), whole(frames, pos, width), whole(3, clips, width)]
        out_shape = grad_shapes + [
            jax.ShapeDtypeStruct((rows, width), F32),
            jax.ShapeDtypeStruct((frames, pos, width), BF),
            jax.ShapeDtypeStruct((3, clips, width), F32),
        ]
        scratch = scratch + [wide, wide, pltpu.VMEM((width // LANES, rows, LANES), F32)]
    else:
        out_specs = grad_specs + [whole(rows, width), whole(rows, width)]
        out_shape = grad_shapes + [jax.ShapeDtypeStruct((rows, width), F32)] * 2
    unused = pl.BlockSpec(memory_space=pl.ANY)
    late = vmem() if last else unused
    if not last:
        branch_in = gnorm_in = midb
    return pl.pallas_call(
        functools.partial(ff_kernel, last),
        grid=(steps,),
        in_specs=[vmem(), vmem(), late, late]
        + [
            pl.BlockSpec((width, chunk), lambda i: (0, first + i)),
            vmem(),
            pl.BlockSpec((chunk, width), lambda i: (first + i, 0)),
        ]
        + [late] * 5
        + [hbm()] * len(before),
        input_output_aliases={12 + i: i for i in range(len(before))},
        out_specs=out_specs,
        out_shape=out_shape,
        scratch_shapes=scratch,
        compiler_params=params(),
        cost_estimate=BRIEF,
        name="ff_half_%d" % half,
    )(normed, gbranch, branch_in, gnorm_in, up, upb, down, midb, cot, table, clip_col, downb, *before)


def put(grads, core, quarter, value):
    rows = pl.ds((quarter % 2) * value.shape[0], value.shape[0])
    value = value.astype(BF)
    for target, owner in zip(grads, (quarter // 2, 1 - quarter // 2)):

        @pl.when(core == owner)
        def _(target=target):
            target[rows, :] = value


def this_core():
    return lax.rem(lax.axis_index("seq"), 2)


def qkv_back(normed, grad_packed, wqkv_ref, grads, gqv_ref, gnorm, width):
    for c in range(3):
        cols = pl.ds(c * width, width)
        gp = grad_packed[:, cols]
        put(grads, this_core(), c, dot_tn(normed[...], gp))
        if c != 1:
            gqv_ref[c // 2 : c // 2 + 1, :] = jnp.sum(gp.astype(F32), axis=0, keepdims=True)
        back = dot_nt(gp, wqkv_ref[:, cols])
        gnorm[...] = back if c == 0 else gnorm[...] + back


def owner_backward_kernel(
    xa_ref, packed_ref, attended_ref, branch_ref, gmid_ref, table_ref, clip_col_ref, ids_row_ref,
    wqkv_ref, wout_ref,
    send_ref, kept_ref, other_ref, gclip_ref, goutb_ref, gqv_ref,
    stage, normed, gbranch, gatt, gpacked, bias, gnorm,
):
    frames, pos, width = send_ref.shape
    rows = frames * pos
    blocks = rows // BLOCK
    per_block = BLOCK // frames
    clips = table_ref.shape[1]
    clip_col = clip_col_ref[...]

    def modvec(member):
        return spread(frame_rows(table_ref, member, clip_col), per_block)

    shift, scale, gate = modvec(0), modvec(1), modvec(2)
    bias[...] = time_mask(ids_row_ref, clip_col, per_block, clips)
    gate_sum = 0.0
    for b in range(blocks):
        part = pl.ds(b * BLOCK, BLOCK)
        gm = gmid_ref[part, :]
        gate_sum = gate_sum + gather_frames(branch_ref[part, :] * gm, frames)
        gb = (gate * gm).astype(BF)
        gbranch[part, :] = gb
        gatt[part, :] = dot_nt(gb, wout_ref[...]).astype(BF)
        n, _ = normalize(xa_ref[part, :].astype(F32))
        normed[part, :] = (n * (1.0 + scale) + shift).astype(BF)
    per_clip_sums(gclip_ref, 2, gate_sum, clip_col)
    goutb_ref[...] = jnp.sum(gbranch[...].astype(F32), axis=0, keepdims=True)
    grads = (kept_ref, other_ref)
    put(grads, this_core(), 3, dot_tn(attended_ref[...], gbranch[...]))
    attend_back(packed_ref, gatt, gpacked, lambda b: bias[...], blocks, width)
    qkv_back(normed, gpacked, wqkv_ref, grads, gqv_ref, gnorm, width)
    sums = [0.0, 0.0]
    for b in range(blocks):
        part = pl.ds(b * BLOCK, BLOCK)
        n, r = normalize(xa_ref[part, :].astype(F32))
        g = gnorm[part, :]
        sums[0] = sums[0] + gather_frames(g, frames)
        sums[1] = sums[1] + gather_frames(g * n, frames)
        total = gmid_ref[part, :] + normalize_back(n, r, g * (1.0 + scale))
        stage_positions(stage, total, frames, pos, b * per_block)
    to_frames(stage, send_ref)
    for member in range(2):
        per_clip_sums(gclip_ref, member, sums[member], clip_col)


def owner_backward(xa, packed, attended, branch, gmid, table, clip_col, ids_row, wqkv, wout):
    frames = clip_col.shape[0]
    rows, width = xa.shape
    clips = table.shape[1]
    return pl.pallas_call(
        owner_backward_kernel,
        in_specs=[vmem()] * 10,
        out_specs=[vmem()] * 6,
        out_shape=[
            jax.ShapeDtypeStruct((frames, rows // frames, width), BF),
            jax.ShapeDtypeStruct((2 * width, width), BF),
            jax.ShapeDtypeStruct((2 * width, width), BF),
            jax.ShapeDtypeStruct((3, clips, width), F32),
            jax.ShapeDtypeStruct((1, width), F32),
            jax.ShapeDtypeStruct((2, width), F32),
        ],
        scratch_shapes=[
            pltpu.VMEM((width // LANES, rows, LANES), F32),
            pltpu.VMEM((rows, width), BF),
            pltpu.VMEM((rows, width), BF),
            pltpu.VMEM((rows, width), BF),
            pltpu.VMEM((rows, 3 * width), BF),
            pltpu.VMEM((BLOCK, BLOCK), F32),
            pltpu.VMEM((rows, width), F32),
        ],
        compiler_params=params(),
        cost_estimate=LONG,
        name="owner_backward",
    )(xa, packed, attended, branch, gmid, table, clip_col, ids_row, wqkv, wout)


def space_backward_kernel(
    clip_ref, box_ref, x_ref, packed_ref, attended_ref, branch_ref, gmid_ref, table_ref,
    wqkv_ref, wout_ref, t_ref, gclip_b_ref, gclip_c_ref, gqv_b_ref, goutb_b_ref, gupb_0_ref, gupb_1_ref,
    gdownb_ref,
    gx_ref, kept_ref, other_ref, small_ref,
    normed, gbranch, gatt, gpacked, gnorm, goutb_ref, gqv_ref,
):
    frames = box_ref.shape[0]
    width = x_ref.shape[1]
    clips = table_ref.shape[1]
    clip = own_clips(clip_ref, frames)
    sums = [[None] * frames for _ in range(3)]
    for f in range(frames):
        part = pl.ds(f * BLOCK, BLOCK)
        gm = gmid_ref[:, f].reshape(BLOCK, width).astype(F32)
        sums[2][f] = jnp.sum(branch_ref[part, :] * gm, axis=0, keepdims=True)
        gb = (frame_row(table_ref, 2, clip[f]) * gm).astype(BF)
        gbranch[part, :] = gb
        gatt[part, :] = dot_nt(gb, wout_ref[...]).astype(BF)
        n, _ = normalize(x_ref[part, :].astype(F32))
        shift = frame_row(table_ref, 0, clip[f])
        scale = frame_row(table_ref, 1, clip[f])
        normed[part, :] = (n * (1.0 + scale) + shift).astype(BF)
    goutb_ref[...] = jnp.sum(gbranch[...].astype(F32), axis=0, keepdims=True)
    grads = (kept_ref, other_ref)
    put(grads, this_core(), 3, dot_tn(attended_ref[...], gbranch[...]))
    biases = [visible_bias(box_ref, f, BLOCK) for f in range(frames)]
    attend_back(packed_ref, gatt, gpacked, lambda b: biases[b], frames, width)
    qkv_back(normed, gpacked, wqkv_ref, grads, gqv_ref, gnorm, width)
    for f in range(frames):
        part = pl.ds(f * BLOCK, BLOCK)
        n, r = normalize(x_ref[part, :].astype(F32))
        g = gnorm[part, :]
        sums[0][f] = jnp.sum(g, axis=0, keepdims=True)
        sums[1][f] = jnp.sum(g * n, axis=0, keepdims=True)
        scale = frame_row(table_ref, 1, clip[f])
        gm = gmid_ref[:, f].reshape(BLOCK, width).astype(F32)
        gx_ref[part, :] = (gm + normalize_back(n, r, g * (1.0 + scale))).astype(BF)
    all_clips = clips * lax.axis_size("dp")
    mine = lax.axis_index("dp") * clips
    small_ref[...] = jnp.zeros_like(small_ref)
    for member in range(9):
        for c in range(clips):
            if member < 3:
                total = jnp.zeros((1, width), F32)
                for f in range(frames):
                    total = total + jnp.where(clip[f] == c, sums[member][f], 0.0)
            else:
                source = gclip_b_ref if member < 6 else gclip_c_ref
                total = source[member % 3, c : c + 1, :]
            small_ref[pl.ds(member * all_clips + mine + c, 1), :] = total
    at = 9 * all_clips
    t = jnp.where(lax.axis_index("seq") == 0, t_ref[...].astype(F32), 0.0)
    for c in range(clips):
        small_ref[pl.ds(at + mine + c, 1), :] = t[c : c + 1]
    at += all_clips
    for source in (gqv_ref, goutb_ref, gqv_b_ref, goutb_b_ref, gupb_0_ref, gupb_1_ref, gdownb_ref):
        for i in range(source.shape[0]):
            small_ref[at : at + 1, :] = source[i] if len(source.shape) == 3 else source[i : i + 1, :]
            at += 1


def space_backward(frame_clip, boxes, tokens, *rest):
    rows, width = tokens.shape
    t_embed = rest[7]
    members = rest[-1].shape[0] + sum(value.shape[0] for value in rest[10:-1])
    extra = 3 + 10 * t_embed.shape[0] * lax.axis_size("dp") + members
    return pl.pallas_call(
        space_backward_kernel,
        in_specs=[smem(), smem()] + [vmem()] * (1 + len(rest)),
        out_specs=[vmem()] * 4,
        out_shape=[
            jax.ShapeDtypeStruct((rows, width), BF),
            jax.ShapeDtypeStruct((2 * width, width), BF),
            jax.ShapeDtypeStruct((2 * width, width), BF),
            jax.ShapeDtypeStruct((-(-extra // 8) * 8, width), F32),
        ],
        scratch_shapes=[
            pltpu.VMEM((rows, width), BF),
            pltpu.VMEM((rows, width), BF),
            pltpu.VMEM((rows, width), BF),
            pltpu.VMEM((rows, 3 * width), BF),
            pltpu.VMEM((rows, width), F32),
            pltpu.VMEM((1, width), F32),
            pltpu.VMEM((2, width), F32),
        ],
        compiler_params=params(),
        cost_estimate=LONG,
        name="space_backward",
    )(frame_clip, boxes, tokens, *rest)


def routes(owners):
    depth = owners // 4
    places = [
        (x, z, y, c) for x in range(2) for z in range(depth) for y in range(2) for c in range(2)
    ]
    number = lambda x, z, y, c: x * owners + (z * 2 + y) * 2 + c
    pairs = lambda move: [(number(*p), number(*move(*p))) for p in places]
    over_x = lambda x, z, y, c: (1 - x, z, y, c)
    over_y = lambda x, z, y, c: (x, z, 1 - y, c)
    return {
        "core": pairs(lambda x, z, y, c: (x, z, y, 1 - c)),
        "first": pairs(lambda *p: (over_y if p[3] else over_x)(*p)),
        "second": pairs(lambda *p: (over_x if p[3] else over_y)(*p)),
        "x": pairs(over_x),
        "y": pairs(over_y),
        "depth": [
            pairs(lambda x, z, y, c, s=s: (x, (z + s) % depth, y, c)) for s in range(1, depth)
        ],
        "swap": [
            pairs(lambda x, z, y, c, s=s: (x, z ^ s, y, c))
            for s in (1 << i for i in range(depth.bit_length() - 1))
        ],
    }


def place():
    x, s = lax.axis_index("dp"), lax.axis_index("seq")
    return x, s >> 2, (s >> 1) & 1, s & 1


def move(value, pairs):
    return lax.ppermute(value, BOTH, pairs)


def tie(*values):
    return lax.optimization_barrier(values)


def hbm():
    return pl.BlockSpec(memory_space=pltpu.HBM)


def dma(count):
    return pltpu.SemaphoreType.DMA((count,))


def copies(pairs, semaphores):
    started = [
        pltpu.make_async_copy(source, target, semaphores.at[i])
        for i, (source, target) in enumerate(pairs)
    ]
    for copy in started:
        copy.start()
    return started


def side(stage, core):
    x, _, y, _ = place()
    return jnp.where(core == stage, x, y)


def cross_kernel(stage, kept_ref, got_ref, send_ref, out_ref, a, b, total, sem_a, sem_b, sem_out):
    count, rows, _ = total.shape
    each = count // 2
    bit = side(stage, place()[3])
    spots = [(half, pl.ds(i * rows, rows)) for half in (1 - bit, bit) for i in range(each)]
    from_a = copies([(kept_ref.at[h, r], a.at[i]) for i, (h, r) in enumerate(spots)], sem_a)
    from_b = copies([(got_ref.at[h, r], b.at[i]) for i, (h, r) in enumerate(spots)], sem_b)
    out = []
    for i, (_, r) in enumerate(spots):
        from_a[i].wait()
        from_b[i].wait()
        total[i] = (a[i].astype(F32) + b[i].astype(F32)).astype(BF)
        target = (send_ref if i < each else out_ref).at[r]
        out += copies([(total.at[i], target)], sem_out.at[pl.ds(i, 1)])
    for copy in out:
        copy.wait()


def cross_sum(cost, stage, kept, got):
    height, width = kept.shape[0] // 2, kept.shape[1]
    each = max(1, height // 384)
    buffer = pltpu.VMEM((2 * each, height // each, width), BF)
    half = jax.ShapeDtypeStruct((height, width), BF)
    return pl.pallas_call(
        functools.partial(cross_kernel, stage),
        in_specs=[hbm(), hbm()],
        out_specs=[hbm(), hbm()],
        out_shape=[half, half],
        scratch_shapes=[buffer] * 3 + [dma(2 * each)] * 3,
        compiler_params=alone(),
        cost_estimate=cost,
        name="cross_sum",
    )(kept.reshape(2, height, width), got.reshape(2, height, width))


def along_kernel(kept_ref, got_ref, *refs):
    depth = kept_ref.shape[0]
    targets = refs[:depth]
    a, b, total, sem_a, sem_b, sem_out = refs[depth:]
    z = place()[1]
    turns = list(range(1, depth)) + [0]
    parts = [lax.rem(z + s, depth) for s in turns]
    from_a = copies([(kept_ref.at[p], a.at[i]) for i, p in enumerate(parts)], sem_a)
    from_b = copies([(got_ref.at[p], b.at[i]) for i, p in enumerate(parts)], sem_b)
    out = []
    for i, s in enumerate(turns):
        from_a[i].wait()
        from_b[i].wait()
        total[i] = (a[i].astype(F32) + b[i].astype(F32)).astype(BF)
        out += copies([(total.at[i], targets[s])], sem_out.at[pl.ds(i, 1)])
    for copy in out:
        copy.wait()


def along_sum(cost, depth, kept, got):
    height, width = kept.shape[0] // depth, kept.shape[1]
    buffer = pltpu.VMEM((depth, height, width), BF)
    return pl.pallas_call(
        along_kernel,
        in_specs=[hbm()] * 2,
        out_specs=[hbm()] * depth,
        out_shape=[jax.ShapeDtypeStruct((height, width), BF)] * depth,
        scratch_shapes=[buffer] * 3 + [dma(depth)] * 3,
        compiler_params=alone(),
        cost_estimate=cost,
        name="along_sum",
    )(kept.reshape(depth, height, width), got.reshape(depth, height, width))


def finish_kernel(*refs):
    total = refs[0][...].astype(F32)
    for ref in refs[1:-1]:
        total = total + ref[...].astype(F32)
    refs[-1][...] = total.astype(refs[-1].dtype)


def finish_sum(cost, *parts):
    return pl.pallas_call(
        finish_kernel,
        in_specs=[vmem()] * len(parts),
        out_specs=vmem(),
        out_shape=jax.ShapeDtypeStruct(parts[0].shape, parts[0].dtype),
        compiler_params=alone(),
        cost_estimate=cost,
        name="finish_sum",
    )(*parts)


def collect_kernel(*refs):
    *parts, target, held, sem_in, sem_out = refs
    depth = target.shape[0]
    z = place()[1]
    for copy in copies(
        [(ref, held.at[lax.rem(z + depth - s, depth)]) for s, ref in enumerate(parts)], sem_in
    ):
        copy.wait()
    copies([(held, target)], sem_out)[0].wait()


def collect(cost, *parts):
    depth = len(parts)
    height, width = parts[0].shape
    return pl.pallas_call(
        collect_kernel,
        in_specs=[hbm()] * depth,
        out_specs=hbm(),
        out_shape=jax.ShapeDtypeStruct((depth, height, width), BF),
        scratch_shapes=[pltpu.VMEM((depth, height, width), BF), dma(depth), dma(1)],
        compiler_params=alone(),
        cost_estimate=cost,
        name="collect",
    )(*parts).reshape(depth * height, width)


class Sum:
    def __init__(self, kept, other, route):
        self.route = route
        self.kept = kept
        self.wait = move(other, route["core"])

    def cross(self, stage):
        send, self.kept = cross_sum(self.cost, stage, self.kept, self.wait)
        self.wait = move(send, self.route[("first", "second")[stage]])
        return "kept"

    def along(self):
        self.kept, *send = along_sum(self.cost, len(self.route["depth"]) + 1, self.kept, self.wait)
        self.wait = tuple(move(part, pairs) for part, pairs in zip(send, self.route["depth"]))
        return "kept"

    def finish(self):
        self.kept = finish_sum(self.cost, self.kept, *self.wait)
        self.wait = tuple(move(self.kept, pairs) for pairs in self.route["depth"])
        return "kept"

    def gather(self):
        self.near = collect(self.cost, self.kept, *self.wait)
        self.wait, self.across, self.core = (
            move(self.near, self.route[link]) for link in ("second", "first", "core")
        )
        return "near"

    def relay(self):
        self.far = self.wait
        got, self.core_far = (move(self.far, self.route[link]) for link in ("first", "core"))
        self.wait = (self.across, got)
        return "far"

    def reflect(self):
        self.across, self.across_far = self.wait
        self.wait = (self.core, self.core_far) + tuple(
            move(value, self.route["core"]) for value in self.wait
        )
        return "across"


class Order:
    def __init__(self):
        self.before = None
        self.cost = BRIEF

    def after(self, value):
        if self.before is not None:
            owner, name = self.before
            flat = value if isinstance(value, tuple) else (value,)
            *flat, late = tie(*flat, getattr(owner, name))
            setattr(owner, name, late)
            value = tuple(flat) if isinstance(value, tuple) else flat[0]
        return value

    def run(self, total, step, *args):
        total.cost = self.cost
        total.wait = self.after(total.wait)
        self.before = (total, getattr(total, step)(*args))


class Held:
    def __init__(self, value):
        self.value = value


def widen_kernel(other, spots, *refs):
    sources, (first_ref, second_ref), (held, wide, sem_in, sem_out) = refs[:4], refs[-6:-4], refs[-4:]
    height, width = held.shape[1:]
    loads = copies([(ref, held.at[i]) for i, ref in enumerate(sources)], sem_in)
    core = place()[3] ^ other
    stores = []
    for i, load in enumerate(loads):
        near, far = side(0, core) ^ (i >> 1), side(1, core) ^ (i & 1)
        block = core * 4 + near * 2 + far
        load.wait()
        wide[i] = held[i].astype(F32)
        in_first, (row, column), (row_2, column_2) = spots(block)
        place_1 = first_ref.at[
            pl.ds(pl.multiple_of(row * height, height), height),
            pl.ds(pl.multiple_of(column * width, width), width),
        ]
        place_2 = second_ref.at[
            pl.ds(pl.multiple_of(row_2 * height, height), height),
            pl.ds(pl.multiple_of(column_2 * width, width), width),
        ]
        store_1 = pltpu.make_async_copy(wide.at[i], place_1, sem_out.at[i])
        store_2 = pltpu.make_async_copy(wide.at[i], place_2, sem_out.at[i])
        pl.when(in_first)(store_1.start)
        pl.when(jnp.logical_not(in_first))(store_2.start)
        stores.append((in_first, store_1, store_2))
    for in_first, store_1, store_2 in stores:
        pl.when(in_first)(store_1.wait)
        pl.when(jnp.logical_not(in_first))(store_2.wait)


def widen(cost, other, parts, spots, shapes, before=()):
    height, width = parts[0].shape
    return pl.pallas_call(
        functools.partial(widen_kernel, other, spots),
        in_specs=[hbm()] * (4 + len(before)),
        out_specs=[hbm()] * 2,
        out_shape=[jax.ShapeDtypeStruct(shape, F32) for shape in shapes],
        input_output_aliases={4 + i: i for i in range(len(before))},
        scratch_shapes=[
            pltpu.VMEM((4, height, width), BF),
            pltpu.VMEM((4, height, width), F32),
            dma(4),
            dma(4),
        ],
        compiler_params=alone(),
        cost_estimate=cost,
        name="widen",
    )(*parts, *before)


def spots_of(split, first, second):
    def spots(block):
        return (
            block < split,
            first(jnp.minimum(block, split - 1)),
            second(jnp.maximum(block - split, 0)),
        )

    return spots


def widen_plain_kernel(split, maps, in_ref, first_ref, second_ref, held, wide, sem_in, sem_out):
    count, height, width = held.shape
    loads = copies(
        [(in_ref.at[pl.ds(i * height, height)], held.at[i]) for i in range(count)], sem_in
    )
    stores = []
    for i, load in enumerate(loads):
        load.wait()
        wide[i] = held[i].astype(F32)
        row, column = maps[0](i) if i < split else maps[1](i - split)
        target = (first_ref if i < split else second_ref).at[
            pl.ds(row * height, height), pl.ds(column * width, width)
        ]
        stores += copies([(wide.at[i], target)], sem_out.at[pl.ds(i, 1)])
    for store in stores:
        store.wait()


def widen_plain(summed, split, shapes, maps):
    width = summed.shape[1]
    height = summed.shape[0] // 8
    return pl.pallas_call(
        functools.partial(widen_plain_kernel, split, maps),
        in_specs=[hbm()],
        out_specs=[hbm()] * 2,
        out_shape=[jax.ShapeDtypeStruct(shape, F32) for shape in shapes],
        scratch_shapes=[
            pltpu.VMEM((8, height, width), BF),
            pltpu.VMEM((8, height, width), F32),
            dma(8),
            dma(8),
        ],
        compiler_params=alone(),
        cost_estimate=BRIEF,
        name="widen_plain",
    )(summed)


def mod_weight_kernel(t_ref, g_ref, out_ref, smooth, parts, wide, sem_out):
    members, clips, width = g_ref.shape
    t = t_ref[...]
    value = (t / (1.0 + jnp.exp(-t))).astype(BF).astype(F32)
    smooth[...] = jnp.zeros_like(smooth)
    parts[...] = jnp.zeros_like(parts)
    for i in range(3):
        smooth[i * clips : (i + 1) * clips, :] = value
    left = smooth[...].astype(BF)
    slots = wide.shape[0]
    stores = []
    for member in range(members):
        rest = g_ref[member]
        for i in range(3):
            piece = rest.astype(BF).astype(F32)
            parts[i * clips : (i + 1) * clips, :] = piece
            rest = rest - piece
        if member >= slots:
            stores[member - slots].wait()
        wide[member % slots] = dot_tn(left, parts[...].astype(BF))
        target = out_ref.at[:, pl.ds(member * width, width)]
        stores += copies([(wide.at[member % slots], target)], sem_out.at[pl.ds(member, 1)])
    for store in stores[-slots:]:
        store.wait()


def mod_weight_grad(t_all, grad_clip):
    clips, width = t_all.shape
    members = grad_clip.shape[0]
    deep = -(-3 * clips // 16) * 16
    return pl.pallas_call(
        mod_weight_kernel,
        in_specs=[vmem(), vmem()],
        out_specs=hbm(),
        out_shape=jax.ShapeDtypeStruct((width, members * width), F32),
        scratch_shapes=[pltpu.VMEM((deep, width), F32)] * 2
        + [pltpu.VMEM((5, width, width), F32), dma(members)],
        compiler_params=alone(),
        cost_estimate=BRIEF,
        name="mod_weight_grad",
    )(t_all, grad_clip)


def per_device(
    tokens, t_embed, frame_clip, boxes, mod_weight, mod_bias, space_qkv, space_qv_bias, space_out,
    space_out_bias, time_qkv, time_qv_bias, time_out, time_out_bias, up_weight, up_bias,
    down_weight, down_bias, cotangent,
):
    owners = lax.axis_size("seq")
    groups = lax.axis_size("dp")
    frames = boxes.shape[0]
    width = tokens.shape[1]
    patches = tokens.shape[0] // frames
    group_frames = frame_clip.shape[0]
    pos = patches // owners
    clips = t_embed.shape[0]
    ff = up_weight.shape[1]
    depth = owners // 4
    own_route = depth <= 4
    route = routes(owners)

    clip_col = frame_clip[:, None]
    per_block = BLOCK // group_frames
    ids_row = (
        jnp.arange(per_block, dtype=jnp.int32)[:, None] * clips + frame_clip[None, :]
    ).reshape(1, BLOCK)

    def exchange(x):
        return lax.all_to_all(x, "seq", split_axis=0, concat_axis=0, tiled=True)

    qkv_maps = (lambda i: (i % 2, i // 2), lambda i: (i, 0))

    cot_send = cotangent.reshape(frames, owners, pos, width).transpose(1, 0, 2, 3)
    cot = exchange(cot_send)
    table_a = modulation(t_embed, mod_weight, mod_bias, 0, 3)
    mid_send, packed_a, attended_a, branch_a = space_forward(
        frame_clip, boxes, tokens, table_a, space_qkv, space_qv_bias, space_out, space_out_bias, owners,
    )
    mid_send, cot, t_late = tie(mid_send, cot, t_embed)
    mid = exchange(mid_send).reshape(group_frames, pos, width)
    cot = cot.reshape(group_frames, pos, width)
    table = modulation(t_late, mod_weight, mod_bias, 3, 6)
    xa, packed_b, attended_b, branch_b, mid_b, normed_c, gbranch_c, cot, gdown_b = time_forward(
        mid, cot, table, clip_col, ids_row, time_qkv, time_qv_bias, time_out, time_out_bias
    )
    ff_args = (up_weight, up_bias, down_weight, mid_b, cot, table, clip_col, down_bias)
    grad_f, gup_b0, branch_c, gnorm_c = ff_half(0, normed_c, gbranch_c, None, None, *ff_args)
    ff_shapes = ((width, ff), (ff, width))
    qkv_shapes = ((width, 3 * width), (width, width))
    qkv_spots = spots_of(6, lambda i: (i % 2, i // 2), lambda i: (i, 0))
    all_clips = clips * groups

    def mod_grads(small):
        gclip = small[: 9 * all_clips].reshape(9, all_clips, width)
        return mod_weight_grad(small[9 * all_clips : 10 * all_clips], gclip), jnp.sum(gclip, axis=1)

    def after_ff(gmid_b):
        return owner_backward(
            xa, packed_b, attended_b, branch_b, gmid_b, table, clip_col, ids_row, time_qkv, time_out
        )

    def after_time(gmid_a, gclip_b, gtout_b, gtqv_b):
        return space_backward(
            frame_clip, boxes, tokens, packed_a, attended_a, branch_a, gmid_a, table_a, space_qkv,
            space_out, t_embed, gclip_b, gclip_c, gtqv_b, gtout_b, gup_b0, gup_b1, gdown_b,
        )

    grad_f, gup_b1, gmid_b, result_send, gclip_c = ff_half(
        1, normed_c, gbranch_c, branch_c, gnorm_c, *ff_args, grad_f
    )
    result_send = result_send.reshape(owners, frames, pos, width)
    grad_f = grad_f.reshape(-1, width)
    part_f = Held(lax.psum_scatter(grad_f, BOTH, scatter_dimension=0, tiled=True))
    if own_route:
        sums = {}
        order = Order()
        wide = {}
        small = Held(None)
        small_links = [route["core"], route["x"], route["y"]] + route["swap"]
        for name, *step in SCHEDULE:
            if name == "time":
                gmid_b = order.after(gmid_b)
                gmid_send, kept_t, other_t, gclip_b, gtout_b, gtqv_b = after_ff(gmid_b)
                result = exchange(result_send)
                gmid_send, result = tie(gmid_send, result)
                gmid_a = exchange(gmid_send.reshape(owners, frames, pos, width))
                sums["t"] = Sum(kept_t, other_t, route)
                order.before = None
            elif name == "space":
                gmid_a = order.after(gmid_a)
                grad_tokens, kept_s, other_s, small.value = after_time(
                    gmid_a, gclip_b, gtout_b, gtqv_b
                )
                sums["s"] = Sum(kept_s, other_s, route)
                order.before = None
                order.cost = LONG
            elif name == "ff":
                part_f.value = order.after(part_f.value)
                order.before = (part_f, "value")
            elif name == "small":
                small.value = order.after(small.value)
                small.value = finish_sum(order.cost, small.value, move(small.value, small_links.pop(0)))
                order.before = (small, "value")
            elif name == "mod":
                small.value = order.after(small.value)
                grad_mod, grad_mod_b = mod_grads(small.value)
                mod = Held(grad_mod)
                order.before = (mod, "value")
            elif step[0] == "widen":
                total = sums[name]
                if step[1]:
                    total.wait = order.after(total.wait)
                    parts = total.wait
                else:
                    total.across = order.after(total.across)
                    parts = (total.near, total.far, total.across, total.across_far)
                before = (wide[name].value, wide[name].other) if name in wide else ()
                pair = widen(order.cost, step[1], parts, qkv_spots, qkv_shapes, before)
                done = wide[name] = Held(pair[0])
                done.other = pair[1]
                order.before = (done, "value")
            else:
                order.run(sums[name], *step)
                order.cost = BRIEF
        small, grad_mod = small.value, mod.value
        wide_time, wide_space = ((wide[k].value, wide[k].other) for k in ("t", "s"))
    else:
        result = exchange(result_send)
        gmid_send, kept_t, other_t, gclip_b, gtout_b, gtqv_b = after_ff(gmid_b)
        gmid_a = exchange(gmid_send.reshape(owners, frames, pos, width))
        grad_tokens, kept_s, other_s, small = after_time(gmid_a, gclip_b, gtout_b, gtqv_b)
        small = lax.psum(small, BOTH)
        grad_mod, grad_mod_b = mod_grads(small)
        core = place()[3]

        def whole(kept, other):
            halves = [jnp.where(core == half, kept, other) for half in range(2)]
            return lax.psum(jnp.concatenate(halves, axis=0), BOTH)

        qkv_maps = (lambda i: (i % 2, i // 2), lambda i: (i, 0))
        wide_time = widen_plain(whole(kept_t, other_t), 6, qkv_shapes, qkv_maps)
        wide_space = widen_plain(whole(kept_s, other_s), 6, qkv_shapes, qkv_maps)
    sum_f = lax.all_gather(part_f.value, BOTH, axis=0, tiled=True)
    wide_ff = widen_plain(sum_f, 4, ff_shapes, (lambda i: (0, i), lambda i: (i, 0)))
    rest = small[10 * all_clips :]
    cut = lambda start, count: rest[start : start + count].reshape(-1)
    up_rows = ff // width
    return (
        result.transpose(1, 0, 2, 3).reshape(tokens.shape),
        grad_tokens,
        grad_mod,
        grad_mod_b.reshape(-1),
        wide_space[0],
        cut(0, 2),
        wide_space[1],
        cut(2, 1),
        wide_time[0],
        cut(3, 2),
        wide_time[1],
        cut(5, 1),
        wide_ff[0],
        cut(6, up_rows),
        wide_ff[1],
        cut(6 + up_rows, 1),
    )


def solution(mesh):
    split = P(BOTH, None)
    placed = (split, P("dp", None), P("dp"), split) + (P(),) * 14 + (split,)
    return jax.shard_map(
        per_device,
        mesh=mesh,
        in_specs=placed,
        out_specs=(split, split) + (P(),) * 14,
        check_vma=False,
    )
```

```python
import functools

import jax
import jax.numpy as jnp
from jax import lax
from jax.experimental import pallas as pl
from jax.experimental.pallas import tpu as pltpu
from jax.sharding import PartitionSpec as P

HD = 64
GRID_W = 16
EPS = 1e-06
NEG = -1e30
BLOCK = 256
LANES = 128
BF = jnp.bfloat16
F32 = jnp.float32
VMEM_BYTES = 56 * 1024 * 1024
BOTH = ("dp", "seq")
BRIEF = pl.CostEstimate(flops=1000, bytes_accessed=1000, transcendentals=0)
MIDDLE = pl.CostEstimate(flops=10**10, bytes_accessed=1000, transcendentals=0)
LONG = pl.CostEstimate(flops=3 * 10**10, bytes_accessed=1000, transcendentals=0)

COSTS = {
    ("t", "cross", 1): LONG,
    ("t", "along"): MIDDLE,
    ("t", "finish"): MIDDLE,
    ("s", "along"): MIDDLE,
    ("t", "gather"): MIDDLE,
    ("s", "finish"): MIDDLE,
    ("s", "gather"): MIDDLE,
}
SCHEDULE = (
    ("time",),
    ("t", "cross", 0),
    ("space",),
    ("t", "cross", 1),
    ("s", "cross", 0),
    ("t", "along"),
    ("s", "cross", 1),
    ("t", "finish"),
    ("s", "along"),
    ("t", "gather"),
    ("s", "finish"),
    ("ff",),
    ("t", "relay"),
    ("s", "gather"),
    ("t", "reflect"),
    ("t", "widen", 0),
    ("s", "relay"),
    ("t", "widen", 1),
    ("s", "reflect"),
    ("s", "widen", 0),
    ("s", "widen", 1),
)


def params():
    return pltpu.CompilerParams(vmem_limit_bytes=VMEM_BYTES)


def alone():
    return pltpu.CompilerParams(vmem_limit_bytes=60 * 1024 * 1024)


def dot_nn(a, b):
    return lax.dot_general(a, b, (((1,), (0,)), ((), ())), preferred_element_type=F32)


def dot_nt(a, b):
    return lax.dot_general(a, b, (((1,), (1,)), ((), ())), preferred_element_type=F32)


def dot_tn(a, b):
    return lax.dot_general(a, b, (((0,), (0,)), ((), ())), preferred_element_type=F32)


def normalize(x):
    center = x - jnp.mean(x, axis=-1, keepdims=True)
    r = lax.rsqrt(jnp.mean(center * center, axis=-1, keepdims=True) + EPS)
    return center * r, r


def normalize_back(n, r, m):
    return r * (
        m - jnp.mean(m, axis=-1, keepdims=True) - n * jnp.mean(m * n, axis=-1, keepdims=True)
    )


def head_halves(width):
    lane = lax.broadcasted_iota(jnp.int32, (1, width), 1)
    low = (lane < HD).astype(F32).astype(BF)
    return low, (lane >= HD).astype(F32).astype(BF)


def attend(packed, attended, bias, blocks, width):
    halves = head_halves(2 * HD)

    def pair(index, carry):
        off = pl.multiple_of(index * 2 * HD, 2 * HD)
        for b in range(blocks):
            rows = pl.ds(b * BLOCK, BLOCK)
            q = packed[rows, pl.ds(off, 2 * HD)]
            k = packed[rows, pl.ds(width + off, 2 * HD)]
            v = packed[rows, pl.ds(2 * width + off, 2 * HD)]
            out = None
            for half in halves:
                s = dot_nt(q, k * half) * (HD**-0.5) + bias(b)
                e = jnp.exp(s - jnp.max(s, axis=-1, keepdims=True))
                p = (e * (1.0 / jnp.sum(e, axis=-1, keepdims=True))).astype(BF)
                o = dot_nn(p, v * half)
                out = o if out is None else out + o
            attended[rows, pl.ds(off, 2 * HD)] = out.astype(BF)
        return carry

    lax.fori_loop(0, width // (2 * HD), pair, 0)


def attend_back(packed, grad_in, grad_packed, bias, blocks, width):
    halves = head_halves(2 * HD)
    factor = HD**-0.5

    def pair(index, carry):
        off = pl.multiple_of(index * 2 * HD, 2 * HD)
        for b in range(blocks):
            rows = pl.ds(b * BLOCK, BLOCK)
            q = packed[rows, pl.ds(off, 2 * HD)]
            k = packed[rows, pl.ds(width + off, 2 * HD)]
            v = packed[rows, pl.ds(2 * width + off, 2 * HD)]
            g = grad_in[rows, pl.ds(off, 2 * HD)]
            dq = dk = dv = 0.0
            for half in halves:
                kh = k * half
                s = dot_nt(kh, q) * factor + bias(b)
                e = jnp.exp(s - jnp.max(s, axis=0, keepdims=True))
                p = e * (1.0 / jnp.sum(e, axis=0, keepdims=True))
                gs = dot_nt(v * half, g)
                ds = (p * (gs - jnp.sum(p * gs, axis=0, keepdims=True))).astype(BF)
                dv = dv + dot_nn(p.astype(BF), g * half)
                dq = dq + dot_tn(ds, kh)
                dk = dk + dot_nn(ds, q * half)
            grad_packed[rows, pl.ds(off, 2 * HD)] = (dq * factor).astype(BF)
            grad_packed[rows, pl.ds(width + off, 2 * HD)] = (dk * factor).astype(BF)
            grad_packed[rows, pl.ds(2 * width + off, 2 * HD)] = dv.astype(BF)
        return carry

    lax.fori_loop(0, width // (2 * HD), pair, 0)


def project_qkv(normed, weight, qv_bias, packed, width):
    for c in range(3):
        cols = pl.ds(c * width, width)
        value = dot_nn(normed[...], weight[:, cols])
        if c != 1:
            value = value + as_row(qv_bias[pl.ds((c // 2) * width, width)])
        packed[:, cols] = value.astype(BF)


def modulation_kernel(first, t_ref, w_ref, b_ref, out_ref):
    t = t_ref[...].astype(F32)
    smooth = (t / (1.0 + jnp.exp(-t))).astype(BF)
    bias = chunk_row(b_ref, first + pl.program_id(0), t.shape[1])
    out_ref[0] = dot_nn(smooth, w_ref[...]) + bias


def modulation(t_embed, weight, bias, first, count):
    clips, width = t_embed.shape
    return pl.pallas_call(
        functools.partial(modulation_kernel, first),
        grid=(count,),
        in_specs=[
            pl.BlockSpec((clips, width), lambda i: (0, 0)),
            pl.BlockSpec((width, width), lambda i: (0, first + i)),
            vmem(),
        ],
        out_specs=pl.BlockSpec((1, clips, width), lambda i: (i, 0, 0)),
        out_shape=jax.ShapeDtypeStruct((count, clips, width), F32),
        cost_estimate=BRIEF,
        name="modulation",
    )(t_embed, weight, bias)


def as_row(vector):
    return vector.astype(F32).reshape(1, -1)


def chunk_row(vector_ref, index, width):
    return as_row(vector_ref[pl.ds(pl.multiple_of(index * width, width), width)])


def own_clips(clip_ref, frames):
    first = lax.axis_index("seq") * frames
    return [clip_ref[first + f] for f in range(frames)]


def frame_row(table, member, clip):
    total = jnp.zeros(table.shape[2:], F32)[None]
    for c in range(table.shape[1]):
        total = jnp.where(clip == c, table[member, c : c + 1, :], total)
    return total


def frame_rows(table, member, clip_col):
    total = jnp.zeros((clip_col.shape[0], table.shape[2]), F32)
    for c in range(table.shape[1]):
        total = jnp.where(clip_col == c, table[member, c : c + 1, :], total)
    return total


def visible_bias(box_ref, frame, patches):
    cell = lax.broadcasted_iota(jnp.int32, (1, patches), 1)
    row, col = cell // GRID_W, cell % GRID_W
    inside = (
        (row >= box_ref[frame, 0])
        & (row < box_ref[frame, 1])
        & (col >= box_ref[frame, 2])
        & (col < box_ref[frame, 3])
    )
    return jnp.where(inside, NEG, 0.0)


def space_forward_kernel(
    ready, flush,
    clip_ref, box_ref, t_ref, modw_ref, modb_ref, x_ref, wqkv_ref, bqv_ref, wout_ref, bout_ref,
    send_ref, packed_ref, attended_ref, branch_ref, table_ref, normed,
):
    frames = box_ref.shape[0]
    width = x_ref.shape[1]
    dst, _, pos, _ = send_ref.shape
    clip = own_clips(clip_ref, frames)
    t = t_ref[...].astype(F32)
    smooth = (t / (1.0 + jnp.exp(-t))).astype(BF)
    ready(modw_ref)
    for k in range(3):
        cols = pl.ds(k * width, width)
        table_ref[k] = dot_nn(smooth, modw_ref[:, cols]) + as_row(modb_ref[cols])
    ready(x_ref)
    for f in range(frames):
        rows = pl.ds(f * BLOCK, BLOCK)
        n, _ = normalize(x_ref[rows, :].astype(F32))
        shift = frame_row(table_ref, 0, clip[f])
        scale = frame_row(table_ref, 1, clip[f])
        normed[rows, :] = (n * (1.0 + scale) + shift).astype(BF)
    ready(wqkv_ref)
    project_qkv(normed, wqkv_ref, bqv_ref, packed_ref, width)
    flush(packed_ref)
    biases = [visible_bias(box_ref, f, BLOCK) for f in range(frames)]
    attend(packed_ref, attended_ref, lambda b: biases[b], frames, width)
    flush(attended_ref)
    ready(wout_ref)
    for f in range(frames):
        rows = pl.ds(f * BLOCK, BLOCK)
        branch = dot_nn(attended_ref[rows, :], wout_ref[...]) + as_row(bout_ref[...])
        branch_ref[rows, :] = branch
        gate = frame_row(table_ref, 2, clip[f])
        mid = x_ref[rows, :].astype(F32) + gate * branch
        send_ref[:, f] = mid.astype(BF).reshape(dst, pos, width)
    flush(send_ref, branch_ref)


def vmem():
    return pl.BlockSpec(memory_space=pltpu.VMEM)


def smem():
    return pl.BlockSpec(memory_space=pltpu.SMEM)


def hbm():
    return pl.BlockSpec(memory_space=pltpu.HBM)


def dma(count):
    return pltpu.SemaphoreType.DMA((count,))


def copies(pairs, semaphores):
    started = [
        pltpu.make_async_copy(source, target, semaphores.at[i])
        for i, (source, target) in enumerate(pairs)
    ]
    for copy in started:
        copy.start()
    return started


def streamed(body, args, late, out_shape, late_out, scratch, cost, name, small=0, cut=()):
    cut = dict(cut)
    n, m = len(args), len(out_shape)

    def shape_of(i):
        shape = args[i].shape
        return shape[:-1] + (cut[i],) if i in cut else shape

    def kernel(*refs):
        refs = list(refs)
        ins, outs, rest = refs[:n], refs[n : n + m], refs[n + m :]
        own, rest = rest[: len(scratch)], rest[len(scratch) :]
        in_buffers, out_buffers, (sem_in, sem_out) = rest[: len(late)], rest[len(late) : -2], rest[-2:]
        sources = [ins[i].at[:, pl.ds(0, cut[i])] if i in cut else ins[i] for i in late]
        waiting = list(zip(in_buffers, copies(list(zip(sources, in_buffers)), sem_in)))
        for i, buffer in zip(late, in_buffers):
            ins[i] = buffer
        pending = dict(zip(late_out, out_buffers))
        targets = {i: outs[i] for i in late_out}
        for i in late_out:
            outs[i] = pending[i]
        leaving = []

        def ready(*buffers):
            for buffer in buffers:
                for entry in list(waiting):
                    if entry[0] is buffer:
                        entry[1].wait()
                        waiting.remove(entry)

        def flush(*buffers):
            for buffer in buffers:
                for k, i in enumerate(late_out):
                    if out_buffers[k] is buffer:
                        leaving.extend(copies([(buffer, targets[i])], sem_out.at[pl.ds(k, 1)]))

        body(ready, flush, *ins, *outs, *own)
        for copy in leaving:
            copy.wait()

    in_specs = [smem() if i < small else hbm() if i in late else vmem() for i in range(n)]
    return pl.pallas_call(
        kernel,
        in_specs=in_specs,
        out_specs=[hbm() if i in late_out else vmem() for i in range(m)],
        out_shape=out_shape,
        scratch_shapes=list(scratch)
        + [pltpu.VMEM(shape_of(i), args[i].dtype) for i in late]
        + [pltpu.VMEM(out_shape[i].shape, out_shape[i].dtype) for i in late_out]
        + [dma(max(1, len(late))), dma(max(1, len(late_out)))],
        compiler_params=params(),
        cost_estimate=cost,
        name=name,
    )(*args)


def space_forward(
    frame_clip, boxes, t_embed, mod_weight, mod_bias, tokens, wqkv, bqv, wout, bout, owners
):
    rows, width = tokens.shape
    frames = boxes.shape[0]
    pos = rows // frames // owners
    args = (frame_clip, boxes, t_embed, mod_weight, mod_bias, tokens, wqkv, bqv, wout, bout)
    return streamed(
        space_forward_kernel,
        args,
        (3, 5, 6, 8),
        [
            jax.ShapeDtypeStruct((owners, frames, pos, width), BF),
            jax.ShapeDtypeStruct((rows, 3 * width), BF),
            jax.ShapeDtypeStruct((rows, width), BF),
            jax.ShapeDtypeStruct((rows, width), F32),
            jax.ShapeDtypeStruct((3, t_embed.shape[0], width), F32),
        ],
        (0, 1, 2, 3),
        [pltpu.VMEM((rows, width), BF)],
        BRIEF,
        "space_forward",
        small=2,
        cut=((3, 3 * width),),
    )


def to_positions(source, stage, target):
    frames, pos, width = source.shape
    for lane in range(0, width, LANES):
        cols = pl.ds(lane, LANES)
        stage[lane // LANES] = source[:, :, cols].astype(F32).reshape(frames * pos, LANES)
        for p in range(pos):
            target[pl.ds(p * frames, frames), cols] = stage[
                lane // LANES, pl.ds(p, frames, stride=pos), :
            ].astype(target.dtype)


def stage_positions(stage, value, frames, pos, first):
    for lane in range(0, value.shape[1], LANES):
        for p in range(value.shape[0] // frames):
            stage[lane // LANES, pl.ds(first + p, frames, stride=pos), :] = value[
                p * frames : (p + 1) * frames, lane : lane + LANES
            ]


def to_frames(stage, target):
    frames, pos, width = target.shape
    for lane in range(0, width, LANES):
        target[:, :, pl.ds(lane, LANES)] = (
            stage[lane // LANES].reshape(frames, pos, LANES).astype(BF)
        )


def time_mask(ids_row_ref, clip_col, positions, clips):
    frames = clip_col.shape[0]
    place = lax.broadcasted_iota(jnp.int32, (positions, frames, 1), 0) * clips
    col = (place + clip_col[None]).reshape(positions * frames, 1)
    return jnp.where(col == ids_row_ref[...], 0.0, NEG)


def spread(rows, positions):
    frames, width = rows.shape
    return jnp.broadcast_to(rows[None], (positions, frames, width)).reshape(
        positions * frames, width
    )


def gather_frames(value, frames):
    return jnp.sum(value.reshape(-1, frames, value.shape[-1]), axis=0)


def per_clip_sums(out_ref, member, rows, clip_col):
    for c in range(out_ref.shape[1]):
        out_ref[member, c : c + 1, :] = jnp.sum(
            jnp.where(clip_col == c, rows, 0.0), axis=0, keepdims=True
        )


def gelu_and_slope(v):
    c = 0.7978845608028654
    square = v * v
    t = jnp.tanh(v * (c + (c * 0.044715) * square))
    half = 0.5 + 0.5 * t
    slope = half + (0.5 * v) * (1.0 - t * t) * (c + (3.0 * c * 0.044715) * square)
    return v * half, slope


def owner_forward_kernel(
    mid_ref, cot_ref, table_ref, clip_col_ref, ids_row_ref, wqkv_ref, bqv_ref, wout_ref, bout_ref,
    up_ref, upb_ref, down_ref, downb_ref,
    xa_ref, packed_ref, attended_ref, branch_ref, gmid_ref, result_ref, grad_ref, gclip_ref, gupb_ref,
    gdownb_ref,
    stage, mid, cot, normed, normed_t, gbranch, bias, act, ghid, branch_acc, gnorm_acc,
    cot_in, wqkv, wout, xa, packed, attended, branch_out, sem_in, sem_out,
):
    step = pl.program_id(0)
    frames, pos, width = mid_ref.shape
    blocks = frames * pos // BLOCK
    per_block = BLOCK // frames
    clips = table_ref.shape[1]
    clip_col = clip_col_ref[...]
    leaving = [
        (xa, xa_ref), (packed, packed_ref), (attended, attended_ref), (branch_out, branch_ref)
    ]

    def modvec(member):
        return spread(frame_rows(table_ref, member, clip_col), per_block)

    @pl.when(step == 0)
    def _():
        loads = copies([(wqkv_ref, wqkv), (cot_ref, cot_in), (wout_ref, wout)], sem_in)
        to_positions(mid_ref, stage, mid)
        xa[...] = mid[...].astype(BF)
        copies(leaving[:1], sem_out)
        bias[...] = time_mask(ids_row_ref, clip_col, per_block, clips)
        shift_b, scale_b = modvec(0), modvec(1)
        for b in range(blocks):
            part = pl.ds(b * BLOCK, BLOCK)
            n, _ = normalize(mid[part, :])
            normed[part, :] = (n * (1.0 + scale_b) + shift_b).astype(BF)
        loads[0].wait()
        project_qkv(normed, wqkv, bqv_ref, packed, width)
        copies(leaving[1:2], sem_out.at[pl.ds(1, 1)])
        attend(packed, attended, lambda b: bias[...], blocks, width)
        copies(leaving[2:3], sem_out.at[pl.ds(2, 1)])
        loads[1].wait()
        to_positions(cot_in, stage, cot)
        gate_b, shift_c, scale_c, gate_c = modvec(2), modvec(3), modvec(4), modvec(5)
        loads[2].wait()
        for b in range(blocks):
            part = pl.ds(b * BLOCK, BLOCK)
            branch = dot_nn(attended[part, :], wout[...]) + as_row(bout_ref[...])
            branch_out[part, :] = branch
            mid_b = mid[part, :] + gate_b * branch
            mid[part, :] = mid_b
            n, _ = normalize(mid_b)
            normed[part, :] = (n * (1.0 + scale_c) + shift_c).astype(BF)
            gbranch[part, :] = (gate_c * cot[part, :]).astype(BF)
        copies(leaving[3:], sem_out.at[pl.ds(3, 1)])
        normed_t[...] = normed[...].T
        gdownb_ref[...] = jnp.sum(gbranch[...].astype(F32), axis=0, keepdims=True)
        branch_acc[...] = jnp.zeros_like(branch_acc)
        gnorm_acc[...] = jnp.zeros_like(gnorm_acc)

    up_bias = chunk_row(upb_ref, step, act.shape[1])
    for b in range(blocks):
        part = pl.ds(b * BLOCK, BLOCK)
        hidden = dot_nn(normed[part, :], up_ref[...]) + up_bias
        value, slope = gelu_and_slope(hidden)
        value = value.astype(BF)
        act[part, :] = value
        gh = (dot_nt(gbranch[part, :], down_ref[...]) * slope).astype(BF)
        ghid[part, :] = gh
        branch_acc[part, :] += dot_nn(value, down_ref[...])
        gnorm_acc[part, :] += dot_nt(gh, up_ref[...])
    grad_ref[0] = dot_nn(normed_t[...], ghid[...]).astype(BF)
    grad_ref[1] = dot_tn(act[...], gbranch[...]).astype(BF)
    gupb_ref[0] = jnp.sum(ghid[...].astype(F32), axis=0, keepdims=True)

    @pl.when(step == pl.num_programs(0) - 1)
    def _():
        scale_c, gate_c = modvec(4), modvec(5)
        sums = [0.0, 0.0, 0.0]
        for b in range(blocks):
            part = pl.ds(b * BLOCK, BLOCK)
            up = cot[part, :]
            branch = branch_acc[part, :] + as_row(downb_ref[...])
            sums[2] = sums[2] + gather_frames(branch * up, frames)
            mid_b = mid[part, :]
            n, r = normalize(mid_b)
            g = gnorm_acc[part, :]
            sums[0] = sums[0] + gather_frames(g, frames)
            sums[1] = sums[1] + gather_frames(g * n, frames)
            gmid_ref[part, :] = up + normalize_back(n, r, g * (1.0 + scale_c))
            stage_positions(stage, mid_b + gate_c * branch, frames, pos, b * per_block)
        to_frames(stage, result_ref)
        for member in range(3):
            per_clip_sums(gclip_ref, member, sums[member], clip_col)
        for i, (source, target) in enumerate(leaving):
            pltpu.make_async_copy(source, target, sem_out.at[i]).wait()


def owner_forward(mid, cot, table, clip_col, ids_row, wqkv, bqv, wout, bout, up, upb, down, downb):
    frames, pos, width = mid.shape
    rows = frames * pos
    clips = table.shape[1]
    ff = up.shape[1]
    chunk = width
    steps = ff // chunk
    whole = lambda *shape: pl.BlockSpec(shape, lambda i: (0,) * len(shape))
    like = lambda cols, dtype: jax.ShapeDtypeStruct((rows, cols), dtype)
    wide = pltpu.VMEM((rows, width), F32)
    half = pltpu.VMEM((rows, width), BF)
    return pl.pallas_call(
        owner_forward_kernel,
        grid=(steps,),
        in_specs=[vmem(), hbm(), vmem(), vmem(), vmem(), hbm(), vmem(), hbm(), vmem()]
        + [
            pl.BlockSpec((width, chunk), lambda i: (0, i)),
            vmem(),
            pl.BlockSpec((chunk, width), lambda i: (i, 0)),
            vmem(),
        ],
        out_specs=[hbm()] * 4
        + [
            whole(rows, width),
            whole(frames, pos, width),
            pl.BlockSpec((2, width, chunk), lambda i: (0, i, 0)),
            whole(3, clips, width),
            pl.BlockSpec((1, 1, chunk), lambda i: (i, 0, 0)),
            whole(1, width),
        ],
        out_shape=[
            like(width, BF),
            like(3 * width, BF),
            like(width, BF),
            like(width, F32),
            like(width, F32),
            jax.ShapeDtypeStruct((frames, pos, width), BF),
            jax.ShapeDtypeStruct((2, ff, width), BF),
            jax.ShapeDtypeStruct((3, clips, width), F32),
            jax.ShapeDtypeStruct((steps, 1, chunk), F32),
            jax.ShapeDtypeStruct((1, width), F32),
        ],
        scratch_shapes=[
            pltpu.VMEM((width // LANES, rows, LANES), F32),
            wide,
            wide,
            half,
            pltpu.VMEM((width, rows), BF),
            half,
            pltpu.VMEM((BLOCK, BLOCK), F32),
            pltpu.VMEM((rows, chunk), BF),
            pltpu.VMEM((rows, chunk), BF),
            wide,
            wide,
            pltpu.VMEM((frames, pos, width), BF),
            pltpu.VMEM((width, 3 * width), BF),
            pltpu.VMEM((width, width), BF),
            half,
            pltpu.VMEM((rows, 3 * width), BF),
            half,
            wide,
            dma(3),
            dma(4),
        ],
        compiler_params=params(),
        cost_estimate=BRIEF,
        name="owner_forward",
    )(mid, cot, table, clip_col, ids_row, wqkv, bqv, wout, bout, up, upb, down, downb)


def put(grads, core, quarter, value):
    rows = pl.ds((quarter % 2) * value.shape[0], value.shape[0])
    value = value.astype(BF)
    for target, owner in zip(grads, (quarter // 2, 1 - quarter // 2)):

        @pl.when(core == owner)
        def _(target=target):
            target[rows, :] = value


def this_core():
    return lax.rem(lax.axis_index("seq"), 2)


def qkv_back(normed, grad_packed, wqkv_ref, grads, gqv_ref, gnorm, width):
    for c in range(3):
        cols = pl.ds(c * width, width)
        gp = grad_packed[:, cols]
        put(grads, this_core(), c, dot_tn(normed[...], gp))
        if c != 1:
            gqv_ref[c // 2 : c // 2 + 1, :] = jnp.sum(gp.astype(F32), axis=0, keepdims=True)
        back = dot_nt(gp, wqkv_ref[:, cols])
        gnorm[...] = back if c == 0 else gnorm[...] + back


def owner_backward_kernel(
    ready, flush,
    xa_ref, packed_ref, attended_ref, branch_ref, gmid_ref, table_ref, clip_col_ref, ids_row_ref,
    wqkv_ref, wout_ref,
    send_ref, kept_ref, other_ref, gclip_ref, goutb_ref, gqv_ref,
    stage, normed, gbranch, gatt, gpacked, bias, gnorm,
):
    frames, pos, width = send_ref.shape
    rows = frames * pos
    blocks = rows // BLOCK
    per_block = BLOCK // frames
    clips = table_ref.shape[1]
    clip_col = clip_col_ref[...]

    def modvec(member):
        return spread(frame_rows(table_ref, member, clip_col), per_block)

    shift, scale, gate = modvec(0), modvec(1), modvec(2)
    bias[...] = time_mask(ids_row_ref, clip_col, per_block, clips)
    gate_sum = 0.0
    ready(gmid_ref, branch_ref, wout_ref, xa_ref)
    for b in range(blocks):
        part = pl.ds(b * BLOCK, BLOCK)
        gm = gmid_ref[part, :]
        gate_sum = gate_sum + gather_frames(branch_ref[part, :] * gm, frames)
        gb = (gate * gm).astype(BF)
        gbranch[part, :] = gb
        gatt[part, :] = dot_nt(gb, wout_ref[...]).astype(BF)
        n, _ = normalize(xa_ref[part, :].astype(F32))
        normed[part, :] = (n * (1.0 + scale) + shift).astype(BF)
    per_clip_sums(gclip_ref, 2, gate_sum, clip_col)
    goutb_ref[...] = jnp.sum(gbranch[...].astype(F32), axis=0, keepdims=True)
    grads = (kept_ref, other_ref)
    ready(attended_ref)
    put(grads, this_core(), 3, dot_tn(attended_ref[...], gbranch[...]))
    ready(packed_ref)
    attend_back(packed_ref, gatt, gpacked, lambda b: bias[...], blocks, width)
    ready(wqkv_ref)
    qkv_back(normed, gpacked, wqkv_ref, grads, gqv_ref, gnorm, width)
    flush(other_ref, kept_ref)
    sums = [0.0, 0.0]
    for b in range(blocks):
        part = pl.ds(b * BLOCK, BLOCK)
        n, r = normalize(xa_ref[part, :].astype(F32))
        g = gnorm[part, :]
        sums[0] = sums[0] + gather_frames(g, frames)
        sums[1] = sums[1] + gather_frames(g * n, frames)
        total = gmid_ref[part, :] + normalize_back(n, r, g * (1.0 + scale))
        stage_positions(stage, total, frames, pos, b * per_block)
    to_frames(stage, send_ref)
    for member in range(2):
        per_clip_sums(gclip_ref, member, sums[member], clip_col)


def owner_backward(xa, packed, attended, branch, gmid, table, clip_col, ids_row, wqkv, wout):
    frames = clip_col.shape[0]
    rows, width = xa.shape
    clips = table.shape[1]
    half = pltpu.VMEM((rows, width), BF)
    return streamed(
        owner_backward_kernel,
        (xa, packed, attended, branch, gmid, table, clip_col, ids_row, wqkv, wout),
        (4, 3, 9, 0, 2, 1, 8),
        [
            jax.ShapeDtypeStruct((frames, rows // frames, width), BF),
            jax.ShapeDtypeStruct((2 * width, width), BF),
            jax.ShapeDtypeStruct((2 * width, width), BF),
            jax.ShapeDtypeStruct((3, clips, width), F32),
            jax.ShapeDtypeStruct((1, width), F32),
            jax.ShapeDtypeStruct((2, width), F32),
        ],
        (1, 2),
        [
            pltpu.VMEM((width // LANES, rows, LANES), F32),
            half,
            half,
            half,
            pltpu.VMEM((rows, 3 * width), BF),
            pltpu.VMEM((BLOCK, BLOCK), F32),
            pltpu.VMEM((rows, width), F32),
        ],
        BRIEF,
        "owner_backward",
    )


def space_backward_kernel(
    ready, flush,
    clip_ref, box_ref, x_ref, packed_ref, attended_ref, branch_ref, gmid_ref, table_ref,
    wqkv_ref, wout_ref, t_ref, gclip_b_ref, gclip_c_ref, gqv_b_ref, goutb_b_ref, gupb_ref, gdownb_ref,
    gx_ref, kept_ref, other_ref, small_out,
    normed, gbranch, gatt, gpacked, gnorm, goutb_ref, gqv_ref, small_ref, bias,
):
    frames = box_ref.shape[0]
    width = x_ref.shape[1]
    clips = table_ref.shape[1]
    clip = own_clips(clip_ref, frames)
    sums = [[None] * frames for _ in range(3)]
    for f in range(frames):
        bias[f] = jnp.broadcast_to(visible_bias(box_ref, f, BLOCK), (BLOCK, BLOCK)).T
    ready(gmid_ref, branch_ref, wout_ref, x_ref)
    for f in range(frames):
        part = pl.ds(f * BLOCK, BLOCK)
        gm = gmid_ref[:, f].reshape(BLOCK, width).astype(F32)
        sums[2][f] = jnp.sum(branch_ref[part, :] * gm, axis=0, keepdims=True)
        gb = (frame_row(table_ref, 2, clip[f]) * gm).astype(BF)
        gbranch[part, :] = gb
        gatt[part, :] = dot_nt(gb, wout_ref[...]).astype(BF)
        n, _ = normalize(x_ref[part, :].astype(F32))
        shift = frame_row(table_ref, 0, clip[f])
        scale = frame_row(table_ref, 1, clip[f])
        normed[part, :] = (n * (1.0 + scale) + shift).astype(BF)
    goutb_ref[...] = jnp.sum(gbranch[...].astype(F32), axis=0, keepdims=True)
    grads = (kept_ref, other_ref)
    ready(attended_ref)
    put(grads, this_core(), 3, dot_tn(attended_ref[...], gbranch[...]))
    ready(packed_ref)
    attend_back(packed_ref, gatt, gpacked, lambda b: bias[b], frames, width)
    ready(wqkv_ref)
    qkv_back(normed, gpacked, wqkv_ref, grads, gqv_ref, gnorm, width)
    flush(other_ref, kept_ref)
    for f in range(frames):
        part = pl.ds(f * BLOCK, BLOCK)
        n, r = normalize(x_ref[part, :].astype(F32))
        g = gnorm[part, :]
        sums[0][f] = jnp.sum(g, axis=0, keepdims=True)
        sums[1][f] = jnp.sum(g * n, axis=0, keepdims=True)
        scale = frame_row(table_ref, 1, clip[f])
        gm = gmid_ref[:, f].reshape(BLOCK, width).astype(F32)
        gx_ref[part, :] = (gm + normalize_back(n, r, g * (1.0 + scale))).astype(BF)
    small_ref[...] = jnp.zeros_like(small_ref)
    for member in range(9):
        for c in range(clips):
            if member < 3:
                total = jnp.zeros((1, width), F32)
                for f in range(frames):
                    total = total + jnp.where(clip[f] == c, sums[member][f], 0.0)
            else:
                source = gclip_b_ref if member < 6 else gclip_c_ref
                total = source[member % 3, c : c + 1, :]
            small_ref[member * clips + c : member * clips + c + 1, :] = total
    at = 9 * clips
    t = jnp.where(lax.axis_index("seq") == 0, t_ref[...].astype(F32), 0.0)
    small_ref[at : at + clips, :] = t
    at += clips
    for source in (gqv_ref, goutb_ref, gqv_b_ref, goutb_b_ref, gupb_ref, gdownb_ref):
        for i in range(source.shape[0]):
            small_ref[at : at + 1, :] = source[i] if len(source.shape) == 3 else source[i : i + 1, :]
            at += 1
    small_out[...] = small_ref[...].astype(BF)
    flush(gx_ref)


def space_backward(frame_clip, boxes, tokens, *rest):
    rows, width = tokens.shape
    t_embed = rest[7]
    members = rest[-1].shape[0] + sum(value.shape[0] for value in rest[10:-1])
    extra = 3 + 10 * t_embed.shape[0] + members
    half = pltpu.VMEM((rows, width), BF)
    extra = -(-extra // 16) * 16
    return streamed(
        space_backward_kernel,
        (frame_clip, boxes, tokens) + rest,
        (6, 5, 9, 2, 4, 3, 8),
        [
            jax.ShapeDtypeStruct((rows, width), BF),
            jax.ShapeDtypeStruct((2 * width, width), BF),
            jax.ShapeDtypeStruct((2 * width, width), BF),
            jax.ShapeDtypeStruct((extra, width), BF),
        ],
        (0, 1, 2),
        [
            half,
            half,
            half,
            pltpu.VMEM((rows, 3 * width), BF),
            pltpu.VMEM((rows, width), F32),
            pltpu.VMEM((1, width), F32),
            pltpu.VMEM((2, width), F32),
            pltpu.VMEM((extra, width), F32),
            pltpu.VMEM((boxes.shape[0], BLOCK, BLOCK), F32),
        ],
        LONG,
        "space_backward",
        small=2,
    )


def routes(owners):
    depth = owners // 4
    places = [
        (x, z, y, c) for x in range(2) for z in range(depth) for y in range(2) for c in range(2)
    ]
    number = lambda x, z, y, c: x * owners + (z * 2 + y) * 2 + c
    pairs = lambda move: [(number(*p), number(*move(*p))) for p in places]
    over_x = lambda x, z, y, c: (1 - x, z, y, c)
    over_y = lambda x, z, y, c: (x, z, 1 - y, c)
    return {
        "core": pairs(lambda x, z, y, c: (x, z, y, 1 - c)),
        "first": pairs(lambda *p: (over_y if p[3] else over_x)(*p)),
        "second": pairs(lambda *p: (over_x if p[3] else over_y)(*p)),
        "x": pairs(over_x),
        "y": pairs(over_y),
        "depth": [
            pairs(lambda x, z, y, c, s=s: (x, (z + s) % depth, y, c)) for s in range(1, depth)
        ],
        "swap": [
            pairs(lambda x, z, y, c, s=s: (x, z ^ s, y, c))
            for s in (1 << i for i in range(depth.bit_length() - 1))
        ],
    }


def place():
    x, s = lax.axis_index("dp"), lax.axis_index("seq")
    return x, s >> 2, (s >> 1) & 1, s & 1


def move(value, pairs):
    return lax.ppermute(value, BOTH, pairs)


def tie(*values):
    return lax.optimization_barrier(values)


def side(stage, core):
    x, _, y, _ = place()
    return jnp.where(core == stage, x, y)


def cross_kernel(stage, kept_ref, got_ref, send_ref, out_ref, a, b, total, sem_a, sem_b, sem_out):
    count, rows, _ = total.shape
    each = count // 2
    bit = side(stage, place()[3])
    spots = [(half, pl.ds(i * rows, rows)) for half in (1 - bit, bit) for i in range(each)]
    from_a = copies([(kept_ref.at[h, r], a.at[i]) for i, (h, r) in enumerate(spots)], sem_a)
    from_b = copies([(got_ref.at[h, r], b.at[i]) for i, (h, r) in enumerate(spots)], sem_b)
    out = []
    for i, (_, r) in enumerate(spots):
        from_a[i].wait()
        from_b[i].wait()
        total[i] = (a[i].astype(F32) + b[i].astype(F32)).astype(BF)
        target = (send_ref if i < each else out_ref).at[r]
        out += copies([(total.at[i], target)], sem_out.at[pl.ds(i, 1)])
    for copy in out:
        copy.wait()


def cross_sum(cost, stage, kept, got):
    height, width = kept.shape[0] // 2, kept.shape[1]
    each = max(1, height // 384)
    buffer = pltpu.VMEM((2 * each, height // each, width), BF)
    half = jax.ShapeDtypeStruct((height, width), BF)
    return pl.pallas_call(
        functools.partial(cross_kernel, stage),
        in_specs=[hbm(), hbm()],
        out_specs=[hbm(), hbm()],
        out_shape=[half, half],
        scratch_shapes=[buffer] * 3 + [dma(2 * each)] * 3,
        compiler_params=alone(),
        cost_estimate=cost,
        name="cross_sum",
    )(kept.reshape(2, height, width), got.reshape(2, height, width))


def along_kernel(kept_ref, got_ref, *refs):
    depth = kept_ref.shape[0]
    targets = refs[:depth]
    a, b, total, sem_a, sem_b, sem_out = refs[depth:]
    z = place()[1]
    turns = list(range(1, depth)) + [0]
    parts = [lax.rem(z + s, depth) for s in turns]
    from_a = copies([(kept_ref.at[p], a.at[i]) for i, p in enumerate(parts)], sem_a)
    from_b = copies([(got_ref.at[p], b.at[i]) for i, p in enumerate(parts)], sem_b)
    out = []
    for i, s in enumerate(turns):
        from_a[i].wait()
        from_b[i].wait()
        total[i] = (a[i].astype(F32) + b[i].astype(F32)).astype(BF)
        out += copies([(total.at[i], targets[s])], sem_out.at[pl.ds(i, 1)])
    for copy in out:
        copy.wait()


def along_sum(cost, depth, kept, got):
    height, width = kept.shape[0] // depth, kept.shape[1]
    buffer = pltpu.VMEM((depth, height, width), BF)
    return pl.pallas_call(
        along_kernel,
        in_specs=[hbm()] * 2,
        out_specs=[hbm()] * depth,
        out_shape=[jax.ShapeDtypeStruct((height, width), BF)] * depth,
        scratch_shapes=[buffer] * 3 + [dma(depth)] * 3,
        compiler_params=alone(),
        cost_estimate=cost,
        name="along_sum",
    )(kept.reshape(depth, height, width), got.reshape(depth, height, width))


def finish_kernel(*refs):
    total = refs[0][...].astype(F32)
    for ref in refs[1:-1]:
        total = total + ref[...].astype(F32)
    refs[-1][...] = total.astype(refs[-1].dtype)


def finish_sum(cost, *parts):
    return pl.pallas_call(
        finish_kernel,
        in_specs=[vmem()] * len(parts),
        out_specs=vmem(),
        out_shape=jax.ShapeDtypeStruct(parts[0].shape, parts[0].dtype),
        compiler_params=alone(),
        cost_estimate=cost,
        name="finish_sum",
    )(*parts)


def collect_kernel(*refs):
    *parts, target, held, sem_in, sem_out = refs
    depth = target.shape[0]
    z = place()[1]
    for copy in copies(
        [(ref, held.at[lax.rem(z + depth - s, depth)]) for s, ref in enumerate(parts)], sem_in
    ):
        copy.wait()
    copies([(held, target)], sem_out)[0].wait()


def collect(cost, *parts):
    depth = len(parts)
    height, width = parts[0].shape
    return pl.pallas_call(
        collect_kernel,
        in_specs=[hbm()] * depth,
        out_specs=hbm(),
        out_shape=jax.ShapeDtypeStruct((depth, height, width), BF),
        scratch_shapes=[pltpu.VMEM((depth, height, width), BF), dma(depth), dma(1)],
        compiler_params=alone(),
        cost_estimate=cost,
        name="collect",
    )(*parts).reshape(depth * height, width)


class Sum:
    def __init__(self, kept, other, route):
        self.route = route
        self.kept = kept
        self.wait = move(other, route["core"])

    def cross(self, stage):
        send, self.kept = cross_sum(self.cost, stage, self.kept, self.wait)
        self.wait = move(send, self.route[("first", "second")[stage]])
        return "kept"

    def along(self):
        self.kept, *send = along_sum(self.cost, len(self.route["depth"]) + 1, self.kept, self.wait)
        self.wait = tuple(move(part, pairs) for part, pairs in zip(send, self.route["depth"]))
        return "kept"

    def finish(self):
        self.kept = finish_sum(self.cost, self.kept, *self.wait)
        self.wait = tuple(move(self.kept, pairs) for pairs in self.route["depth"])
        return "kept"

    def gather(self):
        self.near = collect(self.cost, self.kept, *self.wait)
        self.wait, self.across, self.core = (
            move(self.near, self.route[link]) for link in ("second", "first", "core")
        )
        return "near"

    def relay(self):
        self.far = self.wait
        got, self.core_far = (move(self.far, self.route[link]) for link in ("first", "core"))
        self.wait = (self.across, got)
        return "far"

    def reflect(self):
        self.across, self.across_far = self.wait
        self.wait = (self.core, self.core_far) + tuple(
            move(value, self.route["core"]) for value in self.wait
        )
        return "across"


class Order:
    def __init__(self):
        self.before = None
        self.cost = BRIEF

    def after(self, value):
        if self.before is not None:
            owner, name = self.before
            flat = value if isinstance(value, tuple) else (value,)
            *flat, late = tie(*flat, getattr(owner, name))
            setattr(owner, name, late)
            value = tuple(flat) if isinstance(value, tuple) else flat[0]
        return value

    def run(self, total, step, *args):
        total.cost = self.cost
        total.wait = self.after(total.wait)
        self.before = (total, getattr(total, step)(*args))


class Held:
    def __init__(self, value):
        self.value = value


def widen_kernel(other, spots, *refs):
    sources, (first_ref, second_ref), (held, wide, sem_in, sem_out) = refs[:4], refs[-6:-4], refs[-4:]
    height, width = held.shape[1:]
    loads = copies([(ref, held.at[i]) for i, ref in enumerate(sources)], sem_in)
    core = place()[3] ^ other
    stores = []
    for i, load in enumerate(loads):
        near, far = side(0, core) ^ (i >> 1), side(1, core) ^ (i & 1)
        block = core * 4 + near * 2 + far
        load.wait()
        wide[i] = held[i].astype(F32)
        in_first, (row, column), (row_2, column_2) = spots(block)
        place_1 = first_ref.at[
            pl.ds(pl.multiple_of(row * height, height), height),
            pl.ds(pl.multiple_of(column * width, width), width),
        ]
        place_2 = second_ref.at[
            pl.ds(pl.multiple_of(row_2 * height, height), height),
            pl.ds(pl.multiple_of(column_2 * width, width), width),
        ]
        store_1 = pltpu.make_async_copy(wide.at[i], place_1, sem_out.at[i])
        store_2 = pltpu.make_async_copy(wide.at[i], place_2, sem_out.at[i])
        pl.when(in_first)(store_1.start)
        pl.when(jnp.logical_not(in_first))(store_2.start)
        stores.append((in_first, store_1, store_2))
    for in_first, store_1, store_2 in stores:
        pl.when(in_first)(store_1.wait)
        pl.when(jnp.logical_not(in_first))(store_2.wait)


def widen(cost, other, parts, spots, shapes, before=()):
    height, width = parts[0].shape
    return pl.pallas_call(
        functools.partial(widen_kernel, other, spots),
        in_specs=[hbm()] * (4 + len(before)),
        out_specs=[hbm()] * 2,
        out_shape=[jax.ShapeDtypeStruct(shape, F32) for shape in shapes],
        input_output_aliases={4 + i: i for i in range(len(before))},
        scratch_shapes=[
            pltpu.VMEM((4, height, width), BF),
            pltpu.VMEM((4, height, width), F32),
            dma(4),
            dma(4),
        ],
        compiler_params=alone(),
        cost_estimate=cost,
        name="widen",
    )(*parts, *before)


def spots_of(split, first, second):
    def spots(block):
        return (
            block < split,
            first(jnp.minimum(block, split - 1)),
            second(jnp.maximum(block - split, 0)),
        )

    return spots


def widen_plain_kernel(split, maps, in_ref, first_ref, second_ref, held, wide, sem_in, sem_out):
    count, height, width = held.shape
    loads = copies(
        [(in_ref.at[pl.ds(i * height, height)], held.at[i]) for i in range(count)], sem_in
    )
    stores = []
    for i, load in enumerate(loads):
        load.wait()
        wide[i] = held[i].astype(F32)
        row, column = maps[0](i) if i < split else maps[1](i - split)
        target = (first_ref if i < split else second_ref).at[
            pl.ds(row * height, height), pl.ds(column * width, width)
        ]
        stores += copies([(wide.at[i], target)], sem_out.at[pl.ds(i, 1)])
    for store in stores:
        store.wait()


def widen_plain(summed, split, shapes, maps):
    width = summed.shape[1]
    height = summed.shape[0] // 8
    return pl.pallas_call(
        functools.partial(widen_plain_kernel, split, maps),
        in_specs=[hbm()],
        out_specs=[hbm()] * 2,
        out_shape=[jax.ShapeDtypeStruct(shape, F32) for shape in shapes],
        scratch_shapes=[
            pltpu.VMEM((8, height, width), BF),
            pltpu.VMEM((8, height, width), F32),
            dma(8),
            dma(8),
        ],
        compiler_params=alone(),
        cost_estimate=BRIEF,
        name="widen_plain",
    )(summed)


def pack_kernel(*refs):
    parts, target, held, sem_in, sem_out = refs[:2], refs[2], refs[3], refs[4], refs[5]
    first = parts[0].shape[0]
    places = [held.at[pl.ds(0, first)], held.at[pl.ds(first, parts[1].shape[0])]]
    for copy in copies(list(zip(parts, places)), sem_in):
        copy.wait()
    copies([(held, target)], sem_out)[0].wait()


def pack(*parts):
    shape = (parts[0].shape[0] + parts[1].shape[0], parts[0].shape[1])
    return pl.pallas_call(
        pack_kernel,
        in_specs=[hbm()] * 2,
        out_specs=hbm(),
        out_shape=jax.ShapeDtypeStruct(shape, BF),
        scratch_shapes=[pltpu.VMEM(shape, BF), dma(2), dma(1)],
        compiler_params=alone(),
        cost_estimate=BRIEF,
        name="pack",
    )(*parts)


def last_kernel(rows, groups, clips, sizes, src_ref, up_ref, down_ref, mod_ref, *refs):
    vectors, (parts, held, wide, smooth, split, mods, sem_in, sem_out, sem_mod) = refs[:-9], refs[-9:]
    count, height, width = held.shape
    owners = height // rows
    extra = parts.shape[1]
    copies([(src_ref.at[:, pl.ds(rows, extra)], parts)], sem_in.at[pl.ds(count * owners, 1)])[0].wait()
    loads = copies(
        [
            (src_ref.at[i * owners + k, pl.ds(0, rows)], held.at[i, pl.ds(k * rows, rows)])
            for i in range(count)
            for k in range(owners)
        ],
        sem_in,
    )
    each = parts.shape[0] // groups
    small = [
        jnp.sum(parts[pl.ds(i * each, each)].astype(F32), axis=0) for i in range(groups)
    ]
    members = 9
    smooth[...] = jnp.zeros_like(smooth)
    split[...] = jnp.zeros_like(split)
    for j, sums in enumerate(small):
        t = sums[members * clips : (members + 1) * clips]
        value = (t / (1.0 + jnp.exp(-t))).astype(BF).astype(F32)
        for i in range(3):
            smooth[pl.ds((i * groups + j) * clips, clips), :] = value
    left = smooth[...].astype(BF)
    slots = mods.shape[0]
    stores = []
    for member in range(members):
        row = 0.0
        for j, sums in enumerate(small):
            rest = sums[member * clips : (member + 1) * clips]
            row = row + jnp.sum(rest, axis=0)
            for i in range(3):
                piece = rest.astype(BF).astype(F32)
                split[pl.ds((i * groups + j) * clips, clips), :] = piece
                rest = rest - piece
        vectors[0][pl.ds(member * width, width)] = row
        if member >= slots:
            stores[member - slots].wait()
        mods[member % slots] = dot_tn(left, split[...].astype(BF))
        target = mod_ref.at[:, pl.ds(member * width, width)]
        stores += copies([(mods.at[member % slots], target)], sem_mod.at[pl.ds(member, 1)])
    at = (members + 1) * clips
    for vector, size in zip(vectors[1:], sizes):
        for i in range(size):
            vector[pl.ds(i * width, width)] = sum(sums[at] for sums in small)
            at += 1
    later = []
    for i in range(count):
        for load in loads[i * owners : (i + 1) * owners]:
            load.wait()
        wide[i] = held[i].astype(F32)
        if i < count // 2:
            target = up_ref.at[:, pl.ds(i * width, width)]
        else:
            target = down_ref.at[pl.ds((i - count // 2) * height, height)]
        later += copies([(wide.at[i], target)], sem_out.at[pl.ds(i, 1)])
    for store in stores[-slots:] + later:
        store.wait()


def last_grads(gathered, rows, groups, clips, ff, sizes):
    devices, extra, width = gathered.shape
    extra -= rows
    blocks = 2 * ff // width
    deep = -(-3 * groups * clips // 16) * 16
    vector = lambda size: jax.ShapeDtypeStruct((size * width,), F32)
    return pl.pallas_call(
        functools.partial(last_kernel, rows, groups, clips, sizes),
        in_specs=[hbm()],
        out_specs=[hbm()] * 3 + [vmem()] * (1 + len(sizes)),
        out_shape=[
            jax.ShapeDtypeStruct((width, ff), F32),
            jax.ShapeDtypeStruct((ff, width), F32),
            jax.ShapeDtypeStruct((width, 9 * width), F32),
            vector(9),
        ]
        + [vector(size) for size in sizes],
        scratch_shapes=[
            pltpu.VMEM((devices, extra, width), BF),
            pltpu.VMEM((blocks, width, width), BF),
            pltpu.VMEM((blocks, width, width), F32),
            pltpu.VMEM((deep, width), F32),
            pltpu.VMEM((deep, width), F32),
            pltpu.VMEM((5, width, width), F32),
            dma(devices + 1),
            dma(blocks),
            dma(9),
        ],
        compiler_params=alone(),
        cost_estimate=BRIEF,
        name="last_grads",
    )(gathered)


def per_device(
    tokens, t_embed, frame_clip, boxes, mod_weight, mod_bias, space_qkv, space_qv_bias, space_out,
    space_out_bias, time_qkv, time_qv_bias, time_out, time_out_bias, up_weight, up_bias,
    down_weight, down_bias, cotangent,
):
    owners = lax.axis_size("seq")
    groups = lax.axis_size("dp")
    frames = boxes.shape[0]
    width = tokens.shape[1]
    patches = tokens.shape[0] // frames
    group_frames = frame_clip.shape[0]
    pos = patches // owners
    clips = t_embed.shape[0]
    ff = up_weight.shape[1]
    depth = owners // 4
    own_route = depth <= 4
    route = routes(owners)

    clip_col = frame_clip[:, None]
    per_block = BLOCK // group_frames
    ids_row = (
        jnp.arange(per_block, dtype=jnp.int32)[:, None] * clips + frame_clip[None, :]
    ).reshape(1, BLOCK)

    def exchange(x):
        return lax.all_to_all(x, "seq", split_axis=0, concat_axis=0, tiled=True)

    qkv_maps = (lambda i: (i % 2, i // 2), lambda i: (i, 0))

    cot_send = cotangent.reshape(frames, owners, pos, width).transpose(1, 0, 2, 3)
    cot = exchange(cot_send)
    mid_send, packed_a, attended_a, branch_a, table_a = space_forward(
        frame_clip, boxes, t_embed, mod_weight, mod_bias, tokens, space_qkv, space_qv_bias, space_out,
        space_out_bias, owners,
    )
    mid_send, cot, t_late = tie(mid_send, cot, t_embed)
    mid = exchange(mid_send).reshape(group_frames, pos, width)
    cot = cot.reshape(group_frames, pos, width)
    table = modulation(t_late, mod_weight, mod_bias, 3, 6)
    (
        xa, packed_b, attended_b, branch_b, gmid_b, result_send, grad_f, gclip_c, gup_b, gdown_b,
    ) = owner_forward(
        mid, cot, table, clip_col, ids_row, time_qkv, time_qv_bias, time_out, time_out_bias, up_weight,
        up_bias, down_weight, down_bias,
    )
    ff_shapes = ((width, ff), (ff, width))
    qkv_shapes = ((width, 3 * width), (width, width))
    qkv_spots = spots_of(6, lambda i: (i % 2, i // 2), lambda i: (i, 0))

    def after_ff(gmid_b):
        return owner_backward(
            xa, packed_b, attended_b, branch_b, gmid_b, table, clip_col, ids_row, time_qkv, time_out
        )

    def after_time(gmid_a, gclip_b, gtout_b, gtqv_b):
        return space_backward(
            frame_clip, boxes, tokens, packed_a, attended_a, branch_a, gmid_a, table_a, space_qkv,
            space_out, t_embed, gclip_b, gclip_c, gtqv_b, gtout_b, gup_b, gdown_b,
        )

    result_send = result_send.reshape(owners, frames, pos, width)
    grad_f = grad_f.reshape(-1, width)
    part_f = Held(lax.psum_scatter(grad_f, BOTH, scatter_dimension=0, tiled=True))
    if own_route:
        sums = {}
        order = Order()
        wide = {}
        for name, *step in SCHEDULE:
            if name == "time":
                gmid_b = order.after(gmid_b)
                gmid_send, kept_t, other_t, gclip_b, gtout_b, gtqv_b = after_ff(gmid_b)
                gmid_a = exchange(gmid_send.reshape(owners, frames, pos, width))
                sums["t"] = Sum(kept_t, other_t, route)
                order.before = None
            elif name == "space":
                gmid_a = order.after(gmid_a)
                gmid_a, result_send = tie(gmid_a, result_send)
                result = exchange(result_send)
                grad_tokens, kept_s, other_s, small = after_time(
                    gmid_a, gclip_b, gtout_b, gtqv_b
                )
                sums["s"] = Sum(kept_s, other_s, route)
                kept_s, result = tie(sums["s"].kept, result)
                sums["s"].kept = kept_s
                order.before = None
            elif name == "ff":
                part_f.value = pack(order.after(part_f.value), small)
                order.before = (part_f, "value")
            elif step[0] == "widen":
                total = sums[name]
                if step[1]:
                    total.wait = order.after(total.wait)
                    parts = total.wait
                else:
                    total.across = order.after(total.across)
                    parts = (total.near, total.far, total.across, total.across_far)
                before = (wide[name].value, wide[name].other) if name in wide else ()
                pair = widen(order.cost, step[1], parts, qkv_spots, qkv_shapes, before)
                done = wide[name] = Held(pair[0])
                done.other = pair[1]
                order.before = (done, "value")
            else:
                order.cost = COSTS.get((name, *step), BRIEF)
                order.run(sums[name], *step)
        gathered = lax.all_gather(part_f.value, BOTH, axis=0)
        wide_time, wide_space = ((wide[k].value, wide[k].other) for k in ("t", "s"))
    else:
        result = exchange(result_send)
        gmid_send, kept_t, other_t, gclip_b, gtout_b, gtqv_b = after_ff(gmid_b)
        gmid_a = exchange(gmid_send.reshape(owners, frames, pos, width))
        grad_tokens, kept_s, other_s, small = after_time(gmid_a, gclip_b, gtout_b, gtqv_b)
        small = lax.psum(small.astype(F32), "seq").astype(BF)
        small = lax.all_gather(small, "dp", axis=0)
        blocks = 2 * ff // width
        sum_f = lax.all_gather(part_f.value, BOTH, axis=0, tiled=True).reshape(blocks, -1, width)
        gathered = jnp.zeros((blocks,) + small.shape[1:], BF)
        gathered = gathered.at[jnp.arange(groups) * (blocks // groups)].set(small)
        gathered = jnp.concatenate([sum_f, gathered], axis=1)
        core = place()[3]

        def whole(kept, other):
            halves = [jnp.where(core == half, kept, other) for half in range(2)]
            return lax.psum(jnp.concatenate(halves, axis=0), BOTH)

        qkv_maps = (lambda i: (i % 2, i // 2), lambda i: (i, 0))
        wide_time = widen_plain(whole(kept_t, other_t), 6, qkv_shapes, qkv_maps)
        wide_space = widen_plain(whole(kept_s, other_s), 6, qkv_shapes, qkv_maps)
    rows = 2 * ff // gathered.shape[0]
    sizes = (2, 1, 2, 1, ff // width, 1)
    grad_up, grad_down, grad_mod, grad_mod_b, *biases = last_grads(
        gathered, rows, groups, clips, ff, sizes
    )
    return (
        result.transpose(1, 0, 2, 3).reshape(tokens.shape),
        grad_tokens,
        grad_mod,
        grad_mod_b,
        wide_space[0],
        biases[0],
        wide_space[1],
        biases[1],
        wide_time[0],
        biases[2],
        wide_time[1],
        biases[3],
        grad_up,
        biases[4],
        grad_down,
        biases[5],
    )


def solution(mesh):
    split = P(BOTH, None)
    placed = (split, P("dp", None), P("dp"), split) + (P(),) * 14 + (split,)
    return jax.shard_map(
        per_device,
        mesh=mesh,
        in_specs=placed,
        out_specs=(split, split) + (P(),) * 14,
        check_vma=False,
    )
```

```python
import functools

import jax
import jax.numpy as jnp
from jax import lax
from jax.experimental import pallas as pl
from jax.experimental.pallas import tpu as pltpu
from jax.sharding import PartitionSpec as P

HD = 64
GRID_W = 16
EPS = 1e-06
NEG = -1e30
BLOCK = 256
LANES = 128
BF = jnp.bfloat16
F32 = jnp.float32
VMEM_BYTES = 56 * 1024 * 1024
BOTH = ("dp", "seq")
BRIEF = pl.CostEstimate(flops=1000, bytes_accessed=1000, transcendentals=0)
SHORT = pl.CostEstimate(flops=4 * 10**9, bytes_accessed=1000, transcendentals=0)
MIDDLE = pl.CostEstimate(flops=10**10, bytes_accessed=1000, transcendentals=0)
LONG = pl.CostEstimate(flops=3 * 10**10, bytes_accessed=1000, transcendentals=0)

COSTS = {
    ("t", "cross", 1): LONG,
    ("t", "along"): MIDDLE,
    ("t", "finish"): MIDDLE,
    ("s", "along"): MIDDLE,
    ("t", "gather"): MIDDLE,
    ("s", "finish"): MIDDLE,
    ("s", "gather"): MIDDLE,
}
SCHEDULE = (
    ("time",),
    ("t", "cross", 0),
    ("space",),
    ("t", "cross", 1),
    ("s", "cross", 0),
    ("t", "along"),
    ("s", "cross", 1),
    ("t", "finish"),
    ("small", 0),
    ("s", "along"),
    ("t", "gather"),
    ("small", 1),
    ("s", "finish"),
    ("ff",),
    ("small", 2),
    ("t", "relay"),
    ("s", "gather"),
    ("t", "reflect"),
    ("t", "widen", 0),
    ("s", "relay"),
    ("mod",),
    ("t", "widen", 1),
    ("s", "reflect"),
    ("s", "widen", 0),
    ("s", "widen", 1),
)


def params():
    return pltpu.CompilerParams(vmem_limit_bytes=VMEM_BYTES)


def alone():
    return pltpu.CompilerParams(vmem_limit_bytes=60 * 1024 * 1024)


def dot_nn(a, b):
    return lax.dot_general(a, b, (((1,), (0,)), ((), ())), preferred_element_type=F32)


def dot_nt(a, b):
    return lax.dot_general(a, b, (((1,), (1,)), ((), ())), preferred_element_type=F32)


def dot_tn(a, b):
    return lax.dot_general(a, b, (((0,), (0,)), ((), ())), preferred_element_type=F32)


def normalize(x):
    center = x - jnp.mean(x, axis=-1, keepdims=True)
    r = lax.rsqrt(jnp.mean(center * center, axis=-1, keepdims=True) + EPS)
    return center * r, r


def normalize_back(n, r, m):
    return r * (
        m - jnp.mean(m, axis=-1, keepdims=True) - n * jnp.mean(m * n, axis=-1, keepdims=True)
    )


def head_halves(width):
    lane = lax.broadcasted_iota(jnp.int32, (1, width), 1)
    low = (lane < HD).astype(F32).astype(BF)
    return low, (lane >= HD).astype(F32).astype(BF)


def attend(packed, attended, bias, blocks, width):
    halves = head_halves(2 * HD)

    def pair(index, carry):
        off = pl.multiple_of(index * 2 * HD, 2 * HD)
        for b in range(blocks):
            rows = pl.ds(b * BLOCK, BLOCK)
            q = packed[rows, pl.ds(off, 2 * HD)]
            k = packed[rows, pl.ds(width + off, 2 * HD)]
            v = packed[rows, pl.ds(2 * width + off, 2 * HD)]
            out = None
            for half in halves:
                s = dot_nt(q, k * half) * (HD**-0.5) + bias(b)
                e = jnp.exp(s - jnp.max(s, axis=-1, keepdims=True))
                p = (e * (1.0 / jnp.sum(e, axis=-1, keepdims=True))).astype(BF)
                o = dot_nn(p, v * half)
                out = o if out is None else out + o
            attended[rows, pl.ds(off, 2 * HD)] = out.astype(BF)
        return carry

    lax.fori_loop(0, width // (2 * HD), pair, 0)


def attend_back(packed, grad_in, grad_packed, bias, blocks, width):
    halves = head_halves(2 * HD)
    factor = HD**-0.5

    def pair(index, carry):
        off = pl.multiple_of(index * 2 * HD, 2 * HD)
        for b in range(blocks):
            rows = pl.ds(b * BLOCK, BLOCK)
            q = packed[rows, pl.ds(off, 2 * HD)]
            k = packed[rows, pl.ds(width + off, 2 * HD)]
            v = packed[rows, pl.ds(2 * width + off, 2 * HD)]
            g = grad_in[rows, pl.ds(off, 2 * HD)]
            dq = dk = dv = 0.0
            for half in halves:
                kh = k * half
                s = dot_nt(kh, q) * factor + bias(b)
                e = jnp.exp(s - jnp.max(s, axis=0, keepdims=True))
                p = e * (1.0 / jnp.sum(e, axis=0, keepdims=True))
                gs = dot_nt(v * half, g)
                ds = (p * (gs - jnp.sum(p * gs, axis=0, keepdims=True))).astype(BF)
                dv = dv + dot_nn(p.astype(BF), g * half)
                dq = dq + dot_tn(ds, kh)
                dk = dk + dot_nn(ds, q * half)
            grad_packed[rows, pl.ds(off, 2 * HD)] = (dq * factor).astype(BF)
            grad_packed[rows, pl.ds(width + off, 2 * HD)] = (dk * factor).astype(BF)
            grad_packed[rows, pl.ds(2 * width + off, 2 * HD)] = dv.astype(BF)
        return carry

    lax.fori_loop(0, width // (2 * HD), pair, 0)


def project_qkv(normed, weight, qv_bias, packed, width):
    for c in range(3):
        cols = pl.ds(c * width, width)
        value = dot_nn(normed[...], weight[:, cols])
        if c != 1:
            value = value + as_row(qv_bias[pl.ds((c // 2) * width, width)])
        packed[:, cols] = value.astype(BF)


def modulation_kernel(first, t_ref, w_ref, b_ref, out_ref):
    t = t_ref[...].astype(F32)
    smooth = (t / (1.0 + jnp.exp(-t))).astype(BF)
    bias = chunk_row(b_ref, first + pl.program_id(0), t.shape[1])
    out_ref[0] = dot_nn(smooth, w_ref[...]) + bias


def modulation(t_embed, weight, bias, first, count):
    clips, width = t_embed.shape
    return pl.pallas_call(
        functools.partial(modulation_kernel, first),
        grid=(count,),
        in_specs=[
            pl.BlockSpec((clips, width), lambda i: (0, 0)),
            pl.BlockSpec((width, width), lambda i: (0, first + i)),
            vmem(),
        ],
        out_specs=pl.BlockSpec((1, clips, width), lambda i: (i, 0, 0)),
        out_shape=jax.ShapeDtypeStruct((count, clips, width), F32),
        cost_estimate=BRIEF,
        name="modulation",
    )(t_embed, weight, bias)


def as_row(vector):
    return vector.astype(F32).reshape(1, -1)


def chunk_row(vector_ref, index, width):
    return as_row(vector_ref[pl.ds(pl.multiple_of(index * width, width), width)])


def own_clips(clip_ref, frames):
    first = lax.axis_index("seq") * frames
    return [clip_ref[first + f] for f in range(frames)]


def frame_row(table, member, clip):
    total = jnp.zeros(table.shape[2:], F32)[None]
    for c in range(table.shape[1]):
        total = jnp.where(clip == c, table[member, c : c + 1, :], total)
    return total


def frame_rows(table, member, clip_col):
    total = jnp.zeros((clip_col.shape[0], table.shape[2]), F32)
    for c in range(table.shape[1]):
        total = jnp.where(clip_col == c, table[member, c : c + 1, :], total)
    return total


def visible_bias(box_ref, frame, patches):
    cell = lax.broadcasted_iota(jnp.int32, (1, patches), 1)
    row, col = cell // GRID_W, cell % GRID_W
    inside = (
        (row >= box_ref[frame, 0])
        & (row < box_ref[frame, 1])
        & (col >= box_ref[frame, 2])
        & (col < box_ref[frame, 3])
    )
    return jnp.where(inside, NEG, 0.0)


def space_forward_kernel(
    ready, flush,
    clip_ref, box_ref, t_ref, modw_ref, modb_ref, x_ref, wqkv_ref, bqv_ref, wout_ref, bout_ref,
    send_ref, packed_ref, attended_ref, branch_ref, table_ref, normed,
):
    frames = box_ref.shape[0]
    width = x_ref.shape[1]
    dst, _, pos, _ = send_ref.shape
    clip = own_clips(clip_ref, frames)
    t = t_ref[...].astype(F32)
    smooth = (t / (1.0 + jnp.exp(-t))).astype(BF)
    ready(modw_ref)
    for k in range(3):
        cols = pl.ds(k * width, width)
        table_ref[k] = dot_nn(smooth, modw_ref[:, cols]) + as_row(modb_ref[cols])
    ready(x_ref)
    for f in range(frames):
        rows = pl.ds(f * BLOCK, BLOCK)
        n, _ = normalize(x_ref[rows, :].astype(F32))
        shift = frame_row(table_ref, 0, clip[f])
        scale = frame_row(table_ref, 1, clip[f])
        normed[rows, :] = (n * (1.0 + scale) + shift).astype(BF)
    ready(wqkv_ref)
    project_qkv(normed, wqkv_ref, bqv_ref, packed_ref, width)
    flush(packed_ref)
    biases = [visible_bias(box_ref, f, BLOCK) for f in range(frames)]
    attend(packed_ref, attended_ref, lambda b: biases[b], frames, width)
    flush(attended_ref)
    ready(wout_ref)
    for f in range(frames):
        rows = pl.ds(f * BLOCK, BLOCK)
        branch = dot_nn(attended_ref[rows, :], wout_ref[...]) + as_row(bout_ref[...])
        branch_ref[rows, :] = branch
        gate = frame_row(table_ref, 2, clip[f])
        mid = x_ref[rows, :].astype(F32) + gate * branch
        send_ref[:, f] = mid.astype(BF).reshape(dst, pos, width)
    flush(send_ref, branch_ref)


def vmem():
    return pl.BlockSpec(memory_space=pltpu.VMEM)


def smem():
    return pl.BlockSpec(memory_space=pltpu.SMEM)


def hbm():
    return pl.BlockSpec(memory_space=pltpu.HBM)


def dma(count):
    return pltpu.SemaphoreType.DMA((count,))


def copies(pairs, semaphores):
    started = [
        pltpu.make_async_copy(source, target, semaphores.at[i])
        for i, (source, target) in enumerate(pairs)
    ]
    for copy in started:
        copy.start()
    return started


def streamed(body, args, late, out_shape, late_out, scratch, cost, name, small=0, cut=()):
    cut = dict(cut)
    n, m = len(args), len(out_shape)

    def shape_of(i):
        shape = args[i].shape
        return shape[:-1] + (cut[i],) if i in cut else shape

    def kernel(*refs):
        refs = list(refs)
        ins, outs, rest = refs[:n], refs[n : n + m], refs[n + m :]
        own, rest = rest[: len(scratch)], rest[len(scratch) :]
        in_buffers, out_buffers, (sem_in, sem_out) = rest[: len(late)], rest[len(late) : -2], rest[-2:]
        sources = [ins[i].at[:, pl.ds(0, cut[i])] if i in cut else ins[i] for i in late]
        waiting = list(zip(in_buffers, copies(list(zip(sources, in_buffers)), sem_in)))
        for i, buffer in zip(late, in_buffers):
            ins[i] = buffer
        pending = dict(zip(late_out, out_buffers))
        targets = {i: outs[i] for i in late_out}
        for i in late_out:
            outs[i] = pending[i]
        leaving = []

        def ready(*buffers):
            for buffer in buffers:
                for entry in list(waiting):
                    if entry[0] is buffer:
                        entry[1].wait()
                        waiting.remove(entry)

        def flush(*buffers):
            for buffer in buffers:
                for k, i in enumerate(late_out):
                    if out_buffers[k] is buffer:
                        leaving.extend(copies([(buffer, targets[i])], sem_out.at[pl.ds(k, 1)]))

        body(ready, flush, *ins, *outs, *own)
        for copy in leaving:
            copy.wait()

    in_specs = [smem() if i < small else hbm() if i in late else vmem() for i in range(n)]
    return pl.pallas_call(
        kernel,
        in_specs=in_specs,
        out_specs=[hbm() if i in late_out else vmem() for i in range(m)],
        out_shape=out_shape,
        scratch_shapes=list(scratch)
        + [pltpu.VMEM(shape_of(i), args[i].dtype) for i in late]
        + [pltpu.VMEM(out_shape[i].shape, out_shape[i].dtype) for i in late_out]
        + [dma(max(1, len(late))), dma(max(1, len(late_out)))],
        compiler_params=params(),
        cost_estimate=cost,
        name=name,
    )(*args)


def space_forward(
    frame_clip, boxes, t_embed, mod_weight, mod_bias, tokens, wqkv, bqv, wout, bout, owners
):
    rows, width = tokens.shape
    frames = boxes.shape[0]
    pos = rows // frames // owners
    args = (frame_clip, boxes, t_embed, mod_weight, mod_bias, tokens, wqkv, bqv, wout, bout)
    return streamed(
        space_forward_kernel,
        args,
        (3, 5, 6, 8),
        [
            jax.ShapeDtypeStruct((owners, frames, pos, width), BF),
            jax.ShapeDtypeStruct((rows, 3 * width), BF),
            jax.ShapeDtypeStruct((rows, width), BF),
            jax.ShapeDtypeStruct((rows, width), F32),
            jax.ShapeDtypeStruct((3, t_embed.shape[0], width), F32),
        ],
        (0, 1, 2, 3),
        [pltpu.VMEM((rows, width), BF)],
        BRIEF,
        "space_forward",
        small=2,
        cut=((3, 3 * width),),
    )


def to_positions(source, stage, target):
    frames, pos, width = source.shape
    for lane in range(0, width, LANES):
        cols = pl.ds(lane, LANES)
        stage[lane // LANES] = source[:, :, cols].astype(F32).reshape(frames * pos, LANES)
        for p in range(pos):
            target[pl.ds(p * frames, frames), cols] = stage[
                lane // LANES, pl.ds(p, frames, stride=pos), :
            ].astype(target.dtype)


def stage_positions(stage, value, frames, pos, first):
    for lane in range(0, value.shape[1], LANES):
        for p in range(value.shape[0] // frames):
            stage[lane // LANES, pl.ds(first + p, frames, stride=pos), :] = value[
                p * frames : (p + 1) * frames, lane : lane + LANES
            ]


def to_frames(stage, target):
    frames, pos, width = target.shape
    for lane in range(0, width, LANES):
        target[:, :, pl.ds(lane, LANES)] = (
            stage[lane // LANES].reshape(frames, pos, LANES).astype(BF)
        )


def time_mask(ids_row_ref, clip_col, positions, clips):
    frames = clip_col.shape[0]
    place = lax.broadcasted_iota(jnp.int32, (positions, frames, 1), 0) * clips
    col = (place + clip_col[None]).reshape(positions * frames, 1)
    return jnp.where(col == ids_row_ref[...], 0.0, NEG)


def spread(rows, positions):
    frames, width = rows.shape
    return jnp.broadcast_to(rows[None], (positions, frames, width)).reshape(
        positions * frames, width
    )


def gather_frames(value, frames):
    return jnp.sum(value.reshape(-1, frames, value.shape[-1]), axis=0)


def per_clip_sums(out_ref, member, rows, clip_col):
    for c in range(out_ref.shape[1]):
        out_ref[member, c : c + 1, :] = jnp.sum(
            jnp.where(clip_col == c, rows, 0.0), axis=0, keepdims=True
        )


def gelu_and_slope(v):
    c = 0.7978845608028654
    square = v * v
    t = jnp.tanh(v * (c + (c * 0.044715) * square))
    half = 0.5 + 0.5 * t
    slope = half + (0.5 * v) * (1.0 - t * t) * (c + (3.0 * c * 0.044715) * square)
    return v * half, slope


def owner_forward_kernel(
    mid_ref, cot_ref, table_ref, clip_col_ref, ids_row_ref, wqkv_ref, bqv_ref, wout_ref, bout_ref,
    up_ref, upb_ref, down_ref, downb_ref,
    xa_ref, packed_ref, attended_ref, branch_ref, gmid_ref, result_ref, grad_ref, gclip_ref, gupb_ref,
    gdownb_ref,
    stage, mid, cot, normed, normed_t, gbranch, bias, act, ghid, branch_acc, gnorm_acc,
    cot_in, wqkv, wout, xa, packed, attended, branch_out, sem_in, sem_out,
):
    step = pl.program_id(0)
    frames, pos, width = mid_ref.shape
    blocks = frames * pos // BLOCK
    per_block = BLOCK // frames
    clips = table_ref.shape[1]
    clip_col = clip_col_ref[...]
    leaving = [
        (xa, xa_ref), (packed, packed_ref), (attended, attended_ref), (branch_out, branch_ref)
    ]

    def modvec(member):
        return spread(frame_rows(table_ref, member, clip_col), per_block)

    @pl.when(step == 0)
    def _():
        loads = copies([(wqkv_ref, wqkv), (cot_ref, cot_in), (wout_ref, wout)], sem_in)
        to_positions(mid_ref, stage, mid)
        xa[...] = mid[...].astype(BF)
        copies(leaving[:1], sem_out)
        bias[...] = time_mask(ids_row_ref, clip_col, per_block, clips)
        shift_b, scale_b = modvec(0), modvec(1)
        for b in range(blocks):
            part = pl.ds(b * BLOCK, BLOCK)
            n, _ = normalize(mid[part, :])
            normed[part, :] = (n * (1.0 + scale_b) + shift_b).astype(BF)
        loads[0].wait()
        project_qkv(normed, wqkv, bqv_ref, packed, width)
        copies(leaving[1:2], sem_out.at[pl.ds(1, 1)])
        attend(packed, attended, lambda b: bias[...], blocks, width)
        copies(leaving[2:3], sem_out.at[pl.ds(2, 1)])
        loads[1].wait()
        to_positions(cot_in, stage, cot)
        gate_b, shift_c, scale_c, gate_c = modvec(2), modvec(3), modvec(4), modvec(5)
        loads[2].wait()
        for b in range(blocks):
            part = pl.ds(b * BLOCK, BLOCK)
            branch = dot_nn(attended[part, :], wout[...]) + as_row(bout_ref[...])
            branch_out[part, :] = branch
            mid_b = mid[part, :] + gate_b * branch
            mid[part, :] = mid_b
            n, _ = normalize(mid_b)
            normed[part, :] = (n * (1.0 + scale_c) + shift_c).astype(BF)
            gbranch[part, :] = (gate_c * cot[part, :]).astype(BF)
        copies(leaving[3:], sem_out.at[pl.ds(3, 1)])
        normed_t[...] = normed[...].T
        gdownb_ref[...] = jnp.sum(gbranch[...].astype(F32), axis=0, keepdims=True)
        branch_acc[...] = jnp.zeros_like(branch_acc)
        gnorm_acc[...] = jnp.zeros_like(gnorm_acc)

    up_bias = chunk_row(upb_ref, step, act.shape[1])
    for b in range(blocks):
        part = pl.ds(b * BLOCK, BLOCK)
        hidden = dot_nn(normed[part, :], up_ref[...]) + up_bias
        value, slope = gelu_and_slope(hidden)
        value = value.astype(BF)
        act[part, :] = value
        gh = (dot_nt(gbranch[part, :], down_ref[...]) * slope).astype(BF)
        ghid[part, :] = gh
        branch_acc[part, :] += dot_nn(value, down_ref[...])
        gnorm_acc[part, :] += dot_nt(gh, up_ref[...])
    grad_ref[0] = dot_nn(normed_t[...], ghid[...]).astype(BF)
    grad_ref[1] = dot_tn(act[...], gbranch[...]).astype(BF)
    gupb_ref[0] = jnp.sum(ghid[...].astype(F32), axis=0, keepdims=True)

    @pl.when(step == pl.num_programs(0) - 1)
    def _():
        scale_c, gate_c = modvec(4), modvec(5)
        sums = [0.0, 0.0, 0.0]
        for b in range(blocks):
            part = pl.ds(b * BLOCK, BLOCK)
            up = cot[part, :]
            branch = branch_acc[part, :] + as_row(downb_ref[...])
            sums[2] = sums[2] + gather_frames(branch * up, frames)
            mid_b = mid[part, :]
            n, r = normalize(mid_b)
            g = gnorm_acc[part, :]
            sums[0] = sums[0] + gather_frames(g, frames)
            sums[1] = sums[1] + gather_frames(g * n, frames)
            gmid_ref[part, :] = up + normalize_back(n, r, g * (1.0 + scale_c))
            stage_positions(stage, mid_b + gate_c * branch, frames, pos, b * per_block)
        to_frames(stage, result_ref)
        for member in range(3):
            per_clip_sums(gclip_ref, member, sums[member], clip_col)
        for i, (source, target) in enumerate(leaving):
            pltpu.make_async_copy(source, target, sem_out.at[i]).wait()


def owner_forward(mid, cot, table, clip_col, ids_row, wqkv, bqv, wout, bout, up, upb, down, downb):
    frames, pos, width = mid.shape
    rows = frames * pos
    clips = table.shape[1]
    ff = up.shape[1]
    chunk = width
    steps = ff // chunk
    whole = lambda *shape: pl.BlockSpec(shape, lambda i: (0,) * len(shape))
    like = lambda cols, dtype: jax.ShapeDtypeStruct((rows, cols), dtype)
    wide = pltpu.VMEM((rows, width), F32)
    half = pltpu.VMEM((rows, width), BF)
    return pl.pallas_call(
        owner_forward_kernel,
        grid=(steps,),
        in_specs=[vmem(), hbm(), vmem(), vmem(), vmem(), hbm(), vmem(), hbm(), vmem()]
        + [
            pl.BlockSpec((width, chunk), lambda i: (0, i)),
            vmem(),
            pl.BlockSpec((chunk, width), lambda i: (i, 0)),
            vmem(),
        ],
        out_specs=[hbm()] * 4
        + [
            whole(rows, width),
            whole(frames, pos, width),
            pl.BlockSpec((2, width, chunk), lambda i: (0, i, 0)),
            whole(3, clips, width),
            pl.BlockSpec((1, 1, chunk), lambda i: (i, 0, 0)),
            whole(1, width),
        ],
        out_shape=[
            like(width, BF),
            like(3 * width, BF),
            like(width, BF),
            like(width, F32),
            like(width, F32),
            jax.ShapeDtypeStruct((frames, pos, width), BF),
            jax.ShapeDtypeStruct((2, ff, width), BF),
            jax.ShapeDtypeStruct((3, clips, width), F32),
            jax.ShapeDtypeStruct((steps, 1, chunk), F32),
            jax.ShapeDtypeStruct((1, width), F32),
        ],
        scratch_shapes=[
            pltpu.VMEM((width // LANES, rows, LANES), F32),
            wide,
            wide,
            half,
            pltpu.VMEM((width, rows), BF),
            half,
            pltpu.VMEM((BLOCK, BLOCK), F32),
            pltpu.VMEM((rows, chunk), BF),
            pltpu.VMEM((rows, chunk), BF),
            wide,
            wide,
            pltpu.VMEM((frames, pos, width), BF),
            pltpu.VMEM((width, 3 * width), BF),
            pltpu.VMEM((width, width), BF),
            half,
            pltpu.VMEM((rows, 3 * width), BF),
            half,
            wide,
            dma(3),
            dma(4),
        ],
        compiler_params=params(),
        cost_estimate=BRIEF,
        name="owner_forward",
    )(mid, cot, table, clip_col, ids_row, wqkv, bqv, wout, bout, up, upb, down, downb)


def put(grads, core, quarter, value):
    rows = pl.ds((quarter % 2) * value.shape[0], value.shape[0])
    value = value.astype(BF)
    for target, owner in zip(grads, (quarter // 2, 1 - quarter // 2)):

        @pl.when(core == owner)
        def _(target=target):
            target[rows, :] = value


def this_core():
    return lax.rem(lax.axis_index("seq"), 2)


def qkv_back(normed, grad_packed, wqkv_ref, grads, gqv_ref, gnorm, width):
    for c in range(3):
        cols = pl.ds(c * width, width)
        gp = grad_packed[:, cols]
        put(grads, this_core(), c, dot_tn(normed[...], gp))
        if c != 1:
            gqv_ref[c // 2 : c // 2 + 1, :] = jnp.sum(gp.astype(F32), axis=0, keepdims=True)
        back = dot_nt(gp, wqkv_ref[:, cols])
        gnorm[...] = back if c == 0 else gnorm[...] + back


def owner_backward_kernel(
    ready, flush,
    xa_ref, packed_ref, attended_ref, branch_ref, gmid_ref, table_ref, clip_col_ref, ids_row_ref,
    wqkv_ref, wout_ref,
    send_ref, kept_ref, other_ref, gclip_ref, goutb_ref, gqv_ref,
    stage, normed, gbranch, gatt, gpacked, bias, gnorm,
):
    frames, pos, width = send_ref.shape
    rows = frames * pos
    blocks = rows // BLOCK
    per_block = BLOCK // frames
    clips = table_ref.shape[1]
    clip_col = clip_col_ref[...]

    def modvec(member):
        return spread(frame_rows(table_ref, member, clip_col), per_block)

    shift, scale, gate = modvec(0), modvec(1), modvec(2)
    bias[...] = time_mask(ids_row_ref, clip_col, per_block, clips)
    gate_sum = 0.0
    ready(gmid_ref, branch_ref, wout_ref, xa_ref)
    for b in range(blocks):
        part = pl.ds(b * BLOCK, BLOCK)
        gm = gmid_ref[part, :]
        gate_sum = gate_sum + gather_frames(branch_ref[part, :] * gm, frames)
        gb = (gate * gm).astype(BF)
        gbranch[part, :] = gb
        gatt[part, :] = dot_nt(gb, wout_ref[...]).astype(BF)
        n, _ = normalize(xa_ref[part, :].astype(F32))
        normed[part, :] = (n * (1.0 + scale) + shift).astype(BF)
    per_clip_sums(gclip_ref, 2, gate_sum, clip_col)
    goutb_ref[...] = jnp.sum(gbranch[...].astype(F32), axis=0, keepdims=True)
    grads = (kept_ref, other_ref)
    ready(attended_ref)
    put(grads, this_core(), 3, dot_tn(attended_ref[...], gbranch[...]))
    ready(packed_ref)
    attend_back(packed_ref, gatt, gpacked, lambda b: bias[...], blocks, width)
    ready(wqkv_ref)
    qkv_back(normed, gpacked, wqkv_ref, grads, gqv_ref, gnorm, width)
    flush(other_ref, kept_ref)
    sums = [0.0, 0.0]
    for b in range(blocks):
        part = pl.ds(b * BLOCK, BLOCK)
        n, r = normalize(xa_ref[part, :].astype(F32))
        g = gnorm[part, :]
        sums[0] = sums[0] + gather_frames(g, frames)
        sums[1] = sums[1] + gather_frames(g * n, frames)
        total = gmid_ref[part, :] + normalize_back(n, r, g * (1.0 + scale))
        stage_positions(stage, total, frames, pos, b * per_block)
    to_frames(stage, send_ref)
    for member in range(2):
        per_clip_sums(gclip_ref, member, sums[member], clip_col)


def owner_backward(xa, packed, attended, branch, gmid, table, clip_col, ids_row, wqkv, wout):
    frames = clip_col.shape[0]
    rows, width = xa.shape
    clips = table.shape[1]
    half = pltpu.VMEM((rows, width), BF)
    return streamed(
        owner_backward_kernel,
        (xa, packed, attended, branch, gmid, table, clip_col, ids_row, wqkv, wout),
        (4, 3, 9, 0, 2, 1, 8),
        [
            jax.ShapeDtypeStruct((frames, rows // frames, width), BF),
            jax.ShapeDtypeStruct((2 * width, width), BF),
            jax.ShapeDtypeStruct((2 * width, width), BF),
            jax.ShapeDtypeStruct((3, clips, width), F32),
            jax.ShapeDtypeStruct((1, width), F32),
            jax.ShapeDtypeStruct((2, width), F32),
        ],
        (1, 2),
        [
            pltpu.VMEM((width // LANES, rows, LANES), F32),
            half,
            half,
            half,
            pltpu.VMEM((rows, 3 * width), BF),
            pltpu.VMEM((BLOCK, BLOCK), F32),
            pltpu.VMEM((rows, width), F32),
        ],
        BRIEF,
        "owner_backward",
    )


def space_backward_kernel(
    ready, flush,
    clip_ref, box_ref, x_ref, packed_ref, attended_ref, branch_ref, gmid_ref, table_ref,
    wqkv_ref, wout_ref, t_ref, gclip_b_ref, gclip_c_ref, gqv_b_ref, goutb_b_ref, gupb_ref, gdownb_ref,
    gx_ref, kept_ref, other_ref, small_ref,
    normed, gbranch, gatt, gpacked, gnorm, goutb_ref, gqv_ref, bias,
):
    frames = box_ref.shape[0]
    width = x_ref.shape[1]
    clips = table_ref.shape[1]
    clip = own_clips(clip_ref, frames)
    sums = [[None] * frames for _ in range(3)]
    for f in range(frames):
        bias[f] = jnp.broadcast_to(visible_bias(box_ref, f, BLOCK), (BLOCK, BLOCK)).T
    ready(gmid_ref, branch_ref, wout_ref, x_ref)
    for f in range(frames):
        part = pl.ds(f * BLOCK, BLOCK)
        gm = gmid_ref[:, f].reshape(BLOCK, width).astype(F32)
        sums[2][f] = jnp.sum(branch_ref[part, :] * gm, axis=0, keepdims=True)
        gb = (frame_row(table_ref, 2, clip[f]) * gm).astype(BF)
        gbranch[part, :] = gb
        gatt[part, :] = dot_nt(gb, wout_ref[...]).astype(BF)
        n, _ = normalize(x_ref[part, :].astype(F32))
        shift = frame_row(table_ref, 0, clip[f])
        scale = frame_row(table_ref, 1, clip[f])
        normed[part, :] = (n * (1.0 + scale) + shift).astype(BF)
    goutb_ref[...] = jnp.sum(gbranch[...].astype(F32), axis=0, keepdims=True)
    grads = (kept_ref, other_ref)
    ready(attended_ref)
    put(grads, this_core(), 3, dot_tn(attended_ref[...], gbranch[...]))
    ready(packed_ref)
    attend_back(packed_ref, gatt, gpacked, lambda b: bias[b], frames, width)
    ready(wqkv_ref)
    qkv_back(normed, gpacked, wqkv_ref, grads, gqv_ref, gnorm, width)
    flush(other_ref, kept_ref)
    for f in range(frames):
        part = pl.ds(f * BLOCK, BLOCK)
        n, r = normalize(x_ref[part, :].astype(F32))
        g = gnorm[part, :]
        sums[0][f] = jnp.sum(g, axis=0, keepdims=True)
        sums[1][f] = jnp.sum(g * n, axis=0, keepdims=True)
        scale = frame_row(table_ref, 1, clip[f])
        gm = gmid_ref[:, f].reshape(BLOCK, width).astype(F32)
        gx_ref[part, :] = (gm + normalize_back(n, r, g * (1.0 + scale))).astype(BF)
    all_clips = clips * lax.axis_size("dp")
    mine = lax.axis_index("dp") * clips
    small_ref[...] = jnp.zeros_like(small_ref)
    for member in range(9):
        for c in range(clips):
            if member < 3:
                total = jnp.zeros((1, width), F32)
                for f in range(frames):
                    total = total + jnp.where(clip[f] == c, sums[member][f], 0.0)
            else:
                source = gclip_b_ref if member < 6 else gclip_c_ref
                total = source[member % 3, c : c + 1, :]
            small_ref[pl.ds(member * all_clips + mine + c, 1), :] = total
    at = 9 * all_clips
    t = jnp.where(lax.axis_index("seq") == 0, t_ref[...].astype(F32), 0.0)
    for c in range(clips):
        small_ref[pl.ds(at + mine + c, 1), :] = t[c : c + 1]
    at += all_clips
    for source in (gqv_ref, goutb_ref, gqv_b_ref, goutb_b_ref, gupb_ref, gdownb_ref):
        for i in range(source.shape[0]):
            small_ref[at : at + 1, :] = source[i] if len(source.shape) == 3 else source[i : i + 1, :]
            at += 1
    flush(gx_ref)


def space_backward(frame_clip, boxes, tokens, *rest):
    rows, width = tokens.shape
    t_embed = rest[7]
    members = rest[-1].shape[0] + sum(value.shape[0] for value in rest[10:-1])
    extra = 3 + 10 * t_embed.shape[0] * lax.axis_size("dp") + members
    half = pltpu.VMEM((rows, width), BF)
    extra = -(-extra // 8) * 8
    return streamed(
        space_backward_kernel,
        (frame_clip, boxes, tokens) + rest,
        (6, 5, 9, 2, 4, 3, 8),
        [
            jax.ShapeDtypeStruct((rows, width), BF),
            jax.ShapeDtypeStruct((2 * width, width), BF),
            jax.ShapeDtypeStruct((2 * width, width), BF),
            jax.ShapeDtypeStruct((extra, width), F32),
        ],
        (0, 1, 2),
        [
            half,
            half,
            half,
            pltpu.VMEM((rows, 3 * width), BF),
            pltpu.VMEM((rows, width), F32),
            pltpu.VMEM((1, width), F32),
            pltpu.VMEM((2, width), F32),
            pltpu.VMEM((boxes.shape[0], BLOCK, BLOCK), F32),
        ],
        LONG,
        "space_backward",
        small=2,
    )


def routes(owners):
    depth = owners // 4
    places = [
        (x, z, y, c) for x in range(2) for z in range(depth) for y in range(2) for c in range(2)
    ]
    number = lambda x, z, y, c: x * owners + (z * 2 + y) * 2 + c
    pairs = lambda move: [(number(*p), number(*move(*p))) for p in places]
    over_x = lambda x, z, y, c: (1 - x, z, y, c)
    over_y = lambda x, z, y, c: (x, z, 1 - y, c)
    return {
        "core": pairs(lambda x, z, y, c: (x, z, y, 1 - c)),
        "first": pairs(lambda *p: (over_y if p[3] else over_x)(*p)),
        "second": pairs(lambda *p: (over_x if p[3] else over_y)(*p)),
        "x": pairs(over_x),
        "y": pairs(over_y),
        "depth": [
            pairs(lambda x, z, y, c, s=s: (x, (z + s) % depth, y, c)) for s in range(1, depth)
        ],
        "both": pairs(lambda x, z, y, c: (1 - x, z, 1 - y, c)),
        "swap": [pairs(lambda x, z, y, c, s=s: (x, z ^ s, y, c)) for s in range(1, depth)],
    }


def place():
    x, s = lax.axis_index("dp"), lax.axis_index("seq")
    return x, s >> 2, (s >> 1) & 1, s & 1


def move(value, pairs):
    return lax.ppermute(value, BOTH, pairs)


def tie(*values):
    return lax.optimization_barrier(values)


def side(stage, core):
    x, _, y, _ = place()
    return jnp.where(core == stage, x, y)


def cross_kernel(stage, kept_ref, got_ref, send_ref, out_ref, a, b, total, sem_a, sem_b, sem_out):
    count, rows, _ = total.shape
    each = count // 2
    bit = side(stage, place()[3])
    spots = [(half, pl.ds(i * rows, rows)) for half in (1 - bit, bit) for i in range(each)]
    from_a = copies([(kept_ref.at[h, r], a.at[i]) for i, (h, r) in enumerate(spots)], sem_a)
    from_b = copies([(got_ref.at[h, r], b.at[i]) for i, (h, r) in enumerate(spots)], sem_b)
    out = []
    for i, (_, r) in enumerate(spots):
        from_a[i].wait()
        from_b[i].wait()
        total[i] = (a[i].astype(F32) + b[i].astype(F32)).astype(BF)
        target = (send_ref if i < each else out_ref).at[r]
        out += copies([(total.at[i], target)], sem_out.at[pl.ds(i, 1)])
    for copy in out:
        copy.wait()


def cross_sum(cost, stage, kept, got):
    height, width = kept.shape[0] // 2, kept.shape[1]
    each = max(1, height // 384)
    buffer = pltpu.VMEM((2 * each, height // each, width), BF)
    half = jax.ShapeDtypeStruct((height, width), BF)
    return pl.pallas_call(
        functools.partial(cross_kernel, stage),
        in_specs=[hbm(), hbm()],
        out_specs=[hbm(), hbm()],
        out_shape=[half, half],
        scratch_shapes=[buffer] * 3 + [dma(2 * each)] * 3,
        compiler_params=alone(),
        cost_estimate=cost,
        name="cross_sum",
    )(kept.reshape(2, height, width), got.reshape(2, height, width))


def along_kernel(kept_ref, got_ref, *refs):
    depth = kept_ref.shape[0]
    targets = refs[:depth]
    a, b, total, sem_a, sem_b, sem_out = refs[depth:]
    z = place()[1]
    turns = list(range(1, depth)) + [0]
    parts = [lax.rem(z + s, depth) for s in turns]
    from_a = copies([(kept_ref.at[p], a.at[i]) for i, p in enumerate(parts)], sem_a)
    from_b = copies([(got_ref.at[p], b.at[i]) for i, p in enumerate(parts)], sem_b)
    out = []
    for i, s in enumerate(turns):
        from_a[i].wait()
        from_b[i].wait()
        total[i] = (a[i].astype(F32) + b[i].astype(F32)).astype(BF)
        out += copies([(total.at[i], targets[s])], sem_out.at[pl.ds(i, 1)])
    for copy in out:
        copy.wait()


def along_sum(cost, depth, kept, got):
    height, width = kept.shape[0] // depth, kept.shape[1]
    buffer = pltpu.VMEM((depth, height, width), BF)
    return pl.pallas_call(
        along_kernel,
        in_specs=[hbm()] * 2,
        out_specs=[hbm()] * depth,
        out_shape=[jax.ShapeDtypeStruct((height, width), BF)] * depth,
        scratch_shapes=[buffer] * 3 + [dma(depth)] * 3,
        compiler_params=alone(),
        cost_estimate=cost,
        name="along_sum",
    )(kept.reshape(depth, height, width), got.reshape(depth, height, width))


def finish_kernel(*refs):
    total = refs[0][...].astype(F32)
    for ref in refs[1:-1]:
        total = total + ref[...].astype(F32)
    refs[-1][...] = total.astype(refs[-1].dtype)


def finish_sum(cost, *parts):
    return pl.pallas_call(
        finish_kernel,
        in_specs=[vmem()] * len(parts),
        out_specs=vmem(),
        out_shape=jax.ShapeDtypeStruct(parts[0].shape, parts[0].dtype),
        compiler_params=alone(),
        cost_estimate=cost,
        name="finish_sum",
    )(*parts)


def collect_kernel(*refs):
    *parts, target, held, sem_in, sem_out = refs
    depth = target.shape[0]
    z = place()[1]
    for copy in copies(
        [(ref, held.at[lax.rem(z + depth - s, depth)]) for s, ref in enumerate(parts)], sem_in
    ):
        copy.wait()
    copies([(held, target)], sem_out)[0].wait()


def collect(cost, *parts):
    depth = len(parts)
    height, width = parts[0].shape
    return pl.pallas_call(
        collect_kernel,
        in_specs=[hbm()] * depth,
        out_specs=hbm(),
        out_shape=jax.ShapeDtypeStruct((depth, height, width), BF),
        scratch_shapes=[pltpu.VMEM((depth, height, width), BF), dma(depth), dma(1)],
        compiler_params=alone(),
        cost_estimate=cost,
        name="collect",
    )(*parts).reshape(depth * height, width)


class Sum:
    def __init__(self, kept, other, route):
        self.route = route
        self.kept = kept
        self.wait = move(other, route["core"])

    def cross(self, stage):
        send, self.kept = cross_sum(self.cost, stage, self.kept, self.wait)
        self.wait = move(send, self.route[("first", "second")[stage]])
        return "kept"

    def along(self):
        self.kept, *send = along_sum(self.cost, len(self.route["depth"]) + 1, self.kept, self.wait)
        self.wait = tuple(move(part, pairs) for part, pairs in zip(send, self.route["depth"]))
        return "kept"

    def finish(self):
        self.kept = finish_sum(self.cost, self.kept, *self.wait)
        self.wait = tuple(move(self.kept, pairs) for pairs in self.route["depth"])
        return "kept"

    def gather(self):
        self.near = collect(self.cost, self.kept, *self.wait)
        self.wait, self.across, self.core = (
            move(self.near, self.route[link]) for link in ("second", "first", "core")
        )
        return "near"

    def relay(self):
        self.far = self.wait
        got, self.core_far = (move(self.far, self.route[link]) for link in ("first", "core"))
        self.wait = (self.across, got)
        return "far"

    def reflect(self):
        self.across, self.across_far = self.wait
        self.wait = (self.core, self.core_far) + tuple(
            move(value, self.route["core"]) for value in self.wait
        )
        return "across"


class Order:
    def __init__(self):
        self.before = None
        self.cost = BRIEF

    def after(self, value):
        if self.before is not None:
            owner, name = self.before
            flat = value if isinstance(value, tuple) else (value,)
            *flat, late = tie(*flat, getattr(owner, name))
            setattr(owner, name, late)
            value = tuple(flat) if isinstance(value, tuple) else flat[0]
        return value

    def run(self, total, step, *args):
        total.cost = self.cost
        total.wait = self.after(total.wait)
        self.before = (total, getattr(total, step)(*args))


class Held:
    def __init__(self, value):
        self.value = value


def widen_kernel(other, spots, *refs):
    sources, (first_ref, second_ref), (held, wide, sem_in, sem_out) = refs[:4], refs[-6:-4], refs[-4:]
    height, width = held.shape[1:]
    loads = copies([(ref, held.at[i]) for i, ref in enumerate(sources)], sem_in)
    core = place()[3] ^ other
    stores = []
    for i, load in enumerate(loads):
        near, far = side(0, core) ^ (i >> 1), side(1, core) ^ (i & 1)
        block = core * 4 + near * 2 + far
        load.wait()
        wide[i] = held[i].astype(F32)
        in_first, (row, column), (row_2, column_2) = spots(block)
        place_1 = first_ref.at[
            pl.ds(pl.multiple_of(row * height, height), height),
            pl.ds(pl.multiple_of(column * width, width), width),
        ]
        place_2 = second_ref.at[
            pl.ds(pl.multiple_of(row_2 * height, height), height),
            pl.ds(pl.multiple_of(column_2 * width, width), width),
        ]
        store_1 = pltpu.make_async_copy(wide.at[i], place_1, sem_out.at[i])
        store_2 = pltpu.make_async_copy(wide.at[i], place_2, sem_out.at[i])
        pl.when(in_first)(store_1.start)
        pl.when(jnp.logical_not(in_first))(store_2.start)
        stores.append((in_first, store_1, store_2))
    for in_first, store_1, store_2 in stores:
        pl.when(in_first)(store_1.wait)
        pl.when(jnp.logical_not(in_first))(store_2.wait)


def widen(cost, other, parts, spots, shapes, before=()):
    height, width = parts[0].shape
    return pl.pallas_call(
        functools.partial(widen_kernel, other, spots),
        in_specs=[hbm()] * (4 + len(before)),
        out_specs=[hbm()] * 2,
        out_shape=[jax.ShapeDtypeStruct(shape, F32) for shape in shapes],
        input_output_aliases={4 + i: i for i in range(len(before))},
        scratch_shapes=[
            pltpu.VMEM((4, height, width), BF),
            pltpu.VMEM((4, height, width), F32),
            dma(4),
            dma(4),
        ],
        compiler_params=alone(),
        cost_estimate=cost,
        name="widen",
    )(*parts, *before)


def spots_of(split, first, second):
    def spots(block):
        return (
            block < split,
            first(jnp.minimum(block, split - 1)),
            second(jnp.maximum(block - split, 0)),
        )

    return spots


def widen_plain_kernel(split, maps, in_ref, first_ref, second_ref, held, wide, sem_in, sem_out):
    count, height, width = held.shape
    loads = copies(
        [(in_ref.at[pl.ds(i * height, height)], held.at[i]) for i in range(count)], sem_in
    )
    stores = []
    for i, load in enumerate(loads):
        load.wait()
        wide[i] = held[i].astype(F32)
        row, column = maps[0](i) if i < split else maps[1](i - split)
        target = (first_ref if i < split else second_ref).at[
            pl.ds(row * height, height), pl.ds(column * width, width)
        ]
        stores += copies([(wide.at[i], target)], sem_out.at[pl.ds(i, 1)])
    for store in stores:
        store.wait()


def widen_plain(summed, split, shapes, maps):
    width = summed.shape[1]
    height = summed.shape[0] // 8
    return pl.pallas_call(
        functools.partial(widen_plain_kernel, split, maps),
        in_specs=[hbm()],
        out_specs=[hbm()] * 2,
        out_shape=[jax.ShapeDtypeStruct(shape, F32) for shape in shapes],
        scratch_shapes=[
            pltpu.VMEM((8, height, width), BF),
            pltpu.VMEM((8, height, width), F32),
            dma(8),
            dma(8),
        ],
        compiler_params=alone(),
        cost_estimate=BRIEF,
        name="widen_plain",
    )(summed)


def mod_kernel(clips, sizes, small_ref, mod_ref, *refs):
    vectors, (smooth, split, mods, sem_mod) = refs[:-4], refs[-4:]
    members, width = 9, small_ref.shape[1]
    t = small_ref[pl.ds(members * clips, clips), :]
    value = (t / (1.0 + jnp.exp(-t))).astype(BF).astype(F32)
    smooth[...] = jnp.zeros_like(smooth)
    split[...] = jnp.zeros_like(split)
    for i in range(3):
        smooth[i * clips : (i + 1) * clips, :] = value
    left = smooth[...].astype(BF)
    slots = mods.shape[0]
    stores = []
    for member in range(members):
        rest = small_ref[pl.ds(member * clips, clips), :]
        vectors[0][pl.ds(member * width, width)] = jnp.sum(rest, axis=0)
        for i in range(3):
            piece = rest.astype(BF).astype(F32)
            split[i * clips : (i + 1) * clips, :] = piece
            rest = rest - piece
        if member >= slots:
            stores[member - slots].wait()
        mods[member % slots] = dot_tn(left, split[...].astype(BF))
        target = mod_ref.at[:, pl.ds(member * width, width)]
        stores += copies([(mods.at[member % slots], target)], sem_mod.at[pl.ds(member, 1)])
    at = (members + 1) * clips
    for vector, size in zip(vectors[1:], sizes):
        for i in range(size):
            vector[pl.ds(i * width, width)] = small_ref[at]
            at += 1
    for store in stores[-slots:]:
        store.wait()


def mod_grads(small, clips, sizes):
    width = small.shape[1]
    deep = -(-3 * clips // 16) * 16
    vector = lambda size: jax.ShapeDtypeStruct((size * width,), F32)
    return pl.pallas_call(
        functools.partial(mod_kernel, clips, sizes),
        in_specs=[vmem()],
        out_specs=[hbm()] + [vmem()] * (1 + len(sizes)),
        out_shape=[jax.ShapeDtypeStruct((width, 9 * width), F32), vector(9)]
        + [vector(size) for size in sizes],
        scratch_shapes=[
            pltpu.VMEM((deep, width), F32),
            pltpu.VMEM((deep, width), F32),
            pltpu.VMEM((9, width, width), F32),
            dma(9),
        ],
        compiler_params=alone(),
        cost_estimate=BRIEF,
        name="mod_grads",
    )(small)


def quad_kernel(*refs):
    values = [ref[...] for ref in refs[:-1]]
    while len(values) > 1:
        values = [a + b for a, b in zip(values[::2], values[1::2])]
    refs[-1][...] = values[0]


def pair_sum(*parts):
    return pl.pallas_call(
        quad_kernel,
        in_specs=[vmem()] * len(parts),
        out_specs=vmem(),
        out_shape=jax.ShapeDtypeStruct(parts[0].shape, parts[0].dtype),
        compiler_params=alone(),
        cost_estimate=BRIEF,
        name="pair_sum",
    )(*parts)


def per_device(
    tokens, t_embed, frame_clip, boxes, mod_weight, mod_bias, space_qkv, space_qv_bias, space_out,
    space_out_bias, time_qkv, time_qv_bias, time_out, time_out_bias, up_weight, up_bias,
    down_weight, down_bias, cotangent,
):
    owners = lax.axis_size("seq")
    groups = lax.axis_size("dp")
    frames = boxes.shape[0]
    width = tokens.shape[1]
    patches = tokens.shape[0] // frames
    group_frames = frame_clip.shape[0]
    pos = patches // owners
    clips = t_embed.shape[0]
    ff = up_weight.shape[1]
    depth = owners // 4
    own_route = depth <= 4
    route = routes(owners)

    clip_col = frame_clip[:, None]
    per_block = BLOCK // group_frames
    ids_row = (
        jnp.arange(per_block, dtype=jnp.int32)[:, None] * clips + frame_clip[None, :]
    ).reshape(1, BLOCK)

    def exchange(x):
        return lax.all_to_all(x, "seq", split_axis=0, concat_axis=0, tiled=True)

    qkv_maps = (lambda i: (i % 2, i // 2), lambda i: (i, 0))

    cot_send = cotangent.reshape(frames, owners, pos, width).transpose(1, 0, 2, 3)
    cot = exchange(cot_send)
    mid_send, packed_a, attended_a, branch_a, table_a = space_forward(
        frame_clip, boxes, t_embed, mod_weight, mod_bias, tokens, space_qkv, space_qv_bias, space_out,
        space_out_bias, owners,
    )
    mid_send, cot, t_late = tie(mid_send, cot, t_embed)
    mid = exchange(mid_send).reshape(group_frames, pos, width)
    cot = cot.reshape(group_frames, pos, width)
    table = modulation(t_late, mod_weight, mod_bias, 3, 6)
    (
        xa, packed_b, attended_b, branch_b, gmid_b, result_send, grad_f, gclip_c, gup_b, gdown_b,
    ) = owner_forward(
        mid, cot, table, clip_col, ids_row, time_qkv, time_qv_bias, time_out, time_out_bias, up_weight,
        up_bias, down_weight, down_bias,
    )
    ff_shapes = ((width, ff), (ff, width))
    qkv_shapes = ((width, 3 * width), (width, width))
    all_clips = clips * groups
    sizes = (2, 1, 2, 1, ff // width, 1)
    qkv_spots = spots_of(6, lambda i: (i % 2, i // 2), lambda i: (i, 0))

    def after_ff(gmid_b):
        return owner_backward(
            xa, packed_b, attended_b, branch_b, gmid_b, table, clip_col, ids_row, time_qkv, time_out
        )

    def after_time(gmid_a, gclip_b, gtout_b, gtqv_b):
        return space_backward(
            frame_clip, boxes, tokens, packed_a, attended_a, branch_a, gmid_a, table_a, space_qkv,
            space_out, t_embed, gclip_b, gclip_c, gtqv_b, gtout_b, gup_b, gdown_b,
        )

    result_send = result_send.reshape(owners, frames, pos, width)
    grad_f = grad_f.reshape(-1, width)
    part_f = Held(lax.psum_scatter(grad_f, BOTH, scatter_dimension=0, tiled=True))
    if own_route:
        sums = {}
        order = Order()
        wide = {}
        for name, *step in SCHEDULE:
            if name == "time":
                gmid_b = order.after(gmid_b)
                gmid_send, kept_t, other_t, gclip_b, gtout_b, gtqv_b = after_ff(gmid_b)
                gmid_a = exchange(gmid_send.reshape(owners, frames, pos, width))
                sums["t"] = Sum(kept_t, other_t, route)
                order.before = None
            elif name == "space":
                gmid_a = order.after(gmid_a)
                gmid_a, result_send = tie(gmid_a, result_send)
                result = exchange(result_send)
                grad_tokens, kept_s, other_s, small = after_time(
                    gmid_a, gclip_b, gtout_b, gtqv_b
                )
                sums["s"] = Sum(kept_s, other_s, route)
                kept_s, result = tie(sums["s"].kept, result)
                sums["s"].kept = kept_s
                order.before = None
            elif name == "ff":
                part_f.value = order.after(part_f.value)
                order.before = (part_f, "value")
            elif name == "small":
                links = (
                    [route["core"]]
                    if step[0] == 0
                    else [route["x"], route["y"], route["both"]]
                    if step[0] == 1
                    else route["swap"]
                )
                if step[0]:
                    small_got = order.after(small_got)
                    small = pair_sum(small, *small_got)
                    order.before = (Held(small), "value")
                small_got = tuple(move(small, pairs) for pairs in links)
            elif name == "mod":
                small = pair_sum(small, *order.after(small_got))
                mod = Held(None)
                mod.value, *vectors = mod_grads(small, all_clips, sizes)
                order.before = (mod, "value")
            elif step[0] == "widen":
                total = sums[name]
                if step[1]:
                    total.wait = order.after(total.wait)
                    parts = total.wait
                else:
                    total.across = order.after(total.across)
                    parts = (total.near, total.far, total.across, total.across_far)
                before = (wide[name].value, wide[name].other) if name in wide else ()
                pair = widen(order.cost, step[1], parts, qkv_spots, qkv_shapes, before)
                done = wide[name] = Held(pair[0])
                done.other = pair[1]
                order.before = (done, "value")
            else:
                order.cost = COSTS.get((name, *step), BRIEF)
                order.run(sums[name], *step)
        sum_f = lax.all_gather(part_f.value, BOTH, axis=0, tiled=True)
        grad_mod = mod.value
        wide_time, wide_space = ((wide[k].value, wide[k].other) for k in ("t", "s"))
    else:
        result = exchange(result_send)
        gmid_send, kept_t, other_t, gclip_b, gtout_b, gtqv_b = after_ff(gmid_b)
        gmid_a = exchange(gmid_send.reshape(owners, frames, pos, width))
        grad_tokens, kept_s, other_s, small = after_time(gmid_a, gclip_b, gtout_b, gtqv_b)
        small = lax.psum(small, BOTH)
        grad_mod, *vectors = mod_grads(small, all_clips, sizes)
        sum_f = lax.all_gather(part_f.value, BOTH, axis=0, tiled=True)
        core = place()[3]

        def whole(kept, other):
            halves = [jnp.where(core == half, kept, other) for half in range(2)]
            return lax.psum(jnp.concatenate(halves, axis=0), BOTH)

        qkv_maps = (lambda i: (i % 2, i // 2), lambda i: (i, 0))
        wide_time = widen_plain(whole(kept_t, other_t), 6, qkv_shapes, qkv_maps)
        wide_space = widen_plain(whole(kept_s, other_s), 6, qkv_shapes, qkv_maps)
    grad_up, grad_down = widen_plain(sum_f, 4, ff_shapes, (lambda i: (0, i), lambda i: (i, 0)))
    grad_mod_b, *biases = vectors
    return (
        result.transpose(1, 0, 2, 3).reshape(tokens.shape),
        grad_tokens,
        grad_mod,
        grad_mod_b,
        wide_space[0],
        biases[0],
        wide_space[1],
        biases[1],
        wide_time[0],
        biases[2],
        wide_time[1],
        biases[3],
        grad_up,
        biases[4],
        grad_down,
        biases[5],
    )


def solution(mesh):
    split = P(BOTH, None)
    placed = (split, P("dp", None), P("dp"), split) + (P(),) * 14 + (split,)
    return jax.shard_map(
        per_device,
        mesh=mesh,
        in_specs=placed,
        out_specs=(split, split) + (P(),) * 14,
        check_vma=False,
    )
```

```python
import functools

import jax
import jax.numpy as jnp
from jax import lax
from jax.experimental import pallas as pl
from jax.experimental.pallas import tpu as pltpu
from jax.sharding import PartitionSpec as P

HD = 64
GRID_W = 16
EPS = 1e-06
NEG = -1e30
BLOCK = 256
LANES = 128
BF = jnp.bfloat16
F32 = jnp.float32
VMEM_BYTES = 56 * 1024 * 1024
BOTH = ("dp", "seq")
BRIEF = pl.CostEstimate(flops=1000, bytes_accessed=1000, transcendentals=0)
SHORT = pl.CostEstimate(flops=4 * 10**9, bytes_accessed=1000, transcendentals=0)
MIDDLE = pl.CostEstimate(flops=10**10, bytes_accessed=1000, transcendentals=0)
LONG = pl.CostEstimate(flops=3 * 10**10, bytes_accessed=1000, transcendentals=0)

COSTS = {
    ("t", "cross", 1): LONG,
    ("t", "along"): MIDDLE,
    ("t", "finish"): MIDDLE,
    ("s", "along"): MIDDLE,
    ("t", "gather"): MIDDLE,
    ("s", "finish"): MIDDLE,
    ("s", "gather"): MIDDLE,
}
SCHEDULE = (
    ("time",),
    ("t", "cross", 0),
    ("space",),
    ("t", "cross", 1),
    ("s", "cross", 0),
    ("t", "along"),
    ("s", "cross", 1),
    ("t", "finish"),
    ("small", 0),
    ("s", "along"),
    ("t", "gather"),
    ("small", 1),
    ("s", "finish"),
    ("ff",),
    ("small", 2),
    ("t", "relay"),
    ("s", "gather"),
    ("t", "reflect"),
    ("t", "widen", 0),
    ("s", "relay"),
    ("mod",),
    ("t", "widen", 1),
    ("s", "reflect"),
    ("s", "widen", 0),
    ("s", "widen", 1),
)


def params():
    return pltpu.CompilerParams(vmem_limit_bytes=VMEM_BYTES)


def alone():
    return pltpu.CompilerParams(vmem_limit_bytes=60 * 1024 * 1024)


def dot_nn(a, b):
    return lax.dot_general(a, b, (((1,), (0,)), ((), ())), preferred_element_type=F32)


def dot_nt(a, b):
    return lax.dot_general(a, b, (((1,), (1,)), ((), ())), preferred_element_type=F32)


def dot_tn(a, b):
    return lax.dot_general(a, b, (((0,), (0,)), ((), ())), preferred_element_type=F32)


def normalize(x):
    center = x - jnp.mean(x, axis=-1, keepdims=True)
    r = lax.rsqrt(jnp.mean(center * center, axis=-1, keepdims=True) + EPS)
    return center * r, r


def normalize_back(n, r, m):
    return r * (
        m - jnp.mean(m, axis=-1, keepdims=True) - n * jnp.mean(m * n, axis=-1, keepdims=True)
    )


def head_halves(width):
    lane = lax.broadcasted_iota(jnp.int32, (1, width), 1)
    low = (lane < HD).astype(F32).astype(BF)
    return low, (lane >= HD).astype(F32).astype(BF)


def attend(packed, attended, bias, blocks, width):
    halves = head_halves(2 * HD)

    def pair(index, carry):
        off = pl.multiple_of(index * 2 * HD, 2 * HD)
        for b in range(blocks):
            rows = pl.ds(b * BLOCK, BLOCK)
            q = packed[rows, pl.ds(off, 2 * HD)]
            k = packed[rows, pl.ds(width + off, 2 * HD)]
            v = packed[rows, pl.ds(2 * width + off, 2 * HD)]
            out = None
            for half in halves:
                s = dot_nt(q, k * half) * (HD**-0.5) + bias(b)
                e = jnp.exp(s - jnp.max(s, axis=-1, keepdims=True))
                p = (e * (1.0 / jnp.sum(e, axis=-1, keepdims=True))).astype(BF)
                o = dot_nn(p, v * half)
                out = o if out is None else out + o
            attended[rows, pl.ds(off, 2 * HD)] = out.astype(BF)
        return carry

    lax.fori_loop(0, width // (2 * HD), pair, 0)


def attend_back(packed, grad_in, grad_packed, bias, blocks, width):
    halves = head_halves(2 * HD)
    factor = HD**-0.5

    def pair(index, carry):
        off = pl.multiple_of(index * 2 * HD, 2 * HD)
        for b in range(blocks):
            rows = pl.ds(b * BLOCK, BLOCK)
            q = packed[rows, pl.ds(off, 2 * HD)]
            k = packed[rows, pl.ds(width + off, 2 * HD)]
            v = packed[rows, pl.ds(2 * width + off, 2 * HD)]
            g = grad_in[rows, pl.ds(off, 2 * HD)]
            dq = dk = dv = 0.0
            for half in halves:
                kh = k * half
                s = dot_nt(kh, q) * factor + bias(b)
                e = jnp.exp(s - jnp.max(s, axis=0, keepdims=True))
                p = e * (1.0 / jnp.sum(e, axis=0, keepdims=True))
                gs = dot_nt(v * half, g)
                ds = (p * (gs - jnp.sum(p * gs, axis=0, keepdims=True))).astype(BF)
                dv = dv + dot_nn(p.astype(BF), g * half)
                dq = dq + dot_tn(ds, kh)
                dk = dk + dot_nn(ds, q * half)
            grad_packed[rows, pl.ds(off, 2 * HD)] = (dq * factor).astype(BF)
            grad_packed[rows, pl.ds(width + off, 2 * HD)] = (dk * factor).astype(BF)
            grad_packed[rows, pl.ds(2 * width + off, 2 * HD)] = dv.astype(BF)
        return carry

    lax.fori_loop(0, width // (2 * HD), pair, 0)


def project_qkv(normed, weight, qv_bias, packed, width):
    for c in range(3):
        cols = pl.ds(c * width, width)
        value = dot_nn(normed[...], weight[:, cols])
        if c != 1:
            value = value + as_row(qv_bias[pl.ds((c // 2) * width, width)])
        packed[:, cols] = value.astype(BF)


def modulation_kernel(first, t_ref, w_ref, b_ref, out_ref):
    t = t_ref[...].astype(F32)
    smooth = (t / (1.0 + jnp.exp(-t))).astype(BF)
    bias = chunk_row(b_ref, first + pl.program_id(0), t.shape[1])
    out_ref[0] = dot_nn(smooth, w_ref[...]) + bias


def modulation(t_embed, weight, bias, first, count):
    clips, width = t_embed.shape
    return pl.pallas_call(
        functools.partial(modulation_kernel, first),
        grid=(count,),
        in_specs=[
            pl.BlockSpec((clips, width), lambda i: (0, 0)),
            pl.BlockSpec((width, width), lambda i: (0, first + i)),
            vmem(),
        ],
        out_specs=pl.BlockSpec((1, clips, width), lambda i: (i, 0, 0)),
        out_shape=jax.ShapeDtypeStruct((count, clips, width), F32),
        cost_estimate=BRIEF,
        name="modulation",
    )(t_embed, weight, bias)


def as_row(vector):
    return vector.astype(F32).reshape(1, -1)


def chunk_row(vector_ref, index, width):
    return as_row(vector_ref[pl.ds(pl.multiple_of(index * width, width), width)])


def own_clips(clip_ref, frames):
    first = lax.axis_index("seq") * frames
    return [clip_ref[first + f] for f in range(frames)]


def frame_row(table, member, clip):
    total = jnp.zeros(table.shape[2:], F32)[None]
    for c in range(table.shape[1]):
        total = jnp.where(clip == c, table[member, c : c + 1, :], total)
    return total


def frame_rows(table, member, clip_col):
    total = jnp.zeros((clip_col.shape[0], table.shape[2]), F32)
    for c in range(table.shape[1]):
        total = jnp.where(clip_col == c, table[member, c : c + 1, :], total)
    return total


def visible_bias(box_ref, frame, patches):
    cell = lax.broadcasted_iota(jnp.int32, (1, patches), 1)
    row, col = cell // GRID_W, cell % GRID_W
    inside = (
        (row >= box_ref[frame, 0])
        & (row < box_ref[frame, 1])
        & (col >= box_ref[frame, 2])
        & (col < box_ref[frame, 3])
    )
    return jnp.where(inside, NEG, 0.0)


def space_forward_kernel(
    ready, flush,
    clip_ref, box_ref, t_ref, modw_ref, modb_ref, x_ref, wqkv_ref, bqv_ref, wout_ref, bout_ref,
    send_ref, packed_ref, attended_ref, branch_ref, table_ref, normed,
):
    frames = box_ref.shape[0]
    width = x_ref.shape[1]
    dst, _, pos, _ = send_ref.shape
    clip = own_clips(clip_ref, frames)
    t = t_ref[...].astype(F32)
    smooth = (t / (1.0 + jnp.exp(-t))).astype(BF)
    ready(modw_ref)
    for k in range(3):
        cols = pl.ds(k * width, width)
        table_ref[k] = dot_nn(smooth, modw_ref[:, cols]) + as_row(modb_ref[cols])
    ready(x_ref)
    for f in range(frames):
        rows = pl.ds(f * BLOCK, BLOCK)
        n, _ = normalize(x_ref[rows, :].astype(F32))
        shift = frame_row(table_ref, 0, clip[f])
        scale = frame_row(table_ref, 1, clip[f])
        normed[rows, :] = (n * (1.0 + scale) + shift).astype(BF)
    ready(wqkv_ref)
    project_qkv(normed, wqkv_ref, bqv_ref, packed_ref, width)
    flush(packed_ref)
    biases = [visible_bias(box_ref, f, BLOCK) for f in range(frames)]
    attend(packed_ref, attended_ref, lambda b: biases[b], frames, width)
    flush(attended_ref)
    ready(wout_ref)
    for f in range(frames):
        rows = pl.ds(f * BLOCK, BLOCK)
        branch = dot_nn(attended_ref[rows, :], wout_ref[...]) + as_row(bout_ref[...])
        branch_ref[rows, :] = branch
        gate = frame_row(table_ref, 2, clip[f])
        mid = x_ref[rows, :].astype(F32) + gate * branch
        send_ref[:, f] = mid.astype(BF).reshape(dst, pos, width)
    flush(send_ref, branch_ref)


def vmem():
    return pl.BlockSpec(memory_space=pltpu.VMEM)


def smem():
    return pl.BlockSpec(memory_space=pltpu.SMEM)


def hbm():
    return pl.BlockSpec(memory_space=pltpu.HBM)


def dma(count):
    return pltpu.SemaphoreType.DMA((count,))


def copies(pairs, semaphores):
    started = [
        pltpu.make_async_copy(source, target, semaphores.at[i])
        for i, (source, target) in enumerate(pairs)
    ]
    for copy in started:
        copy.start()
    return started


def streamed(body, args, late, out_shape, late_out, scratch, cost, name, small=0, cut=()):
    cut = dict(cut)
    n, m = len(args), len(out_shape)

    def shape_of(i):
        shape = args[i].shape
        return shape[:-1] + (cut[i],) if i in cut else shape

    def kernel(*refs):
        refs = list(refs)
        ins, outs, rest = refs[:n], refs[n : n + m], refs[n + m :]
        own, rest = rest[: len(scratch)], rest[len(scratch) :]
        in_buffers, out_buffers, (sem_in, sem_out) = rest[: len(late)], rest[len(late) : -2], rest[-2:]
        sources = [ins[i].at[:, pl.ds(0, cut[i])] if i in cut else ins[i] for i in late]
        waiting = list(zip(in_buffers, copies(list(zip(sources, in_buffers)), sem_in)))
        for i, buffer in zip(late, in_buffers):
            ins[i] = buffer
        pending = dict(zip(late_out, out_buffers))
        targets = {i: outs[i] for i in late_out}
        for i in late_out:
            outs[i] = pending[i]
        leaving = []

        def ready(*buffers):
            for buffer in buffers:
                for entry in list(waiting):
                    if entry[0] is buffer:
                        entry[1].wait()
                        waiting.remove(entry)

        def flush(*buffers):
            for buffer in buffers:
                for k, i in enumerate(late_out):
                    if out_buffers[k] is buffer:
                        leaving.extend(copies([(buffer, targets[i])], sem_out.at[pl.ds(k, 1)]))

        body(ready, flush, *ins, *outs, *own)
        for copy in leaving:
            copy.wait()

    in_specs = [smem() if i < small else hbm() if i in late else vmem() for i in range(n)]
    return pl.pallas_call(
        kernel,
        in_specs=in_specs,
        out_specs=[hbm() if i in late_out else vmem() for i in range(m)],
        out_shape=out_shape,
        scratch_shapes=list(scratch)
        + [pltpu.VMEM(shape_of(i), args[i].dtype) for i in late]
        + [pltpu.VMEM(out_shape[i].shape, out_shape[i].dtype) for i in late_out]
        + [dma(max(1, len(late))), dma(max(1, len(late_out)))],
        compiler_params=params(),
        cost_estimate=cost,
        name=name,
    )(*args)


def space_forward(
    frame_clip, boxes, t_embed, mod_weight, mod_bias, tokens, wqkv, bqv, wout, bout, owners
):
    rows, width = tokens.shape
    frames = boxes.shape[0]
    pos = rows // frames // owners
    args = (frame_clip, boxes, t_embed, mod_weight, mod_bias, tokens, wqkv, bqv, wout, bout)
    return streamed(
        space_forward_kernel,
        args,
        (3, 5, 6, 8),
        [
            jax.ShapeDtypeStruct((owners, frames, pos, width), BF),
            jax.ShapeDtypeStruct((rows, 3 * width), BF),
            jax.ShapeDtypeStruct((rows, width), BF),
            jax.ShapeDtypeStruct((rows, width), F32),
            jax.ShapeDtypeStruct((3, t_embed.shape[0], width), F32),
        ],
        (0, 1, 2, 3),
        [pltpu.VMEM((rows, width), BF)],
        BRIEF,
        "space_forward",
        small=2,
        cut=((3, 3 * width),),
    )


def to_positions(source, stage, target):
    frames, pos, width = source.shape
    for lane in range(0, width, LANES):
        cols = pl.ds(lane, LANES)
        stage[lane // LANES, pl.ds(0, frames * pos), :] = (
            source[:, :, cols].astype(F32).reshape(frames * pos, LANES)
        )
        for p in range(pos):
            target[pl.ds(p * frames, frames), cols] = stage[
                lane // LANES, pl.ds(p, frames, stride=pos), :
            ].astype(target.dtype)


def stage_positions(stage, value, frames, pos, first):
    for lane in range(0, value.shape[1], LANES):
        for p in range(value.shape[0] // frames):
            stage[lane // LANES, pl.ds(first + p, frames, stride=pos), :] = value[
                p * frames : (p + 1) * frames, lane : lane + LANES
            ]


def to_frames(stage, target):
    frames, pos, width = target.shape
    for lane in range(0, width, LANES):
        target[:, :, pl.ds(lane, LANES)] = (
            stage[lane // LANES, pl.ds(0, frames * pos), :].reshape(frames, pos, LANES).astype(BF)
        )


def time_mask(ids_row_ref, clip_col, positions, clips):
    frames = clip_col.shape[0]
    place = lax.broadcasted_iota(jnp.int32, (positions, frames, 1), 0) * clips
    col = (place + clip_col[None]).reshape(positions * frames, 1)
    return jnp.where(col == ids_row_ref[...], 0.0, NEG)


def spread(rows, positions):
    frames, width = rows.shape
    return jnp.broadcast_to(rows[None], (positions, frames, width)).reshape(
        positions * frames, width
    )


def gather_frames(value, frames):
    return jnp.sum(value.reshape(-1, frames, value.shape[-1]), axis=0)


def per_clip_sums(out_ref, member, rows, clip_col):
    for c in range(out_ref.shape[1]):
        out_ref[member, c : c + 1, :] = jnp.sum(
            jnp.where(clip_col == c, rows, 0.0), axis=0, keepdims=True
        )


def gelu_and_slope(v):
    c = 0.7978845608028654
    square = v * v
    t = jnp.tanh(v * (c + (c * 0.044715) * square))
    half = 0.5 + 0.5 * t
    slope = half + (0.5 * v) * (1.0 - t * t) * (c + (3.0 * c * 0.044715) * square)
    return v * half, slope


def owner_forward_kernel(
    mid_ref, cot_ref, table_ref, clip_col_ref, ids_row_ref, wqkv_ref, bqv_ref, wout_ref, bout_ref,
    up_ref, upb_ref, down_ref, downb_ref,
    xa_ref, packed_ref, attended_ref, branch_ref, gmid_ref, result_ref, grad_ref, gclip_ref, gupb_ref,
    gdownb_ref,
    stage, mid, cot, normed, normed_t, gbranch, bias, act, ghid, branch_acc, gnorm_acc,
    cot_in, wqkv, wout, xa, packed, attended, branch_out, sem_in, sem_out,
):
    step = pl.program_id(0)
    frames, pos, width = mid_ref.shape
    blocks = frames * pos // BLOCK
    per_block = BLOCK // frames
    clips = table_ref.shape[1]
    clip_col = clip_col_ref[...]
    leaving = [
        (xa, xa_ref), (packed, packed_ref), (attended, attended_ref), (branch_out, branch_ref)
    ]

    def modvec(member):
        return spread(frame_rows(table_ref, member, clip_col), per_block)

    @pl.when(step == 0)
    def _():
        loads = copies([(wqkv_ref, wqkv), (cot_ref, cot_in), (wout_ref, wout)], sem_in)
        to_positions(mid_ref, stage, mid)
        xa[...] = mid[...].astype(BF)
        copies(leaving[:1], sem_out)
        bias[...] = time_mask(ids_row_ref, clip_col, per_block, clips)
        shift_b, scale_b = modvec(0), modvec(1)
        for b in range(blocks):
            part = pl.ds(b * BLOCK, BLOCK)
            n, _ = normalize(mid[part, :])
            normed[part, :] = (n * (1.0 + scale_b) + shift_b).astype(BF)
        loads[0].wait()
        project_qkv(normed, wqkv, bqv_ref, packed, width)
        copies(leaving[1:2], sem_out.at[pl.ds(1, 1)])
        attend(packed, attended, lambda b: bias[...], blocks, width)
        copies(leaving[2:3], sem_out.at[pl.ds(2, 1)])
        loads[1].wait()
        to_positions(cot_in, stage, cot)
        gate_b, shift_c, scale_c, gate_c = modvec(2), modvec(3), modvec(4), modvec(5)
        loads[2].wait()
        for b in range(blocks):
            part = pl.ds(b * BLOCK, BLOCK)
            branch = dot_nn(attended[part, :], wout[...]) + as_row(bout_ref[...])
            branch_out[part, :] = branch
            mid_b = mid[part, :] + gate_b * branch
            mid[part, :] = mid_b
            n, _ = normalize(mid_b)
            normed[part, :] = (n * (1.0 + scale_c) + shift_c).astype(BF)
            gbranch[part, :] = (gate_c * cot[part, :]).astype(BF)
        copies(leaving[3:], sem_out.at[pl.ds(3, 1)])
        normed_t[...] = normed[...].T
        gdownb_ref[...] = jnp.sum(gbranch[...].astype(F32), axis=0, keepdims=True)
        branch_acc[...] = jnp.zeros_like(branch_acc)
        gnorm_acc[...] = jnp.zeros_like(gnorm_acc)

    up_bias = chunk_row(upb_ref, step, act.shape[1])
    for b in range(blocks):
        part = pl.ds(b * BLOCK, BLOCK)
        hidden = dot_nn(normed[part, :], up_ref[...]) + up_bias
        value, slope = gelu_and_slope(hidden)
        value = value.astype(BF)
        act[part, :] = value
        gh = (dot_nt(gbranch[part, :], down_ref[...]) * slope).astype(BF)
        ghid[part, :] = gh
        branch_acc[part, :] += dot_nn(value, down_ref[...])
        gnorm_acc[part, :] += dot_nt(gh, up_ref[...])
    grad_ref[0] = dot_nn(normed_t[...], ghid[...]).astype(BF)
    grad_ref[1] = dot_tn(act[...], gbranch[...]).astype(BF)
    gupb_ref[0] = jnp.sum(ghid[...].astype(F32), axis=0, keepdims=True)

    @pl.when(step == pl.num_programs(0) - 1)
    def _():
        scale_c, gate_c = modvec(4), modvec(5)
        sums = [0.0, 0.0, 0.0]
        for b in range(blocks):
            part = pl.ds(b * BLOCK, BLOCK)
            up = cot[part, :]
            branch = branch_acc[part, :] + as_row(downb_ref[...])
            sums[2] = sums[2] + gather_frames(branch * up, frames)
            mid_b = mid[part, :]
            n, r = normalize(mid_b)
            g = gnorm_acc[part, :]
            sums[0] = sums[0] + gather_frames(g, frames)
            sums[1] = sums[1] + gather_frames(g * n, frames)
            gmid_ref[part, :] = up + normalize_back(n, r, g * (1.0 + scale_c))
            stage_positions(stage, mid_b + gate_c * branch, frames, pos, b * per_block)
        to_frames(stage, result_ref)
        for member in range(3):
            per_clip_sums(gclip_ref, member, sums[member], clip_col)
        for i, (source, target) in enumerate(leaving):
            pltpu.make_async_copy(source, target, sem_out.at[i]).wait()


def owner_forward(mid, cot, table, clip_col, ids_row, wqkv, bqv, wout, bout, up, upb, down, downb):
    frames, pos, width = mid.shape
    rows = frames * pos
    clips = table.shape[1]
    ff = up.shape[1]
    chunk = width
    steps = ff // chunk
    whole = lambda *shape: pl.BlockSpec(shape, lambda i: (0,) * len(shape))
    like = lambda cols, dtype: jax.ShapeDtypeStruct((rows, cols), dtype)
    wide = pltpu.VMEM((rows, width), F32)
    half = pltpu.VMEM((rows, width), BF)
    return pl.pallas_call(
        owner_forward_kernel,
        grid=(steps,),
        in_specs=[vmem(), hbm(), vmem(), vmem(), vmem(), hbm(), vmem(), hbm(), vmem()]
        + [
            pl.BlockSpec((width, chunk), lambda i: (0, i)),
            vmem(),
            pl.BlockSpec((chunk, width), lambda i: (i, 0)),
            vmem(),
        ],
        out_specs=[hbm()] * 4
        + [
            whole(rows, width),
            whole(frames, pos, width),
            pl.BlockSpec((2, width, chunk), lambda i: (0, i, 0)),
            whole(3, clips, width),
            pl.BlockSpec((1, 1, chunk), lambda i: (i, 0, 0)),
            whole(1, width),
        ],
        out_shape=[
            like(width, BF),
            like(3 * width, BF),
            like(width, BF),
            like(width, F32),
            like(width, F32),
            jax.ShapeDtypeStruct((frames, pos, width), BF),
            jax.ShapeDtypeStruct((2, ff, width), BF),
            jax.ShapeDtypeStruct((3, clips, width), F32),
            jax.ShapeDtypeStruct((steps, 1, chunk), F32),
            jax.ShapeDtypeStruct((1, width), F32),
        ],
        scratch_shapes=[
            pltpu.VMEM((width // LANES, rows + 16, LANES), F32),
            wide,
            wide,
            half,
            pltpu.VMEM((width, rows), BF),
            half,
            pltpu.VMEM((BLOCK, BLOCK), F32),
            pltpu.VMEM((rows, chunk), BF),
            pltpu.VMEM((rows, chunk), BF),
            wide,
            wide,
            pltpu.VMEM((frames, pos, width), BF),
            pltpu.VMEM((width, 3 * width), BF),
            pltpu.VMEM((width, width), BF),
            half,
            pltpu.VMEM((rows, 3 * width), BF),
            half,
            wide,
            dma(3),
            dma(4),
        ],
        compiler_params=params(),
        cost_estimate=BRIEF,
        name="owner_forward",
    )(mid, cot, table, clip_col, ids_row, wqkv, bqv, wout, bout, up, upb, down, downb)


def put(grads, core, quarter, value):
    rows = pl.ds((quarter % 2) * value.shape[0], value.shape[0])
    value = value.astype(BF)
    for target, owner in zip(grads, (quarter // 2, 1 - quarter // 2)):

        @pl.when(core == owner)
        def _(target=target):
            target[rows, :] = value


def this_core():
    return lax.rem(lax.axis_index("seq"), 2)


def qkv_back(normed, grad_packed, wqkv_ref, grads, gqv_ref, gnorm, width):
    for c in range(3):
        cols = pl.ds(c * width, width)
        gp = grad_packed[:, cols]
        put(grads, this_core(), c, dot_tn(normed[...], gp))
        if c != 1:
            gqv_ref[c // 2 : c // 2 + 1, :] = jnp.sum(gp.astype(F32), axis=0, keepdims=True)
        back = dot_nt(gp, wqkv_ref[:, cols])
        gnorm[...] = back if c == 0 else gnorm[...] + back


def owner_backward_kernel(
    ready, flush,
    xa_ref, packed_ref, attended_ref, branch_ref, gmid_ref, table_ref, clip_col_ref, ids_row_ref,
    wqkv_ref, wout_ref,
    send_ref, kept_ref, other_ref, gclip_ref, goutb_ref, gqv_ref,
    stage, normed, gbranch, gatt, gpacked, bias, gnorm,
):
    frames, pos, width = send_ref.shape
    rows = frames * pos
    blocks = rows // BLOCK
    per_block = BLOCK // frames
    clips = table_ref.shape[1]
    clip_col = clip_col_ref[...]

    def modvec(member):
        return spread(frame_rows(table_ref, member, clip_col), per_block)

    shift, scale, gate = modvec(0), modvec(1), modvec(2)
    bias[...] = time_mask(ids_row_ref, clip_col, per_block, clips)
    gate_sum = 0.0
    ready(gmid_ref, branch_ref, wout_ref, xa_ref)
    for b in range(blocks):
        part = pl.ds(b * BLOCK, BLOCK)
        gm = gmid_ref[part, :]
        gate_sum = gate_sum + gather_frames(branch_ref[part, :] * gm, frames)
        gb = (gate * gm).astype(BF)
        gbranch[part, :] = gb
        gatt[part, :] = dot_nt(gb, wout_ref[...]).astype(BF)
        n, _ = normalize(xa_ref[part, :].astype(F32))
        normed[part, :] = (n * (1.0 + scale) + shift).astype(BF)
    per_clip_sums(gclip_ref, 2, gate_sum, clip_col)
    goutb_ref[...] = jnp.sum(gbranch[...].astype(F32), axis=0, keepdims=True)
    grads = (kept_ref, other_ref)
    ready(attended_ref)
    put(grads, this_core(), 3, dot_tn(attended_ref[...], gbranch[...]))
    ready(packed_ref)
    attend_back(packed_ref, gatt, gpacked, lambda b: bias[...], blocks, width)
    ready(wqkv_ref)
    qkv_back(normed, gpacked, wqkv_ref, grads, gqv_ref, gnorm, width)
    flush(other_ref, kept_ref)
    sums = [0.0, 0.0]
    for b in range(blocks):
        part = pl.ds(b * BLOCK, BLOCK)
        n, r = normalize(xa_ref[part, :].astype(F32))
        g = gnorm[part, :]
        sums[0] = sums[0] + gather_frames(g, frames)
        sums[1] = sums[1] + gather_frames(g * n, frames)
        total = gmid_ref[part, :] + normalize_back(n, r, g * (1.0 + scale))
        stage_positions(stage, total, frames, pos, b * per_block)
    to_frames(stage, send_ref)
    for member in range(2):
        per_clip_sums(gclip_ref, member, sums[member], clip_col)


def owner_backward(xa, packed, attended, branch, gmid, table, clip_col, ids_row, wqkv, wout):
    frames = clip_col.shape[0]
    rows, width = xa.shape
    clips = table.shape[1]
    half = pltpu.VMEM((rows, width), BF)
    return streamed(
        owner_backward_kernel,
        (xa, packed, attended, branch, gmid, table, clip_col, ids_row, wqkv, wout),
        (4, 3, 9, 0, 2, 1, 8),
        [
            jax.ShapeDtypeStruct((frames, rows // frames, width), BF),
            jax.ShapeDtypeStruct((2 * width, width), BF),
            jax.ShapeDtypeStruct((2 * width, width), BF),
            jax.ShapeDtypeStruct((3, clips, width), F32),
            jax.ShapeDtypeStruct((1, width), F32),
            jax.ShapeDtypeStruct((2, width), F32),
        ],
        (1, 2),
        [
            pltpu.VMEM((width // LANES, rows + 16, LANES), F32),
            half,
            half,
            half,
            pltpu.VMEM((rows, 3 * width), BF),
            pltpu.VMEM((BLOCK, BLOCK), F32),
            pltpu.VMEM((rows, width), F32),
        ],
        BRIEF,
        "owner_backward",
    )


def space_backward_kernel(
    ready, flush,
    clip_ref, box_ref, x_ref, packed_ref, attended_ref, branch_ref, gmid_ref, table_ref,
    wqkv_ref, wout_ref, t_ref, gclip_b_ref, gclip_c_ref, gqv_b_ref, goutb_b_ref, gupb_ref, gdownb_ref,
    gx_ref, kept_ref, other_ref, small_ref,
    normed, gbranch, gatt, gpacked, gnorm, goutb_ref, gqv_ref, bias,
):
    frames = box_ref.shape[0]
    width = x_ref.shape[1]
    clips = table_ref.shape[1]
    clip = own_clips(clip_ref, frames)
    sums = [[None] * frames for _ in range(3)]
    for f in range(frames):
        bias[f] = jnp.broadcast_to(visible_bias(box_ref, f, BLOCK), (BLOCK, BLOCK)).T
    ready(gmid_ref, branch_ref, wout_ref, x_ref)
    for f in range(frames):
        part = pl.ds(f * BLOCK, BLOCK)
        gm = gmid_ref[:, f].reshape(BLOCK, width).astype(F32)
        sums[2][f] = jnp.sum(branch_ref[part, :] * gm, axis=0, keepdims=True)
        gb = (frame_row(table_ref, 2, clip[f]) * gm).astype(BF)
        gbranch[part, :] = gb
        gatt[part, :] = dot_nt(gb, wout_ref[...]).astype(BF)
        n, _ = normalize(x_ref[part, :].astype(F32))
        shift = frame_row(table_ref, 0, clip[f])
        scale = frame_row(table_ref, 1, clip[f])
        normed[part, :] = (n * (1.0 + scale) + shift).astype(BF)
    goutb_ref[...] = jnp.sum(gbranch[...].astype(F32), axis=0, keepdims=True)
    grads = (kept_ref, other_ref)
    ready(attended_ref)
    put(grads, this_core(), 3, dot_tn(attended_ref[...], gbranch[...]))
    ready(packed_ref)
    attend_back(packed_ref, gatt, gpacked, lambda b: bias[b], frames, width)
    ready(wqkv_ref)
    qkv_back(normed, gpacked, wqkv_ref, grads, gqv_ref, gnorm, width)
    flush(other_ref, kept_ref)
    for f in range(frames):
        part = pl.ds(f * BLOCK, BLOCK)
        n, r = normalize(x_ref[part, :].astype(F32))
        g = gnorm[part, :]
        sums[0][f] = jnp.sum(g, axis=0, keepdims=True)
        sums[1][f] = jnp.sum(g * n, axis=0, keepdims=True)
        scale = frame_row(table_ref, 1, clip[f])
        gm = gmid_ref[:, f].reshape(BLOCK, width).astype(F32)
        gx_ref[part, :] = (gm + normalize_back(n, r, g * (1.0 + scale))).astype(BF)
    all_clips = clips * lax.axis_size("dp")
    mine = lax.axis_index("dp") * clips
    small_ref[...] = jnp.zeros_like(small_ref)
    for member in range(9):
        for c in range(clips):
            if member < 3:
                total = jnp.zeros((1, width), F32)
                for f in range(frames):
                    total = total + jnp.where(clip[f] == c, sums[member][f], 0.0)
            else:
                source = gclip_b_ref if member < 6 else gclip_c_ref
                total = source[member % 3, c : c + 1, :]
            small_ref[pl.ds(member * all_clips + mine + c, 1), :] = total
    at = 9 * all_clips
    t = jnp.where(lax.axis_index("seq") == 0, t_ref[...].astype(F32), 0.0)
    for c in range(clips):
        small_ref[pl.ds(at + mine + c, 1), :] = t[c : c + 1]
    at += all_clips
    for source in (gqv_ref, goutb_ref, gqv_b_ref, goutb_b_ref, gupb_ref, gdownb_ref):
        for i in range(source.shape[0]):
            small_ref[at : at + 1, :] = source[i] if len(source.shape) == 3 else source[i : i + 1, :]
            at += 1
    flush(gx_ref)


def space_backward(frame_clip, boxes, tokens, *rest):
    rows, width = tokens.shape
    t_embed = rest[7]
    members = rest[-1].shape[0] + sum(value.shape[0] for value in rest[10:-1])
    extra = 3 + 10 * t_embed.shape[0] * lax.axis_size("dp") + members
    half = pltpu.VMEM((rows, width), BF)
    extra = -(-extra // 8) * 8
    return streamed(
        space_backward_kernel,
        (frame_clip, boxes, tokens) + rest,
        (6, 5, 9, 2, 4, 3, 8),
        [
            jax.ShapeDtypeStruct((rows, width), BF),
            jax.ShapeDtypeStruct((2 * width, width), BF),
            jax.ShapeDtypeStruct((2 * width, width), BF),
            jax.ShapeDtypeStruct((extra, width), F32),
        ],
        (0, 1, 2),
        [
            half,
            half,
            half,
            pltpu.VMEM((rows, 3 * width), BF),
            pltpu.VMEM((rows, width), F32),
            pltpu.VMEM((1, width), F32),
            pltpu.VMEM((2, width), F32),
            pltpu.VMEM((boxes.shape[0], BLOCK, BLOCK), F32),
        ],
        LONG,
        "space_backward",
        small=2,
    )


def routes(owners):
    depth = owners // 4
    places = [
        (x, z, y, c) for x in range(2) for z in range(depth) for y in range(2) for c in range(2)
    ]
    number = lambda x, z, y, c: x * owners + (z * 2 + y) * 2 + c
    pairs = lambda move: [(number(*p), number(*move(*p))) for p in places]
    over_x = lambda x, z, y, c: (1 - x, z, y, c)
    over_y = lambda x, z, y, c: (x, z, 1 - y, c)
    return {
        "core": pairs(lambda x, z, y, c: (x, z, y, 1 - c)),
        "first": pairs(lambda *p: (over_y if p[3] else over_x)(*p)),
        "second": pairs(lambda *p: (over_x if p[3] else over_y)(*p)),
        "x": pairs(over_x),
        "y": pairs(over_y),
        "depth": [
            pairs(lambda x, z, y, c, s=s: (x, (z + s) % depth, y, c)) for s in range(1, depth)
        ],
        "both": pairs(lambda x, z, y, c: (1 - x, z, 1 - y, c)),
        "swap": [pairs(lambda x, z, y, c, s=s: (x, z ^ s, y, c)) for s in range(1, depth)],
    }


def place():
    x, s = lax.axis_index("dp"), lax.axis_index("seq")
    return x, s >> 2, (s >> 1) & 1, s & 1


def move(value, pairs):
    return lax.ppermute(value, BOTH, pairs)


def tie(*values):
    return lax.optimization_barrier(values)


def side(stage, core):
    x, _, y, _ = place()
    return jnp.where(core == stage, x, y)


def cross_kernel(stage, kept_ref, got_ref, send_ref, out_ref, a, b, total, sem_a, sem_b, sem_out):
    count, rows, _ = total.shape
    each = count // 2
    bit = side(stage, place()[3])
    spots = [(half, pl.ds(i * rows, rows)) for half in (1 - bit, bit) for i in range(each)]
    from_a = copies([(kept_ref.at[h, r], a.at[i]) for i, (h, r) in enumerate(spots)], sem_a)
    from_b = copies([(got_ref.at[h, r], b.at[i]) for i, (h, r) in enumerate(spots)], sem_b)
    out = []
    for i, (_, r) in enumerate(spots):
        from_a[i].wait()
        from_b[i].wait()
        total[i] = (a[i].astype(F32) + b[i].astype(F32)).astype(BF)
        target = (send_ref if i < each else out_ref).at[r]
        out += copies([(total.at[i], target)], sem_out.at[pl.ds(i, 1)])
    for copy in out:
        copy.wait()


def cross_sum(cost, stage, kept, got):
    height, width = kept.shape[0] // 2, kept.shape[1]
    each = max(1, height // 384)
    buffer = pltpu.VMEM((2 * each, height // each, width), BF)
    half = jax.ShapeDtypeStruct((height, width), BF)
    return pl.pallas_call(
        functools.partial(cross_kernel, stage),
        in_specs=[hbm(), hbm()],
        out_specs=[hbm(), hbm()],
        out_shape=[half, half],
        scratch_shapes=[buffer] * 3 + [dma(2 * each)] * 3,
        compiler_params=alone(),
        cost_estimate=cost,
        name="cross_sum",
    )(kept.reshape(2, height, width), got.reshape(2, height, width))


def along_kernel(kept_ref, got_ref, *refs):
    depth = kept_ref.shape[0]
    targets = refs[:depth]
    a, b, total, sem_a, sem_b, sem_out = refs[depth:]
    z = place()[1]
    turns = list(range(1, depth)) + [0]
    parts = [lax.rem(z + s, depth) for s in turns]
    from_a = copies([(kept_ref.at[p], a.at[i]) for i, p in enumerate(parts)], sem_a)
    from_b = copies([(got_ref.at[p], b.at[i]) for i, p in enumerate(parts)], sem_b)
    out = []
    for i, s in enumerate(turns):
        from_a[i].wait()
        from_b[i].wait()
        total[i] = (a[i].astype(F32) + b[i].astype(F32)).astype(BF)
        out += copies([(total.at[i], targets[s])], sem_out.at[pl.ds(i, 1)])
    for copy in out:
        copy.wait()


def along_sum(cost, depth, kept, got):
    height, width = kept.shape[0] // depth, kept.shape[1]
    buffer = pltpu.VMEM((depth, height, width), BF)
    return pl.pallas_call(
        along_kernel,
        in_specs=[hbm()] * 2,
        out_specs=[hbm()] * depth,
        out_shape=[jax.ShapeDtypeStruct((height, width), BF)] * depth,
        scratch_shapes=[buffer] * 3 + [dma(depth)] * 3,
        compiler_params=alone(),
        cost_estimate=cost,
        name="along_sum",
    )(kept.reshape(depth, height, width), got.reshape(depth, height, width))


def finish_kernel(*refs):
    total = refs[0][...].astype(F32)
    for ref in refs[1:-1]:
        total = total + ref[...].astype(F32)
    refs[-1][...] = total.astype(refs[-1].dtype)


def finish_sum(cost, *parts):
    return pl.pallas_call(
        finish_kernel,
        in_specs=[vmem()] * len(parts),
        out_specs=vmem(),
        out_shape=jax.ShapeDtypeStruct(parts[0].shape, parts[0].dtype),
        compiler_params=alone(),
        cost_estimate=cost,
        name="finish_sum",
    )(*parts)


def collect_kernel(*refs):
    *parts, target, held, sem_in, sem_out = refs
    depth = target.shape[0]
    z = place()[1]
    for copy in copies(
        [(ref, held.at[lax.rem(z + depth - s, depth)]) for s, ref in enumerate(parts)], sem_in
    ):
        copy.wait()
    copies([(held, target)], sem_out)[0].wait()


def collect(cost, *parts):
    depth = len(parts)
    height, width = parts[0].shape
    return pl.pallas_call(
        collect_kernel,
        in_specs=[hbm()] * depth,
        out_specs=hbm(),
        out_shape=jax.ShapeDtypeStruct((depth, height, width), BF),
        scratch_shapes=[pltpu.VMEM((depth, height, width), BF), dma(depth), dma(1)],
        compiler_params=alone(),
        cost_estimate=cost,
        name="collect",
    )(*parts).reshape(depth * height, width)


class Sum:
    def __init__(self, kept, other, route):
        self.route = route
        self.kept = kept
        self.wait = move(other, route["core"])

    def cross(self, stage):
        send, self.kept = cross_sum(self.cost, stage, self.kept, self.wait)
        self.wait = move(send, self.route[("first", "second")[stage]])
        return "kept"

    def along(self):
        self.kept, *send = along_sum(self.cost, len(self.route["depth"]) + 1, self.kept, self.wait)
        self.wait = tuple(move(part, pairs) for part, pairs in zip(send, self.route["depth"]))
        return "kept"

    def finish(self):
        self.kept = finish_sum(self.cost, self.kept, *self.wait)
        self.wait = tuple(move(self.kept, pairs) for pairs in self.route["depth"])
        return "kept"

    def gather(self):
        self.near = collect(self.cost, self.kept, *self.wait)
        self.wait, self.across, self.core = (
            move(self.near, self.route[link]) for link in ("second", "first", "core")
        )
        return "near"

    def relay(self):
        self.far = self.wait
        got, self.core_far = (move(self.far, self.route[link]) for link in ("first", "core"))
        self.wait = (self.across, got)
        return "far"

    def reflect(self):
        self.across, self.across_far = self.wait
        self.wait = (self.core, self.core_far) + tuple(
            move(value, self.route["core"]) for value in self.wait
        )
        return "across"


class Order:
    def __init__(self):
        self.before = None
        self.cost = BRIEF

    def after(self, value):
        if self.before is not None:
            owner, name = self.before
            flat = value if isinstance(value, tuple) else (value,)
            *flat, late = tie(*flat, getattr(owner, name))
            setattr(owner, name, late)
            value = tuple(flat) if isinstance(value, tuple) else flat[0]
        return value

    def run(self, total, step, *args):
        total.cost = self.cost
        total.wait = self.after(total.wait)
        self.before = (total, getattr(total, step)(*args))


class Held:
    def __init__(self, value):
        self.value = value


def widen_kernel(other, spots, *refs):
    sources, (first_ref, second_ref), (held, wide, sem_in, sem_out) = refs[:4], refs[-6:-4], refs[-4:]
    height, width = held.shape[1:]
    loads = copies([(ref, held.at[i]) for i, ref in enumerate(sources)], sem_in)
    core = place()[3] ^ other
    stores = []
    for i, load in enumerate(loads):
        near, far = side(0, core) ^ (i >> 1), side(1, core) ^ (i & 1)
        block = core * 4 + near * 2 + far
        load.wait()
        wide[i] = held[i].astype(F32)
        in_first, (row, column), (row_2, column_2) = spots(block)
        place_1 = first_ref.at[
            pl.ds(pl.multiple_of(row * height, height), height),
            pl.ds(pl.multiple_of(column * width, width), width),
        ]
        place_2 = second_ref.at[
            pl.ds(pl.multiple_of(row_2 * height, height), height),
            pl.ds(pl.multiple_of(column_2 * width, width), width),
        ]
        store_1 = pltpu.make_async_copy(wide.at[i], place_1, sem_out.at[i])
        store_2 = pltpu.make_async_copy(wide.at[i], place_2, sem_out.at[i])
        pl.when(in_first)(store_1.start)
        pl.when(jnp.logical_not(in_first))(store_2.start)
        stores.append((in_first, store_1, store_2))
    for in_first, store_1, store_2 in stores:
        pl.when(in_first)(store_1.wait)
        pl.when(jnp.logical_not(in_first))(store_2.wait)


def widen(cost, other, parts, spots, shapes, before=()):
    height, width = parts[0].shape
    return pl.pallas_call(
        functools.partial(widen_kernel, other, spots),
        in_specs=[hbm()] * (4 + len(before)),
        out_specs=[hbm()] * 2,
        out_shape=[jax.ShapeDtypeStruct(shape, F32) for shape in shapes],
        input_output_aliases={4 + i: i for i in range(len(before))},
        scratch_shapes=[
            pltpu.VMEM((4, height, width), BF),
            pltpu.VMEM((4, height, width), F32),
            dma(4),
            dma(4),
        ],
        compiler_params=alone(),
        cost_estimate=cost,
        name="widen",
    )(*parts, *before)


def spots_of(split, first, second):
    def spots(block):
        return (
            block < split,
            first(jnp.minimum(block, split - 1)),
            second(jnp.maximum(block - split, 0)),
        )

    return spots


def widen_plain_kernel(split, maps, in_ref, first_ref, second_ref, held, wide, sem_in, sem_out):
    count, height, width = held.shape
    loads = copies(
        [(in_ref.at[pl.ds(i * height, height)], held.at[i]) for i in range(count)], sem_in
    )
    stores = []
    for i, load in enumerate(loads):
        load.wait()
        wide[i] = held[i].astype(F32)
        row, column = maps[0](i) if i < split else maps[1](i - split)
        target = (first_ref if i < split else second_ref).at[
            pl.ds(row * height, height), pl.ds(column * width, width)
        ]
        stores += copies([(wide.at[i], target)], sem_out.at[pl.ds(i, 1)])
    for store in stores:
        store.wait()


def widen_plain(summed, split, shapes, maps):
    width = summed.shape[1]
    height = summed.shape[0] // 8
    return pl.pallas_call(
        functools.partial(widen_plain_kernel, split, maps),
        in_specs=[hbm()],
        out_specs=[hbm()] * 2,
        out_shape=[jax.ShapeDtypeStruct(shape, F32) for shape in shapes],
        scratch_shapes=[
            pltpu.VMEM((8, height, width), BF),
            pltpu.VMEM((8, height, width), F32),
            dma(8),
            dma(8),
        ],
        compiler_params=alone(),
        cost_estimate=BRIEF,
        name="widen_plain",
    )(summed)


def mod_kernel(clips, sizes, small_ref, mod_ref, *refs):
    vectors, (smooth, split, mods, sem_mod) = refs[:-4], refs[-4:]
    members, width = 9, small_ref.shape[1]
    t = small_ref[pl.ds(members * clips, clips), :]
    value = (t / (1.0 + jnp.exp(-t))).astype(BF).astype(F32)
    smooth[...] = jnp.zeros_like(smooth)
    split[...] = jnp.zeros_like(split)
    for i in range(3):
        smooth[i * clips : (i + 1) * clips, :] = value
    left = smooth[...].astype(BF)
    slots = mods.shape[0]
    stores = []
    for member in range(members):
        rest = small_ref[pl.ds(member * clips, clips), :]
        vectors[0][pl.ds(member * width, width)] = jnp.sum(rest, axis=0)
        for i in range(3):
            piece = rest.astype(BF).astype(F32)
            split[i * clips : (i + 1) * clips, :] = piece
            rest = rest - piece
        if member >= slots:
            stores[member - slots].wait()
        mods[member % slots] = dot_tn(left, split[...].astype(BF))
        target = mod_ref.at[:, pl.ds(member * width, width)]
        stores += copies([(mods.at[member % slots], target)], sem_mod.at[pl.ds(member, 1)])
    at = (members + 1) * clips
    for vector, size in zip(vectors[1:], sizes):
        for i in range(size):
            vector[pl.ds(i * width, width)] = small_ref[at]
            at += 1
    for store in stores[-slots:]:
        store.wait()


def mod_grads(small, clips, sizes):
    width = small.shape[1]
    deep = -(-3 * clips // 16) * 16
    vector = lambda size: jax.ShapeDtypeStruct((size * width,), F32)
    return pl.pallas_call(
        functools.partial(mod_kernel, clips, sizes),
        in_specs=[vmem()],
        out_specs=[hbm()] + [vmem()] * (1 + len(sizes)),
        out_shape=[jax.ShapeDtypeStruct((width, 9 * width), F32), vector(9)]
        + [vector(size) for size in sizes],
        scratch_shapes=[
            pltpu.VMEM((deep, width), F32),
            pltpu.VMEM((deep, width), F32),
            pltpu.VMEM((9, width, width), F32),
            dma(9),
        ],
        compiler_params=alone(),
        cost_estimate=BRIEF,
        name="mod_grads",
    )(small)


def quad_kernel(*refs):
    values = [ref[...] for ref in refs[:-1]]
    while len(values) > 1:
        values = [a + b for a, b in zip(values[::2], values[1::2])]
    refs[-1][...] = values[0]


def pair_sum(*parts):
    return pl.pallas_call(
        quad_kernel,
        in_specs=[vmem()] * len(parts),
        out_specs=vmem(),
        out_shape=jax.ShapeDtypeStruct(parts[0].shape, parts[0].dtype),
        compiler_params=alone(),
        cost_estimate=BRIEF,
        name="pair_sum",
    )(*parts)


def per_device(
    tokens, t_embed, frame_clip, boxes, mod_weight, mod_bias, space_qkv, space_qv_bias, space_out,
    space_out_bias, time_qkv, time_qv_bias, time_out, time_out_bias, up_weight, up_bias,
    down_weight, down_bias, cotangent,
):
    owners = lax.axis_size("seq")
    groups = lax.axis_size("dp")
    frames = boxes.shape[0]
    width = tokens.shape[1]
    patches = tokens.shape[0] // frames
    group_frames = frame_clip.shape[0]
    pos = patches // owners
    clips = t_embed.shape[0]
    ff = up_weight.shape[1]
    depth = owners // 4
    own_route = depth <= 4
    route = routes(owners)

    clip_col = frame_clip[:, None]
    per_block = BLOCK // group_frames
    ids_row = (
        jnp.arange(per_block, dtype=jnp.int32)[:, None] * clips + frame_clip[None, :]
    ).reshape(1, BLOCK)

    def exchange(x):
        return lax.all_to_all(x, "seq", split_axis=0, concat_axis=0, tiled=True)

    qkv_maps = (lambda i: (i % 2, i // 2), lambda i: (i, 0))

    cot_send = cotangent.reshape(frames, owners, pos, width).transpose(1, 0, 2, 3)
    cot = exchange(cot_send)
    mid_send, packed_a, attended_a, branch_a, table_a = space_forward(
        frame_clip, boxes, t_embed, mod_weight, mod_bias, tokens, space_qkv, space_qv_bias, space_out,
        space_out_bias, owners,
    )
    mid_send, cot, t_late = tie(mid_send, cot, t_embed)
    mid = exchange(mid_send).reshape(group_frames, pos, width)
    cot = cot.reshape(group_frames, pos, width)
    table = modulation(t_late, mod_weight, mod_bias, 3, 6)
    (
        xa, packed_b, attended_b, branch_b, gmid_b, result_send, grad_f, gclip_c, gup_b, gdown_b,
    ) = owner_forward(
        mid, cot, table, clip_col, ids_row, time_qkv, time_qv_bias, time_out, time_out_bias, up_weight,
        up_bias, down_weight, down_bias,
    )
    ff_shapes = ((width, ff), (ff, width))
    qkv_shapes = ((width, 3 * width), (width, width))
    all_clips = clips * groups
    sizes = (2, 1, 2, 1, ff // width, 1)
    qkv_spots = spots_of(6, lambda i: (i % 2, i // 2), lambda i: (i, 0))

    def after_ff(gmid_b):
        return owner_backward(
            xa, packed_b, attended_b, branch_b, gmid_b, table, clip_col, ids_row, time_qkv, time_out
        )

    def after_time(gmid_a, gclip_b, gtout_b, gtqv_b):
        return space_backward(
            frame_clip, boxes, tokens, packed_a, attended_a, branch_a, gmid_a, table_a, space_qkv,
            space_out, t_embed, gclip_b, gclip_c, gtqv_b, gtout_b, gup_b, gdown_b,
        )

    result_send = result_send.reshape(owners, frames, pos, width)
    grad_f = grad_f.reshape(-1, width)
    part_f = Held(lax.psum_scatter(grad_f, BOTH, scatter_dimension=0, tiled=True))
    if own_route:
        sums = {}
        order = Order()
        wide = {}
        for name, *step in SCHEDULE:
            if name == "time":
                gmid_b = order.after(gmid_b)
                gmid_send, kept_t, other_t, gclip_b, gtout_b, gtqv_b = after_ff(gmid_b)
                gmid_a = exchange(gmid_send.reshape(owners, frames, pos, width))
                sums["t"] = Sum(kept_t, other_t, route)
                order.before = None
            elif name == "space":
                gmid_a = order.after(gmid_a)
                gmid_a, result_send = tie(gmid_a, result_send)
                result = exchange(result_send)
                grad_tokens, kept_s, other_s, small = after_time(
                    gmid_a, gclip_b, gtout_b, gtqv_b
                )
                sums["s"] = Sum(kept_s, other_s, route)
                kept_s, result = tie(sums["s"].kept, result)
                sums["s"].kept = kept_s
                order.before = None
            elif name == "ff":
                part_f.value = order.after(part_f.value)
                order.before = (part_f, "value")
            elif name == "small":
                links = (
                    [route["core"]]
                    if step[0] == 0
                    else [route["x"], route["y"], route["both"]]
                    if step[0] == 1
                    else route["swap"]
                )
                if step[0]:
                    small_got = order.after(small_got)
                    small = pair_sum(small, *small_got)
                    order.before = (Held(small), "value")
                small_got = tuple(move(small, pairs) for pairs in links)
            elif name == "mod":
                small = pair_sum(small, *order.after(small_got))
                mod = Held(None)
                mod.value, *vectors = mod_grads(small, all_clips, sizes)
                order.before = (mod, "value")
            elif step[0] == "widen":
                total = sums[name]
                if step[1]:
                    total.wait = order.after(total.wait)
                    parts = total.wait
                else:
                    total.across = order.after(total.across)
                    parts = (total.near, total.far, total.across, total.across_far)
                before = (wide[name].value, wide[name].other) if name in wide else ()
                pair = widen(order.cost, step[1], parts, qkv_spots, qkv_shapes, before)
                done = wide[name] = Held(pair[0])
                done.other = pair[1]
                order.before = (done, "value")
            else:
                order.cost = COSTS.get((name, *step), BRIEF)
                order.run(sums[name], *step)
        sum_f = lax.all_gather(part_f.value, BOTH, axis=0, tiled=True)
        grad_mod = mod.value
        wide_time, wide_space = ((wide[k].value, wide[k].other) for k in ("t", "s"))
    else:
        result = exchange(result_send)
        gmid_send, kept_t, other_t, gclip_b, gtout_b, gtqv_b = after_ff(gmid_b)
        gmid_a = exchange(gmid_send.reshape(owners, frames, pos, width))
        grad_tokens, kept_s, other_s, small = after_time(gmid_a, gclip_b, gtout_b, gtqv_b)
        small = lax.psum(small, BOTH)
        grad_mod, *vectors = mod_grads(small, all_clips, sizes)
        sum_f = lax.all_gather(part_f.value, BOTH, axis=0, tiled=True)
        core = place()[3]

        def whole(kept, other):
            halves = [jnp.where(core == half, kept, other) for half in range(2)]
            return lax.psum(jnp.concatenate(halves, axis=0), BOTH)

        qkv_maps = (lambda i: (i % 2, i // 2), lambda i: (i, 0))
        wide_time = widen_plain(whole(kept_t, other_t), 6, qkv_shapes, qkv_maps)
        wide_space = widen_plain(whole(kept_s, other_s), 6, qkv_shapes, qkv_maps)
    grad_up, grad_down = widen_plain(sum_f, 4, ff_shapes, (lambda i: (0, i), lambda i: (i, 0)))
    grad_mod_b, *biases = vectors
    return (
        result.transpose(1, 0, 2, 3).reshape(tokens.shape),
        grad_tokens,
        grad_mod,
        grad_mod_b,
        wide_space[0],
        biases[0],
        wide_space[1],
        biases[1],
        wide_time[0],
        biases[2],
        wide_time[1],
        biases[3],
        grad_up,
        biases[4],
        grad_down,
        biases[5],
    )


def solution(mesh):
    split = P(BOTH, None)
    placed = (split, P("dp", None), P("dp"), split) + (P(),) * 14 + (split,)
    return jax.shard_map(
        per_device,
        mesh=mesh,
        in_specs=placed,
        out_specs=(split, split) + (P(),) * 14,
        check_vma=False,
    )
```
